32 devices in a mesh: groups: 2 (over y), tp: 4 (over z), sp: 4 (over x, core).
Axes of the slice: x: 2, y: 2, z: 4, core: 2. Of those that a mesh axis runs over, the one named last changes fastest.
Arguments:
- hidden_cont: bfloat16 [512, 5120], P(('groups', 'sp')), parts along dimension 0, may hold values from -6 to 6
- hidden_prompt: bfloat16 [1024, 5120], P(('groups', 'sp')), parts along dimension 0, may hold values from -6 to 6
- norm_gain: float32 [5120], replicated, may hold values from 0.1 to 1.9
- query_weight: bfloat16 [5120, 4096], P('sp', 'tp'), may hold values from -0.078125 to 0.078125
- keyval_weight: bfloat16 [5120, 1024], P('sp'), may hold values from -0.078125 to 0.078125
- out_weight: bfloat16 [4096, 5120], P('tp', 'sp'), may hold values from -0.125 to 0.125
- query_gain: float32 [128], replicated, may hold values from 0.5 to 5
- key_gain: float32 [128], replicated, may hold values from 0.5 to 5
- sample_lengths: int32 [16], P('groups'), parts along dimension 0, may hold values from 1 to 64, 256 in all
Outputs:
- mixed: bfloat16 [512, 5120], P(('groups', 'sp'), 'tp'), parts along dimension 0
The draws below stay inside these ranges and needn't reach their ends.
There are 2 independent parts, one for each index of `groups`. The reference program is written for one: setup_inputs(seed, part) draws one part's arguments, and reference() takes and returns one part's arrays. A program takes and returns all parts, laid end to end along the dimension named above; an argument that names none is the same for every part. Nothing has to cross between parts.
Inputs may be any that keep to these rules, and one draw needn't show every extreme that they name: `sample_lengths`: the lengths sum to 256 and the longest has exactly 64 tokens.
All inputs are finite; a program needn't handle non-finite values.
Results may differ from the reference program's by a relative error of at most 0.012.
The reference program's roundings to bfloat16 on the way count: a program that leaves them out, or rounds other values in their place, can miss the bound.
Values may be sent and summed in bfloat16 or wider, within the bound.
No kernel may reach another device: no remote copies, remote signals or barrier semaphores. Data moves between devices by JAX's collectives and lax.ppermute only.
A program may use at most 128 MiB of HBM per device.

```python
import math
import jax
import jax.numpy as jnp
import numpy as np
from jax import lax

D = 5120
HS = 128
QH = 32
KVH = 4
CONTS = 8
CONT = 256
PROMPT = 512
MOST = 64
N_TP = 4


def draw_query_gain(key, part):
    key = jax.random.fold_in(key, 11)
    return jnp.exp(jax.random.uniform(key, (HS,), jnp.float32, math.log(0.5), math.log(2.0)))


def draw_key_gain(key, part):
    key = jax.random.fold_in(key, 12)
    return jnp.exp(jax.random.uniform(key, (HS,), jnp.float32, math.log(0.5), math.log(2.0)))


def spiked(values, key, source, target, shards_of, factor):
    def block_of(axis_at):
        return (jnp.arange(values.shape[axis_at]) // (values.shape[axis_at] // shards_of)).reshape((-1,) + (1,) * (values.ndim - 1 - axis_at))

    first = jax.random.permutation(key, shards_of)[block_of(target)]
    far = (block_of(target) + shards_of // 2) % shards_of
    return jnp.where((block_of(source) == first) | (block_of(source) == far), factor * values, values)


def level_of(key, shape, pieces, smallest, high):
    level, own = 1.0, jax.random.fold_in(key, 6)
    for position, shards_of in pieces:
        draws = jnp.exp(jax.random.uniform(jax.random.fold_in(own, position), (shards_of,), jnp.float32, smallest / len(pieces), high / len(pieces)))
        level = level * jnp.repeat(draws, shape[position] // shards_of).reshape([-1 if axis == position else 1 for axis in range(len(shape))])
    return level


def length_profile(count, total, bound, skew):
    portions = [(1 << 20) // math.isqrt(rank ** skew) + 1 for rank in range(2, count + 1)]
    spare, given = total - bound - (count - 1), [1] * (count - 1)
    while spare > 0:
        free = [i for i in range(count - 1) if given[i] < bound]
        whole, left = sum([portions[i] for i in free]), spare
        for i in free:
            extra = min(bound - given[i], max(1, left * portions[i] // whole), spare)
            given[i] = given[i] + extra
            spare = spare - extra
    return np.array([bound] + given)


def uneven(own_key, count, total, limit, skew):
    if count == 2:
        one = jax.random.randint(own_key, (), max(1, total - limit), min(limit, total - 1) + 1)
        return jnp.stack([one, total - one])
    sizes = jnp.asarray(length_profile(count, total, limit, skew), jnp.int32)
    couples = (count - 1) // 2
    donor, taker = sizes[1:1 + 2 * couples:2], sizes[2:2 + 2 * couples:2]
    room = jnp.minimum(donor - 1, limit - taker)
    passed = jax.random.randint(jax.random.fold_in(own_key, 1), (couples,), 0, 1 << 20) % (room + 1)
    sizes = sizes.at[1:1 + 2 * couples:2].set(donor - passed).at[2:2 + 2 * couples:2].set(taker + passed)
    return sizes[jax.random.permutation(jax.random.fold_in(own_key, 2), count)]


def centred(stream_key, shape, scale, most, split=(), held_as=jnp.bfloat16):
    entries = jax.random.normal(stream_key, shape, jnp.float32) * scale
    if len(split) > 0:
        entries = level_of(stream_key, shape, split, -0.22, 0.18) * entries
    return jnp.clip(entries, min=-most, max=most).astype(held_as)


def gaussian_with(own_key, extent, scale, reach, shards, heavy, held_as=jnp.bfloat16):
    result = scale * jax.random.normal(own_key, extent, jnp.float32)
    if shards:
        result = result * level_of(own_key, extent, shards, -0.22, 0.18)
    return jnp.clip(spiked(result, jax.random.fold_in(own_key, 3), *heavy), -reach, reach).astype(held_as)


def setup_inputs(seed: int = 0, part: int = 0) -> dict:
    key_of = jax.random.split(jax.random.key(seed), 10)
    own_keys = jax.random.split(jax.random.fold_in(key_of[9], part), 10)
    hidden_cont = centred(own_keys[0], (CONT, D), 1.0, 6.0, ((0, 4),))
    hidden_prompt = centred(own_keys[1], (PROMPT, D), 1.0, 6.0, ((0, 4),))
    norm_gain = jnp.clip(1.0 + 0.18 * jax.random.normal(key_of[2], (D,), jnp.float32), 0.1, 1.9)
    query_weight = centred(key_of[3], (D, QH * HS), D ** -0.5, 0.078125, ((0, 4), (1, 4)))
    keyval_weight = centred(key_of[4], (D, 2 * KVH * HS), D ** -0.5, 0.078125, ((0, 4),))
    out_weight = gaussian_with(key_of[5], (QH * HS, D), (QH * HS) ** -0.5, 0.125, ((0, 4), (1, 4)), (0, 1, 4, 2.0))
    query_gain = draw_query_gain(jax.random.fold_in(key_of[9], 71), part)
    key_gain = draw_key_gain(jax.random.fold_in(key_of[9], 71), part)
    sample_lengths = uneven(own_keys[8], CONTS, CONT, MOST, 2).astype(jnp.int32)
    return {"hidden_cont": hidden_cont, "hidden_prompt": hidden_prompt, "norm_gain": norm_gain, "query_weight": query_weight, "keyval_weight": keyval_weight, "out_weight": out_weight, "query_gain": query_gain, "key_gain": key_gain, "sample_lengths": sample_lengths}


def rms_rows(values, gain):
    return values * lax.rsqrt(lax.optimization_barrier(jnp.mean(values * values, axis=-1, keepdims=True)) + 1e-06) * gain

def rotate(values, positions):
    half = values.shape[-1] // 2
    frequency = jnp.exp(jnp.arange(half, dtype=jnp.float32) * (-2.0 * math.log(1000000.0) / values.shape[-1]))
    angles = positions.astype(jnp.float32)[:, None] * frequency[None, :]
    shape = (positions.shape[0],) + (1,) * (values.ndim - 2) + (half,)
    cosine = jnp.cos(angles).reshape(shape)
    sine = jnp.sin(angles).reshape(shape)
    first = values[..., :half]
    second = values[..., half:]
    return jnp.concatenate([first * cosine - second * sine, second * cosine + first * sine], axis=-1)

def segments(lengths, index):
    ends = jnp.cumsum(lengths, dtype=jnp.int32)
    segment = lax.optimization_barrier(jnp.sum((index[:, None] >= ends[None, :]).astype(jnp.int32), axis=1, dtype=jnp.int32))
    member = segment[:, None] == jnp.arange(lengths.shape[0], dtype=jnp.int32)[None, :]
    start = lax.optimization_barrier(jnp.sum(jnp.where(member, (ends - lengths)[None, :], 0), axis=1, dtype=jnp.int32))
    return (segment, start)

def attend(query, keys, values, allowed, scale):
    scores = lax.dot_general(query, keys, (((1,), (1,)), ((), ())), preferred_element_type=jnp.float32) * scale
    scores = jnp.where(allowed, scores, -1e+30)
    peak = lax.optimization_barrier(jnp.max(scores, axis=1, keepdims=True))
    raised = jnp.exp(scores - peak)
    weights = (raised / lax.optimization_barrier(jnp.sum(raised, axis=1, keepdims=True))).astype(jnp.bfloat16)
    return jnp.dot(weights, values, preferred_element_type=jnp.float32).astype(jnp.bfloat16)

def reference(hidden_cont, hidden_prompt, norm_gain, query_weight, keyval_weight, out_weight, query_gain, key_gain, sample_lengths):
    scale = 1.0 / math.sqrt(HS)
    stacked = jnp.concatenate([hidden_prompt, hidden_cont], axis=0).astype(jnp.float32)
    normed = rms_rows(stacked, norm_gain).astype(jnp.bfloat16)
    cont_index = jnp.arange(CONT, dtype=jnp.int32)
    segment, start = segments(sample_lengths, cont_index)
    positions = jnp.concatenate([jnp.arange(PROMPT, dtype=jnp.int32), PROMPT + cont_index - start])
    query = jnp.dot(normed[PROMPT:], query_weight, preferred_element_type=jnp.float32).reshape(CONT, QH, HS)
    query = rotate(rms_rows(query, query_gain), positions[PROMPT:]).astype(jnp.bfloat16)
    keyval = jnp.dot(normed, keyval_weight, preferred_element_type=jnp.float32).reshape(PROMPT + CONT, KVH, 2 * HS)
    keys = rotate(rms_rows(keyval[:, :, :HS], key_gain), positions).astype(jnp.bfloat16)
    values = keyval[:, :, HS:].astype(jnp.bfloat16)
    own_part = (segment[None, :] == segment[:, None]) & (cont_index[None, :] <= cont_index[:, None])
    allowed = jnp.concatenate([jnp.ones((CONT, PROMPT), dtype=jnp.bool_), own_part], axis=1)

    def one_head(head):
        shared = head // (QH // KVH)
        return attend(query[:, head], keys[:, shared], values[:, shared], allowed, scale)
    heads = lax.map(one_head, jnp.arange(QH, dtype=jnp.int32))
    heads = jnp.transpose(heads, (1, 0, 2)).reshape(CONT, QH * HS)
    width = QH * HS // N_TP
    mixed = hidden_cont.astype(jnp.float32)
    for group in range(N_TP):
        part_out = jnp.dot(heads[:, group * width:(group + 1) * width], out_weight[group * width:(group + 1) * width], preferred_element_type=jnp.float32)
        part_out = lax.optimization_barrier(part_out.astype(jnp.bfloat16))
        mixed = mixed + part_out.astype(jnp.float32)
    return mixed.astype(jnp.bfloat16)
```

```python
import math

import jax
import jax.numpy as jnp
from jax import lax
from jax.sharding import PartitionSpec as P

QH = 32
KVH = 4


def rms_rows(values, gain):
    return values * lax.rsqrt(jnp.mean(values * values, axis=-1, keepdims=True) + 1e-06) * gain


def rotate(values, positions):
    half = values.shape[-1] // 2
    frequency = jnp.exp(
        jnp.arange(half, dtype=jnp.float32) * (-2.0 * math.log(1000000.0) / values.shape[-1])
    )
    angles = positions.astype(jnp.float32)[:, None] * frequency[None, :]
    shape = (positions.shape[0],) + (1,) * (values.ndim - 2) + (half,)
    cosine = jnp.cos(angles).reshape(shape)
    sine = jnp.sin(angles).reshape(shape)
    first = values[..., :half]
    second = values[..., half:]
    return jnp.concatenate(
        [first * cosine - second * sine, second * cosine + first * sine], axis=-1
    )


def segments(lengths, index):
    ends = jnp.cumsum(lengths, dtype=jnp.int32)
    segment = jnp.sum((index[:, None] >= ends[None, :]).astype(jnp.int32), axis=1, dtype=jnp.int32)
    member = segment[:, None] == jnp.arange(lengths.shape[0], dtype=jnp.int32)[None, :]
    start = jnp.sum(jnp.where(member, (ends - lengths)[None, :], 0), axis=1, dtype=jnp.int32)
    return (segment, start)


def attend(query, keys, values, allowed, scale):
    scores = (
        lax.dot_general(query, keys, (((1,), (1,)), ((), ())), preferred_element_type=jnp.float32)
        * scale
    )
    scores = jnp.where(allowed, scores, -1e30)
    peak = jnp.max(scores, axis=1, keepdims=True)
    raised = jnp.exp(scores - peak)
    weights = (raised / jnp.sum(raised, axis=1, keepdims=True)).astype(jnp.bfloat16)
    return jnp.dot(weights, values, preferred_element_type=jnp.float32).astype(jnp.bfloat16)


def swap(array, axis, bits):
    return lax.ppermute(array, axis, [(i, i ^ bits) for i in range(lax.axis_size(axis))])


def swap_bits(count):
    bits = []
    bit = 1
    while bit < count:
        bits.append(bit)
        bit *= 2
    return bits


def gather_blocks(block, axis, count):
    held = {0: block}
    bits = swap_bits(count)
    for bit in bits[1:] + bits[:1]:
        held.update({d ^ bit: swap(held[d], axis, bit) for d in sorted(held)})
    return [held[d] for d in range(count)]


def sum_blocks(blocks, axis, count):
    held = dict(enumerate(blocks))
    for bit in swap_bits(count):
        sent = [d for d in sorted(held) if d & bit]
        got = {d ^ bit: swap(held[d], axis, bit) for d in sent}
        held = {d: held[d] + got[d] for d in got}
    return held[0]


def on_device(
    hidden_cont,
    hidden_prompt,
    norm_gain,
    query_weight,
    keyval_weight,
    out_weight,
    query_gain,
    key_gain,
    sample_lengths,
):
    head_size = query_gain.shape[0]
    heads_here = query_weight.shape[1] // head_size
    cont_rows = hidden_cont.shape[0]
    prompt_rows = hidden_prompt.shape[0]
    depth = query_weight.shape[0]
    tp_index = lax.axis_index("tp")
    sp_index = lax.axis_index("sp")
    sp_count = lax.axis_size("sp")
    tp_count = lax.axis_size("tp")
    prompt_total = prompt_rows * sp_count
    key_head = tp_index * heads_here // (QH // KVH)
    scale = 1.0 / math.sqrt(head_size)
    owners = [sp_index ^ d for d in range(sp_count)]

    def column_block(array, owner):
        return lax.dynamic_slice_in_dim(array, owner * depth, depth, 1)

    normed_cont = rms_rows(hidden_cont.astype(jnp.float32), norm_gain).astype(jnp.bfloat16)
    cont_columns = [column_block(normed_cont, owner) for owner in owners]
    kv_weight = lax.dynamic_slice_in_dim(keyval_weight, key_head * 2 * head_size, 2 * head_size, 1)
    cont_blocks = [cont_columns[0]] + [
        swap(cont_columns[d], "sp", d) for d in range(1, sp_count)
    ]
    kv_weights = gather_blocks(kv_weight, "sp", sp_count)

    query_part = jnp.dot(
        jnp.concatenate(cont_blocks, axis=0), query_weight, preferred_element_type=jnp.float32
    )
    query = sum_blocks(
        [query_part[d * cont_rows : (d + 1) * cont_rows] for d in range(sp_count)], "sp", sp_count
    )

    normed_prompt = rms_rows(hidden_prompt.astype(jnp.float32), norm_gain).astype(jnp.bfloat16)
    keyval = sum(
        jnp.dot(
            jnp.concatenate([column_block(normed_prompt, owner), columns], axis=0),
            weight,
            preferred_element_type=jnp.float32,
        )
        for owner, columns, weight in zip(owners, cont_columns, kv_weights)
    )
    cont_index = sp_index * cont_rows + jnp.arange(cont_rows, dtype=jnp.int32)
    row_segment, row_start = segments(sample_lengths, cont_index)
    cont_pos = prompt_total + cont_index - row_start
    prompt_pos = sp_index * prompt_rows + jnp.arange(prompt_rows, dtype=jnp.int32)
    positions = jnp.concatenate([prompt_pos, cont_pos])
    keys = rotate(rms_rows(keyval[:, :head_size], key_gain), positions).astype(jnp.bfloat16)
    values = keyval[:, head_size:].astype(jnp.bfloat16)
    pairs = gather_blocks(jnp.concatenate([keys, values], axis=1), "sp", sp_count)
    pairs = jnp.concatenate(pairs, axis=0)
    all_keys = pairs[:, :head_size]
    all_values = pairs[:, head_size:]

    query = query.reshape(cont_rows, heads_here, head_size)
    query = rotate(rms_rows(query, query_gain), cont_pos).astype(jnp.bfloat16)
    query = query.reshape(cont_rows * heads_here, head_size)
    own_rows = jnp.arange(cont_rows, dtype=jnp.int32)
    key_index = jnp.concatenate(
        [
            part
            for owner in owners
            for part in (
                jnp.full((prompt_rows,), -1, dtype=jnp.int32),
                owner * cont_rows + own_rows,
            )
        ]
    )
    key_segment, _ = segments(sample_lengths, key_index)
    allowed = (key_index[None, :] < 0) | (
        (key_segment[None, :] == row_segment[:, None])
        & (key_index[None, :] <= cont_index[:, None])
    )
    allowed = jnp.broadcast_to(
        allowed[:, None, :], (cont_rows, heads_here, allowed.shape[1])
    ).reshape(cont_rows * heads_here, allowed.shape[1])
    heads = attend(query, all_keys, all_values, allowed, scale)
    heads = heads.reshape(cont_rows, heads_here * head_size)

    all_heads = jnp.concatenate(gather_blocks(heads, "sp", sp_count), axis=0)
    partial_out = jnp.dot(
        all_heads, out_weight, preferred_element_type=jnp.float32
    ).astype(jnp.bfloat16)
    assert tp_count == sp_count
    summed = 0.0
    for d in range(sp_count):
        block = lax.dynamic_slice_in_dim(
            partial_out, (tp_index ^ d ^ sp_index) * cont_rows, cont_rows, 0
        )
        block = lax.ppermute(
            block,
            ("tp", "sp"),
            [
                (t * sp_count + s, s * sp_count + (t ^ d))
                for t in range(tp_count)
                for s in range(sp_count)
            ],
        )
        summed = summed + block.astype(jnp.float32)
    out_width = summed.shape[1]
    residual = lax.dynamic_slice_in_dim(hidden_cont, tp_index * out_width, out_width, 1).astype(
        jnp.float32
    )
    return (summed + residual).astype(jnp.bfloat16)


def solution(mesh):
    placed = (
        P(("groups", "sp"), None),
        P(("groups", "sp"), None),
        P(),
        P("sp", "tp"),
        P("sp", None),
        P("tp", "sp"),
        P(),
        P(),
        P("groups"),
    )
    return jax.shard_map(
        on_device, mesh=mesh, in_specs=placed, out_specs=P(("groups", "sp"), "tp"), check_vma=False
    )
```

```python
import functools
import math

import jax
import jax.numpy as jnp
from jax import lax
from jax.experimental import pallas as pl
from jax.experimental.pallas import tpu as pltpu
from jax.sharding import PartitionSpec as P

QH = 32
KVH = 4
SP, TP, GROUP, HEAD = range(4)
BF16 = jnp.bfloat16
F32 = jnp.float32
ROOM = 24 * 1024 * 1024


def call(kernel, place, grid, in_specs, out_specs, out_shape, args, cost, scratch=()):
    flops, moved = cost
    return pl.pallas_call(
        kernel,
        out_shape=out_shape,
        grid_spec=pltpu.PrefetchScalarGridSpec(
            num_scalar_prefetch=1,
            grid=grid,
            in_specs=in_specs,
            out_specs=out_specs,
            scratch_shapes=scratch,
        ),
        compiler_params=pltpu.CompilerParams(vmem_limit_bytes=ROOM),
        cost_estimate=pl.CostEstimate(flops=flops, bytes_accessed=moved, transcendentals=0),
    )(place, *args)


def whole(array):
    zeros = (0,) * array.ndim
    return pl.BlockSpec(array.shape, lambda i, place: zeros)


def shape_of(shape, dtype):
    return jax.ShapeDtypeStruct(shape, dtype)


def rms_rows(values, gain):
    return values * lax.rsqrt(jnp.mean(values * values, axis=-1, keepdims=True) + 1e-06) * gain


def norm_kernel(place, hidden, gain, out):
    count, _, depth = out.shape
    normed = rms_rows(hidden[...].astype(F32), gain[...]).astype(BF16)
    for j in range(count):
        out[j] = normed[:, j * depth : (j + 1) * depth]


def norm_split(place, hidden, gain, count):
    rows, width = hidden.shape
    step = min(rows, 64)
    out = (count, rows, width // count)
    return call(
        norm_kernel,
        place,
        (rows // step,),
        [pl.BlockSpec((step, width), lambda i, place: (i, 0)), whole(gain)],
        pl.BlockSpec((count, step, width // count), lambda i, place: (0, i, 0)),
        shape_of(out, BF16),
        (hidden, gain),
        (4 * rows * width, 4 * rows * width),
    )


def pick_kernel(place, first, second, out_first, out_second):
    out_first[...] = first[...]
    out_second[...] = second[...]


def pick_columns(place, keyval_weight, head_size):
    depth = keyval_weight.shape[0]
    block = (depth, head_size)
    return call(
        pick_kernel,
        place,
        (1,),
        [
            pl.BlockSpec(block, lambda i, place: (0, 2 * place[HEAD] + place[GROUP])),
            pl.BlockSpec(block, lambda i, place: (0, 2 * place[HEAD] + 1 - place[GROUP])),
        ],
        [pl.BlockSpec(block, lambda i, place: (0, 0))] * 2,
        [shape_of(block, BF16)] * 2,
        (keyval_weight, keyval_weight),
        (0, 8 * depth * head_size),
    )


def query_kernel(count, place, rows, weight, *outs):
    block = rows.shape[1]
    left = jnp.concatenate([rows[place[SP] ^ d] for d in range(count)], axis=0)
    part = jnp.dot(left, weight[...], preferred_element_type=F32)
    for d in range(count):
        outs[d][...] = part[d * block : (d + 1) * block]


def query_parts(place, rows, weight):
    count, block, depth = rows.shape
    width = weight.shape[1]
    step = min(width, 256)
    return call(
        functools.partial(query_kernel, count),
        place,
        (width // step,),
        [whole(rows), pl.BlockSpec((depth, step), lambda i, place: (0, i))],
        [pl.BlockSpec((block, step), lambda i, place: (0, i))] * count,
        [shape_of((block, width), F32)] * count,
        (rows, weight),
        (2 * count * block * depth * width, 2 * depth * width),
    )


def turn(values, cosine, sine):
    return values * cosine + pltpu.roll(values, values.shape[-1] // 2, 1) * sine


def keyval_kernel(count, place, prompt, cont, cosine, sine, gain, *refs):
    weights, out = refs[:-1], refs[-1]
    prompt_rows = prompt.shape[1]
    size = gain.shape[1]
    sums = []
    for left in (prompt, cont):
        for half in range(2):
            total = 0.0
            for d in range(count):
                total = total + jnp.dot(
                    left[place[SP] ^ d],
                    weights[2 * d + half][...],
                    preferred_element_type=F32,
                )
            sums.append(total)
    swapped = place[GROUP] == 1
    for at, first, second in ((0, *sums[:2]), (prompt_rows, *sums[2:])):
        rows = slice(at, at + first.shape[0])
        key = jnp.where(swapped, second, first)
        value = jnp.where(swapped, first, second)
        key = turn(rms_rows(key, gain[...]), cosine[rows, :], sine[rows, :])
        out[rows, :size] = key.astype(BF16)
        out[rows, size:] = value.astype(BF16)


def keyval_rows(place, prompt, cont, cosine, sine, gain, weights):
    count, prompt_rows, depth = prompt.shape
    rows = prompt_rows + cont.shape[1]
    size = gain.shape[1]
    args = (prompt, cont, cosine, sine, gain, *weights)
    out = shape_of((rows, 2 * size), BF16)
    return call(
        functools.partial(keyval_kernel, count),
        place,
        (1,),
        [whole(a) for a in args],
        whole(out),
        out,
        args,
        (4 * rows * count * depth * size, 2 * count * depth * (rows + 2 * size)),
    )


def attend_kernel(count, prompt_rows, place, lengths, mine, other, cosine, sine, gain, *refs):
    pairs, out = refs[:-1], refs[-1]
    rows, width = mine.shape
    size = gain.shape[1]
    heads = width // size
    queries = []
    for h in range(heads):
        part = slice(h * size, (h + 1) * size)
        value = rms_rows(mine[:, part] + other[:, part], gain[...])
        queries.append(turn(value, cosine[...], sine[...]).astype(BF16))
    queries = jnp.concatenate(queries, axis=0)
    prompt = jnp.concatenate([pair[:prompt_rows] for pair in pairs], axis=0)
    cont = jnp.concatenate([pair[prompt_rows:] for pair in pairs], axis=0)
    scale = 1.0 / math.sqrt(size)
    by_rows = (((1,), (1,)), ((), ()))
    to_prompt = (
        lax.dot_general(queries, prompt[:, :size], by_rows, preferred_element_type=F32) * scale
    )
    to_cont = (
        lax.dot_general(queries, cont[:, :size], by_rows, preferred_element_type=F32) * scale
    )
    shape = (rows, cont.shape[0])
    own = place[SP] * rows + lax.broadcasted_iota(jnp.int32, shape, 0)
    at = lax.broadcasted_iota(jnp.int32, shape, 1)
    key = jnp.zeros(shape, jnp.int32)
    for d in range(count):
        inside = (at >= d * rows) & (at < (d + 1) * rows)
        key = jnp.where(inside, (place[SP] ^ d) * rows + at - d * rows, key)
    start = jnp.zeros(shape, jnp.int32)
    total = jnp.int32(0)
    for c in range(lengths.shape[0]):
        start = jnp.where(own >= total, total, start)
        total = total + lengths[c]
    allowed = jnp.where((key >= start) & (key <= own), 0.0, -1e30)
    to_cont = to_cont + jnp.concatenate([allowed] * heads, axis=0)
    peak = jnp.maximum(
        jnp.max(to_prompt, axis=1, keepdims=True), jnp.max(to_cont, axis=1, keepdims=True)
    )
    to_prompt = jnp.exp(to_prompt - peak)
    to_cont = jnp.exp(to_cont - peak)
    divisor = jnp.sum(to_prompt, axis=1, keepdims=True) + jnp.sum(to_cont, axis=1, keepdims=True)
    result = jnp.dot(
        (to_prompt / divisor).astype(BF16), prompt[:, size:], preferred_element_type=F32
    ) + jnp.dot((to_cont / divisor).astype(BF16), cont[:, size:], preferred_element_type=F32)
    for h in range(heads):
        out[:, h * size : (h + 1) * size] = result[h * rows : (h + 1) * rows].astype(BF16)


def attend(place, lengths, mine, other, cosine, sine, gain, pairs, prompt_rows):
    rows, width = mine.shape
    args = (mine, other, cosine, sine, gain, *pairs)
    out = shape_of((rows, width), BF16)
    keys = len(pairs) * pairs[0].shape[0]
    return call(
        functools.partial(attend_kernel, len(pairs), prompt_rows),
        place,
        (1,),
        [pl.BlockSpec(memory_space=pltpu.SMEM)] + [whole(a) for a in args],
        whole(out),
        out,
        (lengths, *args),
        (4 * rows * width * keys, 10 * rows * width + 512 * keys),
    )


def out_kernel(place, *refs):
    heads, weight, out = refs[:-2], refs[-2], refs[-1]
    rows = heads[0].shape[0]
    left = jnp.concatenate([head[...] for head in heads], axis=0)
    part = jnp.dot(left, weight[...], preferred_element_type=F32).astype(BF16)
    for d in range(len(heads)):
        out[place[SP] ^ d] = part[d * rows : (d + 1) * rows]


def out_parts(place, heads, weight):
    rows, depth = heads[0].shape
    width = weight.shape[1]
    step = 256 if width % 256 == 0 else width
    count = len(heads)
    return call(
        out_kernel,
        place,
        (width // step,),
        [whole(h) for h in heads] + [pl.BlockSpec((depth, step), lambda i, place: (0, i))],
        pl.BlockSpec((count, rows, step), lambda i, place: (0, 0, i)),
        shape_of((count, rows, width), BF16),
        (*heads, weight),
        (2 * count * rows * depth * width, 2 * depth * width),
    )


def final_kernel(place, parts, hidden, out):
    total = hidden[...].astype(F32)
    for t in range(parts.shape[0]):
        total = total + parts[t].astype(F32)
    out[...] = total.astype(BF16)


def final_sum(place, parts, hidden):
    count, rows, width = parts.shape
    return call(
        final_kernel,
        place,
        (1,),
        [whole(parts), whole(hidden)],
        pl.BlockSpec((rows, width), lambda i, place: (0, 0)),
        shape_of((rows, width), BF16),
        (parts, hidden),
        (count * rows * width, 12 * rows * width),
    )


def swap(array, axis, bits):
    return lax.ppermute(array, axis, [(i, i ^ bits) for i in range(lax.axis_size(axis))])


def swap_bits(count):
    bits = []
    bit = 1
    while bit < count:
        bits.append(bit)
        bit *= 2
    return bits


def gather_blocks(block, axis, count):
    held = {0: block}
    bits = swap_bits(count)
    for bit in bits[1:] + bits[:1]:
        held.update({d ^ bit: swap(held[d], axis, bit) for d in sorted(held)})
    return [held[d] for d in range(count)]


def gather_halves(first, second, axis, count):
    bits = swap_bits(count)
    firsts = {0: first}
    for bit in bits[1:]:
        firsts.update({d ^ bit: swap(firsts[d], axis, bit) for d in sorted(firsts)})
    seconds = {d: second if d == 0 else swap(firsts[d], "groups", 1) for d in firsts}
    pieces = []
    for held in (firsts, seconds):
        held.update({d ^ 1: swap(held[d], axis, 1) for d in sorted(held)})
    for d in range(count):
        pieces += [firsts[d], seconds[d]]
    return pieces


def sum_blocks(blocks, axis, count):
    held = dict(enumerate(blocks))
    bits = swap_bits(count)
    for bit in bits:
        sent = [d for d in sorted(held) if d & bit]
        got = {d ^ bit: swap(held[d], axis, bit) for d in sent}
        if bit == bits[-1]:
            return held[0], got[0]
        held = {d: held[d] + got[d] for d in got}


def tables(positions, size):
    half = size // 2
    frequency = jnp.exp(jnp.arange(half, dtype=F32) * (-2.0 * math.log(1000000.0) / size))
    angles = positions.astype(F32)[:, None] * frequency[None, :]
    cosine = jnp.cos(angles)
    sine = jnp.sin(angles)
    return (
        jnp.concatenate([cosine, cosine], axis=1),
        jnp.concatenate([-sine, sine], axis=1),
    )


def on_device(
    hidden_cont,
    hidden_prompt,
    norm_gain,
    query_weight,
    keyval_weight,
    out_weight,
    query_gain,
    key_gain,
    sample_lengths,
):
    size = query_gain.shape[0]
    heads_here = query_weight.shape[1] // size
    cont_rows = hidden_cont.shape[0]
    prompt_rows = hidden_prompt.shape[0]
    sp_index = lax.axis_index("sp")
    sp_count = lax.axis_size("sp")
    tp_index = lax.axis_index("tp")
    assert lax.axis_size("tp") == sp_count and lax.axis_size("groups") == 2
    place = jnp.stack(
        [
            sp_index,
            tp_index,
            lax.axis_index("groups"),
            tp_index * heads_here // (QH // KVH),
        ]
    ).astype(jnp.int32)
    norm_gain = norm_gain[None, :]
    query_gain = query_gain[None, :]
    key_gain = key_gain[None, :]

    cont = norm_split(place, hidden_cont, norm_gain, sp_count)
    first, second = pick_columns(place, keyval_weight, size)
    cont_all = lax.all_to_all(cont, "sp", 0, 0, tiled=True)
    weights = gather_halves(first, second, "sp", sp_count)
    prompt = norm_split(place, hidden_prompt, norm_gain, sp_count)

    index = sp_index * cont_rows + jnp.arange(cont_rows, dtype=jnp.int32)
    starts = jnp.cumsum(sample_lengths, dtype=jnp.int32) - sample_lengths
    start = jnp.max(jnp.where(index[:, None] >= starts[None, :], starts[None, :], 0), axis=1)
    prompt_pos = sp_index * prompt_rows + jnp.arange(prompt_rows, dtype=jnp.int32)
    positions = jnp.concatenate([prompt_pos, prompt_rows * sp_count + index - start])
    cosine, sine = tables(positions, size)

    parts = query_parts(place, cont_all, query_weight)
    mine, other = sum_blocks(parts, "sp", sp_count)
    pair = keyval_rows(place, prompt, cont, cosine, sine, key_gain, weights)
    pairs = gather_blocks(pair, "sp", sp_count)
    heads = attend(
        place,
        sample_lengths,
        mine,
        other,
        cosine[prompt_rows:],
        sine[prompt_rows:],
        query_gain,
        pairs,
        prompt_rows,
    )
    parts = out_parts(place, gather_blocks(heads, "sp", sp_count), out_weight)
    parts = lax.all_to_all(parts, "sp", 0, 0, tiled=True)
    parts = lax.all_to_all(parts, "tp", 0, 0, tiled=True)
    width = parts.shape[2]
    hidden = lax.dynamic_slice_in_dim(hidden_cont, tp_index * width, width, 1)
    return final_sum(place, parts, hidden)


def solution(mesh):
    placed = (
        P(("groups", "sp"), None),
        P(("groups", "sp"), None),
        P(),
        P("sp", "tp"),
        P("sp", None),
        P("tp", "sp"),
        P(),
        P(),
        P("groups"),
    )
    return jax.shard_map(
        on_device, mesh=mesh, in_specs=placed, out_specs=P(("groups", "sp"), "tp"), check_vma=False
    )
```

```python
import functools
import math

import jax
import jax.numpy as jnp
from jax import lax
from jax.experimental import pallas as pl
from jax.experimental.pallas import tpu as pltpu
from jax.sharding import PartitionSpec as P

QH = 32
KVH = 4
SP, TP, GROUP, HEAD = range(4)
BF16 = jnp.bfloat16
F32 = jnp.float32
ROOM = 24 * 1024 * 1024


def call(kernel, place, grid, in_specs, out_specs, out_shape, args, cost, scratch=()):
    flops, moved = cost
    return pl.pallas_call(
        kernel,
        out_shape=out_shape,
        grid_spec=pltpu.PrefetchScalarGridSpec(
            num_scalar_prefetch=1,
            grid=grid,
            in_specs=in_specs,
            out_specs=out_specs,
            scratch_shapes=scratch,
        ),
        compiler_params=pltpu.CompilerParams(vmem_limit_bytes=ROOM),
        cost_estimate=pl.CostEstimate(flops=flops, bytes_accessed=moved, transcendentals=0),
    )(place, *args)


def whole(array):
    zeros = (0,) * array.ndim
    return pl.BlockSpec(array.shape, lambda i, place: zeros)


def shape_of(shape, dtype):
    return jax.ShapeDtypeStruct(shape, dtype)


def rms_rows(values, gain):
    return values * lax.rsqrt(jnp.mean(values * values, axis=-1, keepdims=True) + 1e-06) * gain


def norm_kernel(place, hidden, gain, *outs):
    split = outs[-1]
    count, _, depth = split.shape
    normed = rms_rows(hidden[...].astype(F32), gain[...]).astype(BF16)
    for j in range(count):
        split[j] = normed[:, j * depth : (j + 1) * depth]
    for d, out in enumerate(outs[:-1], 1):
        out[...] = split[place[SP] ^ d]


def norm_split(place, hidden, gain, count, sent):
    rows, width = hidden.shape
    step = rows if rows % 32 else 32
    depth = width // count
    return call(
        norm_kernel,
        place,
        (rows // step,),
        [pl.BlockSpec((step, width), lambda i, place: (i, 0)), whole(gain)],
        [pl.BlockSpec((step, depth), lambda i, place: (i, 0))] * sent
        + [pl.BlockSpec((count, step, depth), lambda i, place: (0, i, 0))],
        [shape_of((rows, depth), BF16)] * sent + [shape_of((count, rows, depth), BF16)],
        (hidden, gain),
        (4 * rows * width, 4 * rows * width),
    )


def pick_kernel(place, weight, half, both, sems):
    size = half.shape[1]
    at = pl.multiple_of((2 * place[HEAD] + place[GROUP]) * size, size)
    one = pltpu.make_async_copy(weight.at[:, pl.ds(at, size)], half, sems.at[0])
    at = pl.multiple_of(2 * place[HEAD] * size, size)
    two = pltpu.make_async_copy(weight.at[:, pl.ds(at, 2 * size)], both, sems.at[1])
    one.start()
    two.start()
    one.wait()
    two.wait()


def pick_columns(place, weight, size):
    depth = weight.shape[0]
    shapes = [shape_of((depth, size), BF16), shape_of((depth, 2 * size), BF16)]
    return call(
        pick_kernel,
        place,
        (1,),
        [pl.BlockSpec(memory_space=pltpu.HBM)],
        [whole(shape) for shape in shapes],
        shapes,
        (weight,),
        (0, 12 * depth * size),
        [pltpu.SemaphoreType.DMA((2,))],
    )


def query_kernel(count, place, *refs):
    rows, weight, keep, send = refs[:-3], refs[-3], refs[-2], refs[-1]
    block = rows[1].shape[0]
    left = jnp.concatenate(
        [rows[0][place[SP]]] + [row[...] for row in rows[1:]], axis=0
    )
    part = jnp.dot(left, weight[...], preferred_element_type=F32)
    for d in range(count):
        at = d // 2 * block
        (keep, send)[d % 2][at : at + block, :] = part[d * block : (d + 1) * block]


def query_parts(place, rows, weight):
    count = len(rows)
    block, depth = rows[1].shape
    width = weight.shape[1]
    step = min(width, 256)
    half = count // 2 * block
    return call(
        functools.partial(query_kernel, count),
        place,
        (width // step,),
        [whole(r) for r in rows] + [pl.BlockSpec((depth, step), lambda i, place: (0, i))],
        [pl.BlockSpec((half, step), lambda i, place: (0, i))] * 2,
        [shape_of((half, width), F32)] * 2,
        (*rows, weight),
        (2 * count * block * depth * width, 2 * depth * width),
    )


def turn(values, cosine, sine):
    return values * cosine + pltpu.roll(values, values.shape[-1] // 2, 1) * sine


def near_kernel(place, prompt, cont, own, partner, out):
    total = 0.0
    for d, weight in ((0, own), (1, partner)):
        left = jnp.concatenate([prompt[place[SP] ^ d], cont[place[SP] ^ d]], axis=0)
        total = total + jnp.dot(left, weight[...], preferred_element_type=F32)
    out[...] = total


def near_keyval(place, prompt, cont, own, partner):
    rows = prompt.shape[1] + cont.shape[1]
    args = (prompt, cont, own, partner)
    depth, width = own.shape
    out = shape_of((rows, width), F32)
    return call(
        near_kernel,
        place,
        (1,),
        [whole(a) for a in args],
        whole(out),
        out,
        args,
        (4 * rows * depth * width, 4 * depth * (rows + width)),
    )


def keyval_kernel(count, place, prompt, cont, cosine, sine, gain, near, *refs):
    weights, out = refs[:-1], refs[-1]
    size = gain.shape[1]
    total = 0.0
    for d in range(2, count):
        left = jnp.concatenate([prompt[place[SP] ^ d], cont[place[SP] ^ d]], axis=0)
        weight = jnp.concatenate([weights[2 * d - 4][...], weights[2 * d - 3][...]], axis=1)
        total = total + jnp.dot(left, weight, preferred_element_type=F32)
    swapped = place[GROUP] == 1
    first, second = total[:, :size], total[:, size:]
    key = near[:, :size] + jnp.where(swapped, second, first)
    value = near[:, size:] + jnp.where(swapped, first, second)
    out[:, :size] = turn(rms_rows(key, gain[...]), cosine[...], sine[...]).astype(BF16)
    out[:, size:] = value.astype(BF16)


def keyval_rows(place, prompt, cont, cosine, sine, gain, near, weights):
    count, prompt_rows, depth = prompt.shape
    rows = prompt_rows + cont.shape[1]
    size = gain.shape[1]
    args = (prompt, cont, cosine, sine, gain, near, *weights)
    out = shape_of((rows, 2 * size), BF16)
    return call(
        functools.partial(keyval_kernel, count),
        place,
        (1,),
        [whole(a) for a in args],
        whole(out),
        out,
        args,
        (2 * rows * count * depth * size, count * depth * (rows + 2 * size)),
    )


def attend_kernel(count, prompt_rows, place, lengths, mine, near, far, cosine, sine, gain, *refs):
    pairs, out = refs[:-1], refs[-1]
    rows, width = far.shape
    size = gain.shape[1]
    heads = width // size
    queries = []
    for h in range(heads):
        part = slice(h * size, (h + 1) * size)
        value = rms_rows(mine[:rows, part] + near[:rows, part] + far[:, part], gain[...])
        queries.append(turn(value, cosine[...], sine[...]).astype(BF16))
    queries = jnp.concatenate(queries, axis=0)
    prompt = jnp.concatenate([pair[:prompt_rows] for pair in pairs], axis=0)
    cont = jnp.concatenate([pair[prompt_rows:] for pair in pairs], axis=0)
    scale = 1.0 / math.sqrt(size)
    by_rows = (((1,), (1,)), ((), ()))
    to_prompt = (
        lax.dot_general(queries, prompt[:, :size], by_rows, preferred_element_type=F32) * scale
    )
    to_cont = (
        lax.dot_general(queries, cont[:, :size], by_rows, preferred_element_type=F32) * scale
    )
    shape = (rows, cont.shape[0])
    own = place[SP] * rows + lax.broadcasted_iota(jnp.int32, shape, 0)
    at = lax.broadcasted_iota(jnp.int32, shape, 1)
    key = jnp.zeros(shape, jnp.int32)
    for d in range(count):
        inside = (at >= d * rows) & (at < (d + 1) * rows)
        key = jnp.where(inside, (place[SP] ^ d) * rows + at - d * rows, key)
    start = jnp.zeros(shape, jnp.int32)
    total = jnp.int32(0)
    for c in range(lengths.shape[0]):
        start = jnp.where(own >= total, total, start)
        total = total + lengths[c]
    allowed = jnp.where((key >= start) & (key <= own), 0.0, -1e30)
    to_cont = to_cont + jnp.concatenate([allowed] * heads, axis=0)
    peak = jnp.maximum(
        jnp.max(to_prompt, axis=1, keepdims=True), jnp.max(to_cont, axis=1, keepdims=True)
    )
    to_prompt = jnp.exp(to_prompt - peak)
    to_cont = jnp.exp(to_cont - peak)
    divisor = jnp.sum(to_prompt, axis=1, keepdims=True) + jnp.sum(to_cont, axis=1, keepdims=True)
    result = jnp.dot(
        (to_prompt / divisor).astype(BF16), prompt[:, size:], preferred_element_type=F32
    ) + jnp.dot((to_cont / divisor).astype(BF16), cont[:, size:], preferred_element_type=F32)
    for h in range(heads):
        out[:, h * size : (h + 1) * size] = result[h * rows : (h + 1) * rows].astype(BF16)


def attend(place, lengths, mine, near, far, cosine, sine, gain, pairs, prompt_rows):
    rows, width = far.shape
    args = (mine, near, far, cosine, sine, gain, *pairs)
    out = shape_of((rows, width), BF16)
    keys = len(pairs) * pairs[0].shape[0]
    return call(
        functools.partial(attend_kernel, len(pairs), prompt_rows),
        place,
        (1,),
        [pl.BlockSpec(memory_space=pltpu.SMEM)] + [whole(a) for a in args],
        whole(out),
        out,
        (lengths, *args),
        (4 * rows * width * keys, 10 * rows * width + 512 * keys),
    )


def out_kernel(count, place, *refs):
    heads, weight, outs, part = refs[:count], refs[count], refs[count + 1 : -1], refs[-1]
    rows = heads[0].shape[0]
    left = jnp.concatenate([head[...] for head in heads], axis=0)
    total = jnp.dot(left, weight[...], preferred_element_type=F32).astype(BF16)
    for d in range(count):
        part[d] = total[d * rows : (d + 1) * rows]
    for e in range(count):
        outs[e][...] = part[place[TP] ^ e ^ place[SP]]


def out_parts(place, heads, weight):
    rows, depth = heads[0].shape
    width = weight.shape[1]
    step = 256 if width % 256 == 0 else width
    count = len(heads)
    return call(
        functools.partial(out_kernel, count),
        place,
        (width // step,),
        [whole(h) for h in heads] + [pl.BlockSpec((depth, step), lambda i, place: (0, i))],
        [pl.BlockSpec((rows, step), lambda i, place: (0, i))] * count,
        [shape_of((rows, width), BF16)] * count,
        (*heads, weight),
        (2 * count * rows * depth * width, 2 * depth * width),
        [pltpu.VMEM((count, rows, step), BF16)],
    )


def final_kernel(place, hidden, *refs):
    out = refs[-1]
    total = hidden[...].astype(F32)
    for part in refs[:-1]:
        total = total + part[...].astype(F32)
    out[...] = total.astype(BF16)


def final_sum(place, parts, hidden):
    rows, width = hidden.shape
    return call(
        final_kernel,
        place,
        (1,),
        [whole(a) for a in (hidden, *parts)],
        whole(hidden),
        shape_of((rows, width), BF16),
        (hidden, *parts),
        (len(parts) * rows * width, 12 * rows * width),
    )


def swap(array, axis, bits):
    return lax.ppermute(array, axis, [(i, i ^ bits) for i in range(lax.axis_size(axis))])


def swap_bits(count):
    bits = []
    bit = 1
    while bit < count:
        bits.append(bit)
        bit *= 2
    return bits


def gather_blocks(block, axis, count):
    held = {0: block}
    bits = swap_bits(count)
    for bit in bits[1:] + bits[:1]:
        held.update({d ^ bit: swap(held[d], axis, bit) for d in sorted(held)})
    return [held[d] for d in range(count)]


def gather_halves(half, both, axis, count):
    firsts = {0: half}
    for bit in swap_bits(count)[1:]:
        firsts.update({d ^ bit: swap(firsts[d], axis, bit) for d in sorted(firsts)})
    del firsts[0]
    seconds = {d: swap(firsts[d], "groups", 1) for d in firsts}
    for held in (firsts, seconds):
        held.update({d ^ 1: swap(held[d], axis, 1) for d in sorted(held)})
    return [held[d] for d in range(2, count) for held in (firsts, seconds)]


def sum_blocks(keep, send, axis, count):
    near = swap(send, axis, 1)
    rows = keep.shape[0] // (count // 2)
    held = {
        d: keep[d // 2 * rows :][:rows] + near[d // 2 * rows :][:rows]
        for d in range(0, count, 2)
    }
    far = 0.0
    for bit in swap_bits(count)[1:]:
        sent = [d for d in sorted(held) if d & bit]
        got = {d ^ bit: swap(held[d], axis, bit) for d in sent}
        far = far + got.pop(0)
        held = {d: held[d] + got[d] for d in got}
    return keep, near, far


def tables(positions, size):
    half = size // 2
    frequency = jnp.exp(jnp.arange(half, dtype=F32) * (-2.0 * math.log(1000000.0) / size))
    angles = positions.astype(F32)[:, None] * frequency[None, :]
    cosine = jnp.cos(angles)
    sine = jnp.sin(angles)
    return (
        jnp.concatenate([cosine, cosine], axis=1),
        jnp.concatenate([-sine, sine], axis=1),
    )


def on_device(
    hidden_cont,
    hidden_prompt,
    norm_gain,
    query_weight,
    keyval_weight,
    out_weight,
    query_gain,
    key_gain,
    sample_lengths,
):
    size = query_gain.shape[0]
    heads_here = query_weight.shape[1] // size
    cont_rows = hidden_cont.shape[0]
    prompt_rows = hidden_prompt.shape[0]
    sp_index = lax.axis_index("sp")
    sp_count = lax.axis_size("sp")
    tp_index = lax.axis_index("tp")
    assert lax.axis_size("tp") == sp_count and lax.axis_size("groups") == 2
    place = jnp.stack(
        [
            sp_index,
            tp_index,
            lax.axis_index("groups"),
            tp_index * heads_here // (QH // KVH),
        ]
    ).astype(jnp.int32)
    norm_gain = norm_gain[None, :]
    query_gain = query_gain[None, :]
    key_gain = key_gain[None, :]

    half, both = pick_columns(place, keyval_weight, size)
    *sent, cont = norm_split(place, hidden_cont, norm_gain, sp_count, sp_count - 1)
    got = [swap(block, "sp", d) for d, block in enumerate(sent, 1)]
    partner = swap(both, "sp", 1)
    weights = gather_halves(half, both, "sp", sp_count)
    (prompt,) = norm_split(place, hidden_prompt, norm_gain, sp_count, 0)

    index = sp_index * cont_rows + jnp.arange(cont_rows, dtype=jnp.int32)
    starts = jnp.cumsum(sample_lengths, dtype=jnp.int32) - sample_lengths
    start = jnp.max(jnp.where(index[:, None] >= starts[None, :], starts[None, :], 0), axis=1)
    prompt_pos = sp_index * prompt_rows + jnp.arange(prompt_rows, dtype=jnp.int32)
    positions = jnp.concatenate([prompt_pos, prompt_rows * sp_count + index - start])
    cosine, sine = tables(positions, size)

    near_pair = near_keyval(place, prompt, cont, both, partner)
    keep, send = query_parts(place, [cont] + got, query_weight)
    mine, near, far = sum_blocks(keep, send, "sp", sp_count)
    pair = keyval_rows(place, prompt, cont, cosine, sine, key_gain, near_pair, weights)
    pairs = gather_blocks(pair, "sp", sp_count)
    heads = attend(
        place,
        sample_lengths,
        mine,
        near,
        far,
        cosine[prompt_rows:],
        sine[prompt_rows:],
        query_gain,
        pairs,
        prompt_rows,
    )
    parts = out_parts(place, gather_blocks(heads, "sp", sp_count), out_weight)
    parts = [
        lax.ppermute(
            part,
            ("tp", "sp"),
            [
                (t * sp_count + s, s * sp_count + (t ^ e))
                for t in range(sp_count)
                for s in range(sp_count)
            ],
        )
        for e, part in enumerate(parts)
    ]
    width = parts[0].shape[1]
    hidden = lax.dynamic_slice_in_dim(hidden_cont, tp_index * width, width, 1)
    return final_sum(place, parts, hidden)


def solution(mesh):
    placed = (
        P(("groups", "sp"), None),
        P(("groups", "sp"), None),
        P(),
        P("sp", "tp"),
        P("sp", None),
        P("tp", "sp"),
        P(),
        P(),
        P("groups"),
    )
    return jax.shard_map(
        on_device, mesh=mesh, in_specs=placed, out_specs=P(("groups", "sp"), "tp"), check_vma=False
    )
```

```python
import functools
import math

import jax
import jax.numpy as jnp
from jax import lax
from jax.experimental import pallas as pl
from jax.experimental.pallas import tpu as pltpu
from jax.sharding import PartitionSpec as P

QH = 32
KVH = 4
SP, TP, GROUP, HEAD = range(4)
BF16 = jnp.bfloat16
F32 = jnp.float32
ROOM = 24 * 1024 * 1024
ALL = 62 * 1024 * 1024


def call(kernel, place, grid, in_specs, out_specs, out_shape, args, cost, scratch=(), room=ROOM):
    flops, moved = cost
    return pl.pallas_call(
        kernel,
        out_shape=out_shape,
        grid_spec=pltpu.PrefetchScalarGridSpec(
            num_scalar_prefetch=1,
            grid=grid,
            in_specs=in_specs,
            out_specs=out_specs,
            scratch_shapes=scratch,
        ),
        compiler_params=pltpu.CompilerParams(vmem_limit_bytes=room),
        cost_estimate=pl.CostEstimate(flops=flops, bytes_accessed=moved, transcendentals=0),
    )(place, *args)


def whole(array):
    zeros = (0,) * array.ndim
    return pl.BlockSpec(array.shape, lambda i, place: zeros)


def shape_of(shape, dtype):
    return jax.ShapeDtypeStruct(shape, dtype)


def rms_rows(values, gain):
    return values * lax.rsqrt(jnp.mean(values * values, axis=-1, keepdims=True) + 1e-06) * gain


def split_normed(hidden, gain, out):
    count, _, depth = out.shape
    normed = rms_rows(hidden[...].astype(F32), gain[...]).astype(BF16)
    for j in range(count):
        out[j] = normed[:, j * depth : (j + 1) * depth]


def first_kernel(place, weight, hidden, gain, half, both, *rest):
    outs, split, sems = rest[:-2], rest[-2], rest[-1]
    size = half.shape[1]
    at = pl.multiple_of((2 * place[HEAD] + place[GROUP]) * size, size)
    one = pltpu.make_async_copy(weight.at[:, pl.ds(at, size)], half, sems.at[0])
    at = pl.multiple_of(2 * place[HEAD] * size, size)
    two = pltpu.make_async_copy(weight.at[:, pl.ds(at, 2 * size)], both, sems.at[1])
    one.start()
    two.start()
    split_normed(hidden, gain, split)
    for d, out in enumerate(outs, 1):
        out[...] = split[place[SP] ^ d]
    one.wait()
    two.wait()


def first_step(place, weight, hidden, gain, size, count):
    depth = weight.shape[0]
    rows = hidden.shape[0]
    shapes = [shape_of((depth, size), BF16), shape_of((depth, 2 * size), BF16)]
    shapes += [shape_of((rows, depth), BF16)] * (count - 1)
    shapes += [shape_of((count, rows, depth), BF16)]
    return call(
        first_kernel,
        place,
        (1,),
        [pl.BlockSpec(memory_space=pl.ANY), whole(hidden), whole(gain)],
        [whole(shape) for shape in shapes],
        shapes,
        (weight, hidden, gain),
        (0, 12 * depth * size + 6 * rows * depth * count),
        [pltpu.SemaphoreType.DMA((2,))],
        ALL,
    )


def query_kernel(count, place, *refs):
    rows, weight, keep, send = refs[:-3], refs[-3], refs[-2], refs[-1]
    block = rows[1].shape[0]
    left = jnp.concatenate(
        [rows[0][place[SP]]] + [row[...] for row in rows[1:]], axis=0
    )
    part = jnp.dot(left, weight[...], preferred_element_type=F32)
    for d in range(count):
        at = d // 2 * block
        (keep, send)[d % 2][at : at + block, :] = part[d * block : (d + 1) * block]


def query_parts(place, rows, weight):
    count = len(rows)
    block, depth = rows[1].shape
    width = weight.shape[1]
    step = min(width, 256)
    half = count // 2 * block
    return call(
        functools.partial(query_kernel, count),
        place,
        (width // step,),
        [whole(r) for r in rows] + [pl.BlockSpec((depth, step), lambda i, place: (0, i))],
        [pl.BlockSpec((half, step), lambda i, place: (0, i))] * 2,
        [shape_of((half, width), F32)] * 2,
        (*rows, weight),
        (2 * count * block * depth * width, 2 * depth * width),
    )


def turn(values, cosine, sine):
    return values * cosine + pltpu.roll(values, values.shape[-1] // 2, 1) * sine


def near_kernel(place, hidden, norm_gain, cont, own, partner, prompt, out):
    split_normed(hidden, norm_gain, prompt)
    total = 0.0
    for d, weight in ((0, own), (1, partner)):
        left = jnp.concatenate([prompt[place[SP] ^ d], cont[place[SP] ^ d]], axis=0)
        total = total + jnp.dot(left, weight[...], preferred_element_type=F32)
    out[...] = total


def near_keyval(place, hidden, norm_gain, cont, own, partner):
    args = (hidden, norm_gain, cont, own, partner)
    count, cont_rows, depth = cont.shape
    prompt_rows = hidden.shape[0]
    rows = prompt_rows + cont_rows
    width = own.shape[1]
    outs = [shape_of((count, prompt_rows, depth), BF16), shape_of((rows, width), F32)]
    return call(
        near_kernel,
        place,
        (1,),
        [whole(a) for a in args],
        [whole(out) for out in outs],
        outs,
        args,
        (4 * rows * depth * width, 4 * depth * (rows * count + width)),
    )


def keyval_kernel(count, place, prompt, cont, cosine, sine, gain, near, *refs):
    weights, out = refs[:-1], refs[-1]
    size = gain.shape[1]
    total = 0.0
    for d in range(2, count):
        left = jnp.concatenate([prompt[place[SP] ^ d], cont[place[SP] ^ d]], axis=0)
        weight = jnp.concatenate([weights[2 * d - 4][...], weights[2 * d - 3][...]], axis=1)
        total = total + jnp.dot(left, weight, preferred_element_type=F32)
    swapped = place[GROUP] == 1
    first, second = total[:, :size], total[:, size:]
    key = near[:, :size] + jnp.where(swapped, second, first)
    value = near[:, size:] + jnp.where(swapped, first, second)
    out[:, :size] = turn(rms_rows(key, gain[...]), cosine[...], sine[...]).astype(BF16)
    out[:, size:] = value.astype(BF16)


def keyval_rows(place, prompt, cont, cosine, sine, gain, near, weights):
    count, prompt_rows, depth = prompt.shape
    rows = prompt_rows + cont.shape[1]
    size = gain.shape[1]
    args = (prompt, cont, cosine, sine, gain, near, *weights)
    out = shape_of((rows, 2 * size), BF16)
    return call(
        functools.partial(keyval_kernel, count),
        place,
        (1,),
        [whole(a) for a in args],
        whole(out),
        out,
        args,
        (2 * rows * count * depth * size, count * depth * (rows + 2 * size)),
    )


def attend_kernel(count, prompt_rows, place, lengths, mine, near, far, cosine, sine, gain, *refs):
    pairs, out = refs[:-1], refs[-1]
    rows, width = far.shape
    size = gain.shape[1]
    heads = width // size
    queries = []
    for h in range(heads):
        part = slice(h * size, (h + 1) * size)
        value = rms_rows(mine[:rows, part] + near[:rows, part] + far[:, part], gain[...])
        queries.append(turn(value, cosine[...], sine[...]).astype(BF16))
    queries = jnp.concatenate(queries, axis=0)
    prompt = jnp.concatenate([pair[:prompt_rows] for pair in pairs], axis=0)
    cont = jnp.concatenate([pair[prompt_rows:] for pair in pairs], axis=0)
    scale = 1.0 / math.sqrt(size)
    by_rows = (((1,), (1,)), ((), ()))
    to_prompt = (
        lax.dot_general(queries, prompt[:, :size], by_rows, preferred_element_type=F32) * scale
    )
    to_cont = (
        lax.dot_general(queries, cont[:, :size], by_rows, preferred_element_type=F32) * scale
    )
    shape = (rows, cont.shape[0])
    own = place[SP] * rows + lax.broadcasted_iota(jnp.int32, shape, 0)
    at = lax.broadcasted_iota(jnp.int32, shape, 1)
    key = jnp.zeros(shape, jnp.int32)
    for d in range(count):
        inside = (at >= d * rows) & (at < (d + 1) * rows)
        key = jnp.where(inside, (place[SP] ^ d) * rows + at - d * rows, key)
    start = jnp.zeros(shape, jnp.int32)
    total = jnp.int32(0)
    for c in range(lengths.shape[0]):
        start = jnp.where(own >= total, total, start)
        total = total + lengths[c]
    allowed = jnp.where((key >= start) & (key <= own), 0.0, -1e30)
    to_cont = to_cont + jnp.concatenate([allowed] * heads, axis=0)
    peak = jnp.maximum(
        jnp.max(to_prompt, axis=1, keepdims=True), jnp.max(to_cont, axis=1, keepdims=True)
    )
    to_prompt = jnp.exp(to_prompt - peak)
    to_cont = jnp.exp(to_cont - peak)
    divisor = jnp.sum(to_prompt, axis=1, keepdims=True) + jnp.sum(to_cont, axis=1, keepdims=True)
    result = jnp.dot(
        (to_prompt / divisor).astype(BF16), prompt[:, size:], preferred_element_type=F32
    ) + jnp.dot((to_cont / divisor).astype(BF16), cont[:, size:], preferred_element_type=F32)
    for h in range(heads):
        out[:, h * size : (h + 1) * size] = result[h * rows : (h + 1) * rows].astype(BF16)


def attend(place, lengths, mine, near, far, cosine, sine, gain, pairs, prompt_rows):
    rows, width = far.shape
    args = (mine, near, far, cosine, sine, gain, *pairs)
    out = shape_of((rows, width), BF16)
    keys = len(pairs) * pairs[0].shape[0]
    return call(
        functools.partial(attend_kernel, len(pairs), prompt_rows),
        place,
        (1,),
        [pl.BlockSpec(memory_space=pltpu.SMEM)] + [whole(a) for a in args],
        whole(out),
        out,
        (lengths, *args),
        (4 * rows * width * keys, 10 * rows * width + 512 * keys),
    )


def out_kernel(count, direct, place, *refs):
    heads, weight, outs, part = refs[:count], refs[count], refs[count + 1 : -1], refs[-1]
    rows = heads[0].shape[0]
    left = jnp.concatenate([head[...] for head in heads], axis=0)
    total = jnp.dot(left, weight[...], preferred_element_type=F32).astype(BF16)
    if direct:
        for d in range(count):
            part[d] = total[d * rows : (d + 1) * rows]
        for e in range(count):
            outs[e][...] = part[place[TP] ^ e ^ place[SP]]
    else:
        for d in range(count):
            outs[d][...] = total[d * rows : (d + 1) * rows]


def out_parts(place, heads, weight, start, stop, step, direct):
    rows, depth = heads[0].shape
    count = len(heads)
    skipped = start // step
    return call(
        functools.partial(out_kernel, count, direct),
        place,
        ((stop - start) // step,),
        [whole(h) for h in heads]
        + [pl.BlockSpec((depth, step), lambda i, place: (0, i + skipped))],
        [pl.BlockSpec((rows, step), lambda i, place: (0, i))] * count,
        [shape_of((rows, stop - start), BF16)] * count,
        (*heads, weight),
        (2 * count * rows * depth * (stop - start), 2 * depth * (stop - start)),
        [pltpu.VMEM((count, rows, step), BF16)],
    )


def select_kernel(count, place, *refs):
    ins, outs, held = refs[:count], refs[count:-1], refs[-1]
    for d in range(count):
        held[d] = ins[d][...]
    for e in range(count):
        outs[e][...] = held[place[SP] ^ place[TP] ^ e]


def select(place, blocks):
    count = len(blocks)
    shape = blocks[0].shape
    return call(
        functools.partial(select_kernel, count),
        place,
        (1,),
        [whole(b) for b in blocks],
        [whole(b) for b in blocks],
        [shape_of(shape, BF16)] * count,
        blocks,
        (0, 4 * count * shape[0] * shape[1]),
        [pltpu.VMEM((count, *shape), BF16)],
    )


def final_kernel(count, place, hidden, *refs):
    parts, out = refs[:-1], refs[-1]
    at = 0
    for group in range(0, len(parts), count):
        width = parts[group].shape[1]
        columns = slice(at, at + width)
        total = hidden[:, columns].astype(F32)
        for part in parts[group : group + count]:
            total = total + part[...].astype(F32)
        out[:, columns] = total.astype(BF16)
        at += width


def final_sum(place, parts, hidden, count):
    rows, width = hidden.shape
    return call(
        functools.partial(final_kernel, count),
        place,
        (1,),
        [whole(a) for a in (hidden, *parts)],
        whole(hidden),
        shape_of((rows, width), BF16),
        (hidden, *parts),
        (count * rows * width, 12 * rows * width),
    )


def after(arrays, *others):
    return lax.optimization_barrier((arrays, others))[0]


def swap(array, axis, bits):
    return lax.ppermute(array, axis, [(i, i ^ bits) for i in range(lax.axis_size(axis))])


def swap_bits(count):
    bits = []
    bit = 1
    while bit < count:
        bits.append(bit)
        bit *= 2
    return bits


def gather_blocks(block, axis, count):
    held = {0: block}
    bits = swap_bits(count)
    for bit in bits[1:] + bits[:1]:
        held.update({d ^ bit: swap(held[d], axis, bit) for d in sorted(held)})
    return [held[d] for d in range(count)]


def other_halves(half, axis, count):
    firsts = {0: half}
    for bit in swap_bits(count)[1:]:
        firsts.update({d ^ bit: swap(firsts[d], axis, bit) for d in sorted(firsts)})
    del firsts[0]
    return firsts


def both_cores(held, axis):
    return {**held, **{d ^ 1: swap(held[d], axis, 1) for d in sorted(held)}}


def sum_blocks(keep, send, axis, count):
    near = swap(send, axis, 1)
    rows = keep.shape[0] // (count // 2)
    held = {
        d: keep[d // 2 * rows :][:rows] + near[d // 2 * rows :][:rows]
        for d in range(0, count, 2)
    }
    far = 0.0
    for bit in swap_bits(count)[1:]:
        sent = [d for d in sorted(held) if d & bit]
        got = {d ^ bit: swap(held[d], axis, bit) for d in sent}
        far = far + got.pop(0)
        held = {d: held[d] + got[d] for d in got}
    return keep, near, far


def tables(positions, size):
    half = size // 2
    frequency = jnp.exp(jnp.arange(half, dtype=F32) * (-2.0 * math.log(1000000.0) / size))
    angles = positions.astype(F32)[:, None] * frequency[None, :]
    cosine = jnp.cos(angles)
    sine = jnp.sin(angles)
    return (
        jnp.concatenate([cosine, cosine], axis=1),
        jnp.concatenate([-sine, sine], axis=1),
    )


def on_device(
    hidden_cont,
    hidden_prompt,
    norm_gain,
    query_weight,
    keyval_weight,
    out_weight,
    query_gain,
    key_gain,
    sample_lengths,
):
    size = query_gain.shape[0]
    heads_here = query_weight.shape[1] // size
    cont_rows = hidden_cont.shape[0]
    prompt_rows = hidden_prompt.shape[0]
    sp_index = lax.axis_index("sp")
    sp_count = lax.axis_size("sp")
    tp_index = lax.axis_index("tp")
    assert lax.axis_size("tp") == sp_count and lax.axis_size("groups") == 2
    place = jnp.stack(
        [
            sp_index,
            tp_index,
            lax.axis_index("groups"),
            tp_index * heads_here // (QH // KVH),
        ]
    ).astype(jnp.int32)
    norm_gain = norm_gain[None, :]
    query_gain = query_gain[None, :]
    key_gain = key_gain[None, :]

    half, both, *sent, cont = first_step(
        place, keyval_weight, hidden_cont, norm_gain, size, sp_count
    )
    halves = other_halves(half, "sp", sp_count)
    partner = swap(both, "sp", 1)
    got = [swap(block, "sp", d) for d, block in enumerate(sent, 1)]
    prompt, near_pair = near_keyval(place, hidden_prompt, norm_gain, cont, both, partner)

    index = sp_index * cont_rows + jnp.arange(cont_rows, dtype=jnp.int32)
    starts = jnp.cumsum(sample_lengths, dtype=jnp.int32) - sample_lengths
    start = jnp.max(jnp.where(index[:, None] >= starts[None, :], starts[None, :], 0), axis=1)
    prompt_pos = sp_index * prompt_rows + jnp.arange(prompt_rows, dtype=jnp.int32)
    positions = jnp.concatenate([prompt_pos, prompt_rows * sp_count + index - start])
    cosine, sine = tables(positions, size)

    halves = after(halves, near_pair, cosine, sine)
    others = {d: swap(half, "groups", 1) for d, half in halves.items()}
    halves = both_cores(halves, "sp")
    got = after(got, halves)
    keep, send = query_parts(place, [cont] + got, query_weight)
    mine, near, far = sum_blocks(keep, send, "sp", sp_count)
    others = both_cores(after(others, near), "sp")
    weights = [held[d] for d in range(2, sp_count) for held in (halves, others)]
    pair = keyval_rows(place, prompt, cont, cosine, sine, key_gain, near_pair, weights)
    pairs = gather_blocks(pair, "sp", sp_count)
    heads = attend(
        place,
        sample_lengths,
        mine,
        near,
        far,
        cosine[prompt_rows:],
        sine[prompt_rows:],
        query_gain,
        pairs,
        prompt_rows,
    )
    all_heads = gather_blocks(heads, "sp", sp_count)
    width = out_weight.shape[1]
    step = 256 if width % 256 == 0 else width
    split = 2 * step if width > 2 * step else width
    stepped = []
    if split < width:
        stepped = out_parts(place, all_heads, out_weight, split, width, step, False)
        stepped = [stepped[0]] + [swap(stepped[d], "sp", d) for d in range(1, sp_count)]
    parts = [
        lax.ppermute(
            part,
            ("tp", "sp"),
            [
                (t * sp_count + s, s * sp_count + (t ^ e))
                for t in range(sp_count)
                for s in range(sp_count)
            ],
        )
        for e, part in enumerate(
            out_parts(place, all_heads, out_weight, 0, split, step, True)
        )
    ]
    if stepped:
        stepped = select(place, stepped)
        parts += [stepped[0]] + [swap(stepped[e], "tp", e) for e in range(1, sp_count)]
    hidden = lax.dynamic_slice_in_dim(hidden_cont, tp_index * width, width, 1)
    return final_sum(place, parts, hidden, sp_count)


def solution(mesh):
    placed = (
        P(("groups", "sp"), None),
        P(("groups", "sp"), None),
        P(),
        P("sp", "tp"),
        P("sp", None),
        P("tp", "sp"),
        P(),
        P(),
        P("groups"),
    )
    return jax.shard_map(
        on_device, mesh=mesh, in_specs=placed, out_specs=P(("groups", "sp"), "tp"), check_vma=False
    )
```

```python
import functools
import math

import jax
import jax.numpy as jnp
from jax import lax
from jax.experimental import pallas as pl
from jax.experimental.pallas import tpu as pltpu
from jax.sharding import PartitionSpec as P

QH = 32
KVH = 4
SP, TP, GROUP, HEAD = range(4)
BF16 = jnp.bfloat16
F32 = jnp.float32
ROOM = 24 * 1024 * 1024


def call(kernel, place, grid, in_specs, out_specs, out_shape, args, cost, scratch=()):
    flops, moved = cost
    return pl.pallas_call(
        kernel,
        out_shape=out_shape,
        grid_spec=pltpu.PrefetchScalarGridSpec(
            num_scalar_prefetch=1,
            grid=grid,
            in_specs=in_specs,
            out_specs=out_specs,
            scratch_shapes=scratch,
        ),
        compiler_params=pltpu.CompilerParams(vmem_limit_bytes=ROOM),
        cost_estimate=pl.CostEstimate(flops=flops, bytes_accessed=moved, transcendentals=0),
    )(place, *args)


def whole(array):
    zeros = (0,) * array.ndim
    return pl.BlockSpec(array.shape, lambda i, place: zeros)


def shape_of(shape, dtype):
    return jax.ShapeDtypeStruct(shape, dtype)


def rms_rows(values, gain):
    return values * lax.rsqrt(jnp.mean(values * values, axis=-1, keepdims=True) + 1e-06) * gain


def split_normed(hidden, gain, out):
    count, _, depth = out.shape
    normed = rms_rows(hidden[...].astype(F32), gain[...]).astype(BF16)
    for j in range(count):
        out[j] = normed[:, j * depth : (j + 1) * depth]


def norm_kernel(place, hidden, gain, out):
    split_normed(hidden, gain, out)


def norm_split(place, hidden, gain, count):
    rows, width = hidden.shape
    step = min(rows, 64)
    out = (count, rows, width // count)
    return call(
        norm_kernel,
        place,
        (rows // step,),
        [pl.BlockSpec((step, width), lambda i, place: (i, 0)), whole(gain)],
        pl.BlockSpec((count, step, width // count), lambda i, place: (0, i, 0)),
        shape_of(out, BF16),
        (hidden, gain),
        (4 * rows * width, 4 * rows * width),
    )


def pick_kernel(place, first, key, value, half, both):
    size = half.shape[1]
    half[...] = first[...]
    both[:, :size] = key[...]
    both[:, size:] = value[...]


def pick_columns(place, weight, size):
    depth = weight.shape[0]
    block = (depth, size)
    outs = [shape_of(block, BF16), shape_of((depth, 2 * size), BF16)]
    return call(
        pick_kernel,
        place,
        (1,),
        [
            pl.BlockSpec(block, lambda i, place: (0, 2 * place[HEAD] + place[GROUP])),
            pl.BlockSpec(block, lambda i, place: (0, 2 * place[HEAD])),
            pl.BlockSpec(block, lambda i, place: (0, 2 * place[HEAD] + 1)),
        ],
        [whole(out) for out in outs],
        outs,
        (weight, weight, weight),
        (0, 12 * depth * size),
    )


def query_kernel(count, place, rows, weight, *outs):
    block = rows.shape[1]
    left = jnp.concatenate([rows[place[SP] ^ d] for d in range(count)], axis=0)
    part = jnp.dot(left, weight[...], preferred_element_type=F32)
    for d in range(count):
        outs[d][...] = part[d * block : (d + 1) * block]


def query_parts(place, rows, weight):
    count, block, depth = rows.shape
    width = weight.shape[1]
    step = min(width, 256)
    return call(
        functools.partial(query_kernel, count),
        place,
        (width // step,),
        [whole(rows), pl.BlockSpec((depth, step), lambda i, place: (0, i))],
        [pl.BlockSpec((block, step), lambda i, place: (0, i))] * count,
        [shape_of((block, width), F32)] * count,
        (rows, weight),
        (2 * count * block * depth * width, 2 * depth * width),
    )


def turn(values, cosine, sine):
    return values * cosine + pltpu.roll(values, values.shape[-1] // 2, 1) * sine


def near_kernel(place, hidden, norm_gain, cont, own, partner, prompt, out):
    split_normed(hidden, norm_gain, prompt)
    total = 0.0
    for d, weight in ((0, own), (1, partner)):
        left = jnp.concatenate([prompt[place[SP] ^ d], cont[place[SP] ^ d]], axis=0)
        total = total + jnp.dot(left, weight[...], preferred_element_type=F32)
    out[...] = total


def near_keyval(place, hidden, norm_gain, cont, own, partner):
    args = (hidden, norm_gain, cont, own, partner)
    count, cont_rows, depth = cont.shape
    prompt_rows = hidden.shape[0]
    rows = prompt_rows + cont_rows
    width = own.shape[1]
    outs = [shape_of((count, prompt_rows, depth), BF16), shape_of((rows, width), F32)]
    return call(
        near_kernel,
        place,
        (1,),
        [whole(a) for a in args],
        [whole(out) for out in outs],
        outs,
        args,
        (4 * rows * depth * width, 4 * depth * (rows * count + width)),
    )


def keyval_kernel(count, place, prompt, cont, cosine, sine, gain, near, *refs):
    weights, out = refs[:-1], refs[-1]
    size = gain.shape[1]
    total = 0.0
    for d in range(2, count):
        left = jnp.concatenate([prompt[place[SP] ^ d], cont[place[SP] ^ d]], axis=0)
        weight = jnp.concatenate([weights[2 * d - 4][...], weights[2 * d - 3][...]], axis=1)
        total = total + jnp.dot(left, weight, preferred_element_type=F32)
    swapped = place[GROUP] == 1
    first, second = total[:, :size], total[:, size:]
    key = near[:, :size] + jnp.where(swapped, second, first)
    value = near[:, size:] + jnp.where(swapped, first, second)
    out[:, :size] = turn(rms_rows(key, gain[...]), cosine[...], sine[...]).astype(BF16)
    out[:, size:] = value.astype(BF16)


def keyval_rows(place, prompt, cont, cosine, sine, gain, near, weights):
    count, prompt_rows, depth = prompt.shape
    rows = prompt_rows + cont.shape[1]
    size = gain.shape[1]
    args = (prompt, cont, cosine, sine, gain, near, *weights)
    out = shape_of((rows, 2 * size), BF16)
    return call(
        functools.partial(keyval_kernel, count),
        place,
        (1,),
        [whole(a) for a in args],
        whole(out),
        out,
        args,
        (2 * rows * count * depth * size, count * depth * (rows + 2 * size)),
    )


def attend_kernel(count, prompt_rows, place, lengths, mine, other, cosine, sine, gain, *refs):
    pairs, out = refs[:-1], refs[-1]
    rows, width = mine.shape
    size = gain.shape[1]
    heads = width // size
    queries = []
    for h in range(heads):
        part = slice(h * size, (h + 1) * size)
        value = rms_rows(mine[:, part] + other[:, part], gain[...])
        queries.append(turn(value, cosine[...], sine[...]).astype(BF16))
    queries = jnp.concatenate(queries, axis=0)
    prompt = jnp.concatenate([pair[:prompt_rows] for pair in pairs], axis=0)
    cont = jnp.concatenate([pair[prompt_rows:] for pair in pairs], axis=0)
    scale = 1.0 / math.sqrt(size)
    by_rows = (((1,), (1,)), ((), ()))
    to_prompt = (
        lax.dot_general(queries, prompt[:, :size], by_rows, preferred_element_type=F32) * scale
    )
    to_cont = (
        lax.dot_general(queries, cont[:, :size], by_rows, preferred_element_type=F32) * scale
    )
    shape = (rows, cont.shape[0])
    own = place[SP] * rows + lax.broadcasted_iota(jnp.int32, shape, 0)
    at = lax.broadcasted_iota(jnp.int32, shape, 1)
    key = jnp.zeros(shape, jnp.int32)
    for d in range(count):
        inside = (at >= d * rows) & (at < (d + 1) * rows)
        key = jnp.where(inside, (place[SP] ^ d) * rows + at - d * rows, key)
    start = jnp.zeros(shape, jnp.int32)
    total = jnp.int32(0)
    for c in range(lengths.shape[0]):
        start = jnp.where(own >= total, total, start)
        total = total + lengths[c]
    allowed = jnp.where((key >= start) & (key <= own), 0.0, -1e30)
    to_cont = to_cont + jnp.concatenate([allowed] * heads, axis=0)
    peak = jnp.maximum(
        jnp.max(to_prompt, axis=1, keepdims=True), jnp.max(to_cont, axis=1, keepdims=True)
    )
    to_prompt = jnp.exp(to_prompt - peak)
    to_cont = jnp.exp(to_cont - peak)
    divisor = jnp.sum(to_prompt, axis=1, keepdims=True) + jnp.sum(to_cont, axis=1, keepdims=True)
    result = jnp.dot(
        (to_prompt / divisor).astype(BF16), prompt[:, size:], preferred_element_type=F32
    ) + jnp.dot((to_cont / divisor).astype(BF16), cont[:, size:], preferred_element_type=F32)
    for h in range(heads):
        out[:, h * size : (h + 1) * size] = result[h * rows : (h + 1) * rows].astype(BF16)


def attend(place, lengths, mine, other, cosine, sine, gain, pairs, prompt_rows):
    rows, width = mine.shape
    args = (mine, other, cosine, sine, gain, *pairs)
    out = shape_of((rows, width), BF16)
    keys = len(pairs) * pairs[0].shape[0]
    return call(
        functools.partial(attend_kernel, len(pairs), prompt_rows),
        place,
        (1,),
        [pl.BlockSpec(memory_space=pltpu.SMEM)] + [whole(a) for a in args],
        whole(out),
        out,
        (lengths, *args),
        (4 * rows * width * keys, 10 * rows * width + 512 * keys),
    )


def out_kernel(count, place, *refs):
    heads, weights, outs, part = refs[: 2 * count], refs[-count - 3 : -count - 1], refs[-count - 1 : -1], refs[-1]
    rows = heads[0].shape[0]
    total = 0.0
    for side, weight in enumerate(weights):
        left = jnp.concatenate([h[...] for h in heads[side * count : (side + 1) * count]], axis=0)
        share = jnp.dot(left, weight[...], preferred_element_type=F32)
        total = total + share.astype(BF16).astype(F32)
    total = total.astype(BF16)
    for d in range(count):
        part[d] = total[d * rows : (d + 1) * rows]
    for e in range(count):
        outs[e][...] = part[place[TP] ^ e ^ place[SP]]


def out_parts(place, heads, weights):
    count = len(heads) // 2
    rows = heads[0].shape[0]
    depth, width = weights[0].shape
    args = (*heads, *weights)
    return call(
        functools.partial(out_kernel, count),
        place,
        (1,),
        [whole(a) for a in args],
        [pl.BlockSpec((rows, width), lambda i, place: (0, 0))] * count,
        [shape_of((rows, width), BF16)] * count,
        args,
        (4 * count * rows * depth * width, 4 * depth * width),
        [pltpu.VMEM((count, rows, width), BF16)],
    )


def final_kernel(count, place, hidden, *refs):
    parts, out = refs[:-1], refs[-1]
    width = parts[0].shape[1]
    sums = [0.0, 0.0]
    for e, part in enumerate(parts):
        sums[e % 2] = sums[e % 2] + part[...].astype(F32)
    odd = place[SP] % 2 == 1
    left = jnp.where(odd, sums[1], sums[0])
    right = jnp.where(odd, sums[0], sums[1])
    out[:, :width] = (hidden[:, :width].astype(F32) + left).astype(BF16)
    out[:, width:] = (hidden[:, width:].astype(F32) + right).astype(BF16)


def final_sum(place, parts, hidden):
    rows, width = hidden.shape
    count = len(parts)
    return call(
        functools.partial(final_kernel, count),
        place,
        (1,),
        [whole(a) for a in (hidden, *parts)],
        whole(hidden),
        shape_of((rows, width), BF16),
        (hidden, *parts),
        (count * rows * width, 12 * rows * width),
    )


def after(arrays, *others):
    return lax.optimization_barrier((arrays, others))[0]


def swap(array, axis, bits):
    return lax.ppermute(array, axis, [(i, i ^ bits) for i in range(lax.axis_size(axis))])


def swap_both(array, tp_bits, sp_bits, count):
    pairs = [
        (t * count + s, (t ^ tp_bits) * count + (s ^ sp_bits))
        for t in range(count)
        for s in range(count)
    ]
    return lax.ppermute(array, ("tp", "sp"), pairs)


def swap_bits(count):
    bits = []
    bit = 1
    while bit < count:
        bits.append(bit)
        bit *= 2
    return bits


def gather_blocks(block, axis, count):
    held = {0: block}
    bits = swap_bits(count)
    for bit in bits[1:] + bits[:1]:
        held.update({d ^ bit: swap(held[d], axis, bit) for d in sorted(held)})
    return [held[d] for d in range(count)]


def other_halves(half, axis, count):
    firsts = {0: half}
    for bit in swap_bits(count)[1:]:
        firsts.update({d ^ bit: swap(firsts[d], axis, bit) for d in sorted(firsts)})
    del firsts[0]
    return firsts


def both_cores(held, axis):
    return {**held, **{d ^ 1: swap(held[d], axis, 1) for d in sorted(held)}}


def sum_blocks(blocks, axis, count):
    held = dict(enumerate(blocks))
    bits = swap_bits(count)
    for bit in bits:
        sent = [d for d in sorted(held) if d & bit]
        got = {d ^ bit: swap(held[d], axis, bit) for d in sent}
        if bit == bits[-1]:
            return held[0], got[0]
        held = {d: held[d] + got[d] for d in got}


def tables(positions, size):
    half = size // 2
    frequency = jnp.exp(jnp.arange(half, dtype=F32) * (-2.0 * math.log(1000000.0) / size))
    angles = positions.astype(F32)[:, None] * frequency[None, :]
    cosine = jnp.cos(angles)
    sine = jnp.sin(angles)
    return (
        jnp.concatenate([cosine, cosine], axis=1),
        jnp.concatenate([-sine, sine], axis=1),
    )


def on_device(
    hidden_cont,
    hidden_prompt,
    norm_gain,
    query_weight,
    keyval_weight,
    out_weight,
    query_gain,
    key_gain,
    sample_lengths,
):
    size = query_gain.shape[0]
    heads_here = query_weight.shape[1] // size
    cont_rows = hidden_cont.shape[0]
    prompt_rows = hidden_prompt.shape[0]
    sp_index = lax.axis_index("sp")
    sp_count = lax.axis_size("sp")
    tp_index = lax.axis_index("tp")
    assert lax.axis_size("tp") == sp_count and lax.axis_size("groups") == 2
    place = jnp.stack(
        [
            sp_index,
            tp_index,
            lax.axis_index("groups"),
            tp_index * heads_here // (QH // KVH),
        ]
    ).astype(jnp.int32)
    norm_gain = norm_gain[None, :]
    query_gain = query_gain[None, :]
    key_gain = key_gain[None, :]

    cont = norm_split(place, hidden_cont, norm_gain, sp_count)
    half, both = pick_columns(place, keyval_weight, size)
    cont_all = lax.all_to_all(cont, "sp", 0, 0, tiled=True)
    halves = other_halves(half, "sp", sp_count)
    partner = swap(both, "sp", 1)
    prompt, near_pair = near_keyval(place, hidden_prompt, norm_gain, cont, both, partner)

    index = sp_index * cont_rows + jnp.arange(cont_rows, dtype=jnp.int32)
    starts = jnp.cumsum(sample_lengths, dtype=jnp.int32) - sample_lengths
    start = jnp.max(jnp.where(index[:, None] >= starts[None, :], starts[None, :], 0), axis=1)
    prompt_pos = sp_index * prompt_rows + jnp.arange(prompt_rows, dtype=jnp.int32)
    positions = jnp.concatenate([prompt_pos, prompt_rows * sp_count + index - start])
    cosine, sine = tables(positions, size)

    halves = after(halves, near_pair)
    others = {d: swap(half, "groups", 1) for d, half in halves.items()}
    halves = both_cores(halves, "sp")
    others = both_cores(others, "sp")
    width = out_weight.shape[1]
    side = tp_index % 2
    out_early = after(out_weight, near_pair)
    sent = lax.dynamic_slice_in_dim(out_early, (1 - side) * (width // 2), width // 2, 1)
    out_weights = [
        lax.dynamic_slice_in_dim(out_early, side * (width // 2), width // 2, 1),
        swap(sent, "tp", 1),
    ]

    parts = query_parts(place, cont_all, query_weight)
    mine, other = sum_blocks(parts, "sp", sp_count)
    weights = [held[d] for d in range(2, sp_count) for held in (halves, others)]
    pair = keyval_rows(place, prompt, cont, cosine, sine, key_gain, near_pair, weights)
    pairs = gather_blocks(pair, "sp", sp_count)
    heads = attend(
        place,
        sample_lengths,
        mine,
        other,
        cosine[prompt_rows:],
        sine[prompt_rows:],
        query_gain,
        pairs,
        prompt_rows,
    )
    chips = range(0, sp_count, 2)
    near_heads = {d: swap(heads, "sp", d) if d else heads for d in chips}
    far_heads = {d: swap_both(heads, 1, d, sp_count) for d in chips}
    near_heads = both_cores(near_heads, "sp")
    far_heads = both_cores(far_heads, "sp")
    all_heads = [held[d] for held in (near_heads, far_heads) for d in range(sp_count)]
    parts = out_parts(place, all_heads, out_weights)
    parts = [
        lax.ppermute(
            part,
            ("tp", "sp"),
            [
                (t * sp_count + s, s * sp_count + (t ^ e))
                for t in range(sp_count)
                for s in range(sp_count)
            ],
        )
        for e, part in enumerate(parts)
    ]
    hidden = lax.dynamic_slice_in_dim(hidden_cont, tp_index * width, width, 1)
    return final_sum(place, parts, hidden)


def solution(mesh):
    placed = (
        P(("groups", "sp"), None),
        P(("groups", "sp"), None),
        P(),
        P("sp", "tp"),
        P("sp", None),
        P("tp", "sp"),
        P(),
        P(),
        P("groups"),
    )
    return jax.shard_map(
        on_device, mesh=mesh, in_specs=placed, out_specs=P(("groups", "sp"), "tp"), check_vma=False
    )
```

```python
import functools
import math

import jax
import jax.numpy as jnp
from jax import lax
from jax.experimental import pallas as pl
from jax.experimental.pallas import tpu as pltpu
from jax.sharding import PartitionSpec as P

QH = 32
KVH = 4
SP, TP, GROUP, HEAD = range(4)
BF16 = jnp.bfloat16
F32 = jnp.float32
ROOM = 24 * 1024 * 1024


def call(kernel, place, grid, in_specs, out_specs, out_shape, args, cost, scratch=()):
    flops, moved = cost
    return pl.pallas_call(
        kernel,
        out_shape=out_shape,
        grid_spec=pltpu.PrefetchScalarGridSpec(
            num_scalar_prefetch=1,
            grid=grid,
            in_specs=in_specs,
            out_specs=out_specs,
            scratch_shapes=scratch,
        ),
        compiler_params=pltpu.CompilerParams(vmem_limit_bytes=ROOM),
        cost_estimate=pl.CostEstimate(flops=flops, bytes_accessed=moved, transcendentals=0),
    )(place, *args)


def whole(array):
    zeros = (0,) * array.ndim
    return pl.BlockSpec(array.shape, lambda i, place: zeros)


def shape_of(shape, dtype):
    return jax.ShapeDtypeStruct(shape, dtype)


def rms_rows(values, gain):
    return values * lax.rsqrt(jnp.mean(values * values, axis=-1, keepdims=True) + 1e-06) * gain


def split_normed(hidden, gain, out):
    count, _, depth = out.shape
    normed = rms_rows(hidden[...].astype(F32), gain[...]).astype(BF16)
    for j in range(count):
        out[j] = normed[:, j * depth : (j + 1) * depth]


def norm_kernel(place, hidden, gain, out):
    split_normed(hidden, gain, out)


def norm_split(place, hidden, gain, count):
    rows, width = hidden.shape
    step = min(rows, 64)
    out = (count, rows, width // count)
    return call(
        norm_kernel,
        place,
        (rows // step,),
        [pl.BlockSpec((step, width), lambda i, place: (i, 0)), whole(gain)],
        pl.BlockSpec((count, step, width // count), lambda i, place: (0, i, 0)),
        shape_of(out, BF16),
        (hidden, gain),
        (4 * rows * width, 4 * rows * width),
    )


def pick_kernel(place, first, key, value, half, both):
    size = half.shape[1]
    half[...] = first[...]
    both[:, :size] = key[...]
    both[:, size:] = value[...]


def pick_columns(place, weight, size):
    depth = weight.shape[0]
    block = (depth, size)
    outs = [shape_of(block, BF16), shape_of((depth, 2 * size), BF16)]
    return call(
        pick_kernel,
        place,
        (1,),
        [
            pl.BlockSpec(block, lambda i, place: (0, 2 * place[HEAD] + place[GROUP])),
            pl.BlockSpec(block, lambda i, place: (0, 2 * place[HEAD])),
            pl.BlockSpec(block, lambda i, place: (0, 2 * place[HEAD] + 1)),
        ],
        [whole(out) for out in outs],
        outs,
        (weight, weight, weight),
        (0, 12 * depth * size),
    )


def query_kernel(count, place, rows, weight, *outs):
    block = rows.shape[1]
    left = jnp.concatenate([rows[place[SP] ^ d] for d in range(count)], axis=0)
    part = jnp.dot(left, weight[...], preferred_element_type=F32)
    for d in range(count):
        outs[d][...] = part[d * block : (d + 1) * block]


def query_parts(place, rows, weight):
    count, block, depth = rows.shape
    width = weight.shape[1]
    step = min(width, 256)
    return call(
        functools.partial(query_kernel, count),
        place,
        (width // step,),
        [whole(rows), pl.BlockSpec((depth, step), lambda i, place: (0, i))],
        [pl.BlockSpec((block, step), lambda i, place: (0, i))] * count,
        [shape_of((block, width), F32)] * count,
        (rows, weight),
        (2 * count * block * depth * width, 2 * depth * width),
    )


def turn(values, cosine, sine):
    return values * cosine + pltpu.roll(values, values.shape[-1] // 2, 1) * sine


def near_kernel(place, hidden, norm_gain, cont, own, partner, prompt, out):
    split_normed(hidden, norm_gain, prompt)
    total = 0.0
    for d, weight in ((0, own), (1, partner)):
        left = jnp.concatenate([prompt[place[SP] ^ d], cont[place[SP] ^ d]], axis=0)
        total = total + jnp.dot(left, weight[...], preferred_element_type=F32)
    out[...] = total


def near_keyval(place, hidden, norm_gain, cont, own, partner):
    args = (hidden, norm_gain, cont, own, partner)
    count, cont_rows, depth = cont.shape
    prompt_rows = hidden.shape[0]
    rows = prompt_rows + cont_rows
    width = own.shape[1]
    outs = [shape_of((count, prompt_rows, depth), BF16), shape_of((rows, width), F32)]
    return call(
        near_kernel,
        place,
        (1,),
        [whole(a) for a in args],
        [whole(out) for out in outs],
        outs,
        args,
        (4 * rows * depth * width, 4 * depth * (rows * count + width)),
    )


def keyval_kernel(count, place, prompt, cont, cosine, sine, gain, near, *refs):
    weights, out = refs[:-1], refs[-1]
    size = gain.shape[1]
    total = 0.0
    for d in range(2, count):
        left = jnp.concatenate([prompt[place[SP] ^ d], cont[place[SP] ^ d]], axis=0)
        weight = jnp.concatenate([weights[2 * d - 4][...], weights[2 * d - 3][...]], axis=1)
        total = total + jnp.dot(left, weight, preferred_element_type=F32)
    swapped = place[GROUP] == 1
    first, second = total[:, :size], total[:, size:]
    key = near[:, :size] + jnp.where(swapped, second, first)
    value = near[:, size:] + jnp.where(swapped, first, second)
    out[:, :size] = turn(rms_rows(key, gain[...]), cosine[...], sine[...]).astype(BF16)
    out[:, size:] = value.astype(BF16)


def keyval_rows(place, prompt, cont, cosine, sine, gain, near, weights):
    count, prompt_rows, depth = prompt.shape
    rows = prompt_rows + cont.shape[1]
    size = gain.shape[1]
    args = (prompt, cont, cosine, sine, gain, near, *weights)
    out = shape_of((rows, 2 * size), BF16)
    return call(
        functools.partial(keyval_kernel, count),
        place,
        (1,),
        [whole(a) for a in args],
        whole(out),
        out,
        args,
        (2 * rows * count * depth * size, count * depth * (rows + 2 * size)),
    )


def attend_kernel(count, prompt_rows, place, lengths, mine, other, cosine, sine, gain, *refs):
    pairs, out = refs[:-1], refs[-1]
    rows, width = mine.shape
    size = gain.shape[1]
    heads = width // size
    queries = []
    for h in range(heads):
        part = slice(h * size, (h + 1) * size)
        value = rms_rows(mine[:, part] + other[:, part], gain[...])
        queries.append(turn(value, cosine[...], sine[...]).astype(BF16))
    queries = jnp.concatenate(queries, axis=0)
    prompt = jnp.concatenate([pair[:prompt_rows] for pair in pairs], axis=0)
    cont = jnp.concatenate([pair[prompt_rows:] for pair in pairs], axis=0)
    scale = 1.0 / math.sqrt(size)
    by_rows = (((1,), (1,)), ((), ()))
    to_prompt = (
        lax.dot_general(queries, prompt[:, :size], by_rows, preferred_element_type=F32) * scale
    )
    to_cont = (
        lax.dot_general(queries, cont[:, :size], by_rows, preferred_element_type=F32) * scale
    )
    shape = (rows, cont.shape[0])
    own = place[SP] * rows + lax.broadcasted_iota(jnp.int32, shape, 0)
    at = lax.broadcasted_iota(jnp.int32, shape, 1)
    key = jnp.zeros(shape, jnp.int32)
    for d in range(count):
        inside = (at >= d * rows) & (at < (d + 1) * rows)
        key = jnp.where(inside, (place[SP] ^ d) * rows + at - d * rows, key)
    start = jnp.zeros(shape, jnp.int32)
    total = jnp.int32(0)
    for c in range(lengths.shape[0]):
        start = jnp.where(own >= total, total, start)
        total = total + lengths[c]
    allowed = jnp.where((key >= start) & (key <= own), 0.0, -1e30)
    to_cont = to_cont + jnp.concatenate([allowed] * heads, axis=0)
    peak = jnp.maximum(
        jnp.max(to_prompt, axis=1, keepdims=True), jnp.max(to_cont, axis=1, keepdims=True)
    )
    to_prompt = jnp.exp(to_prompt - peak)
    to_cont = jnp.exp(to_cont - peak)
    divisor = jnp.sum(to_prompt, axis=1, keepdims=True) + jnp.sum(to_cont, axis=1, keepdims=True)
    result = jnp.dot(
        (to_prompt / divisor).astype(BF16), prompt[:, size:], preferred_element_type=F32
    ) + jnp.dot((to_cont / divisor).astype(BF16), cont[:, size:], preferred_element_type=F32)
    for h in range(heads):
        out[:, h * size : (h + 1) * size] = result[h * rows : (h + 1) * rows].astype(BF16)


def attend(place, lengths, mine, other, cosine, sine, gain, pairs, prompt_rows):
    rows, width = mine.shape
    args = (mine, other, cosine, sine, gain, *pairs)
    out = shape_of((rows, width), BF16)
    keys = len(pairs) * pairs[0].shape[0]
    return call(
        functools.partial(attend_kernel, len(pairs), prompt_rows),
        place,
        (1,),
        [pl.BlockSpec(memory_space=pltpu.SMEM)] + [whole(a) for a in args],
        whole(out),
        out,
        (lengths, *args),
        (4 * rows * width * keys, 10 * rows * width + 512 * keys),
    )


def out_kernel(count, place, *refs):
    heads, weights, outs, part = refs[: 2 * count], refs[-count - 3 : -count - 1], refs[-count - 1 : -1], refs[-1]
    rows = heads[0].shape[0]
    total = 0.0
    for side, weight in enumerate(weights):
        left = jnp.concatenate([h[...] for h in heads[side * count : (side + 1) * count]], axis=0)
        share = jnp.dot(left, weight[...], preferred_element_type=F32)
        total = total + share.astype(BF16).astype(F32)
    total = total.astype(BF16)
    for d in range(count):
        part[d] = total[d * rows : (d + 1) * rows]
    for e in range(count):
        outs[e][...] = part[place[TP] ^ e ^ place[SP]]


def out_parts(place, heads, weights):
    count = len(heads) // 2
    rows = heads[0].shape[0]
    depth, width = weights[0].shape
    args = (*heads, *weights)
    return call(
        functools.partial(out_kernel, count),
        place,
        (1,),
        [whole(a) for a in args],
        [pl.BlockSpec((rows, width), lambda i, place: (0, 0))] * count,
        [shape_of((rows, width), BF16)] * count,
        args,
        (4 * count * rows * depth * width, 4 * depth * width),
        [pltpu.VMEM((count, rows, width), BF16)],
    )


def final_kernel(count, place, hidden, *refs):
    parts, out = refs[:-1], refs[-1]
    width = parts[0].shape[1]
    sums = [0.0, 0.0]
    for e, part in enumerate(parts):
        sums[e % 2] = sums[e % 2] + part[...].astype(F32)
    odd = place[SP] % 2 == 1
    left = jnp.where(odd, sums[1], sums[0])
    right = jnp.where(odd, sums[0], sums[1])
    out[:, :width] = (hidden[:, :width].astype(F32) + left).astype(BF16)
    out[:, width:] = (hidden[:, width:].astype(F32) + right).astype(BF16)


def final_sum(place, parts, hidden):
    rows, width = hidden.shape
    count = len(parts)
    return call(
        functools.partial(final_kernel, count),
        place,
        (1,),
        [whole(a) for a in (hidden, *parts)],
        whole(hidden),
        shape_of((rows, width), BF16),
        (hidden, *parts),
        (count * rows * width, 12 * rows * width),
    )


def after(arrays, *others):
    return lax.optimization_barrier((arrays, others))[0]


def swap(array, axis, bits):
    return lax.ppermute(array, axis, [(i, i ^ bits) for i in range(lax.axis_size(axis))])


def swap_both(array, tp_bits, sp_bits, count):
    pairs = [
        (t * count + s, (t ^ tp_bits) * count + (s ^ sp_bits))
        for t in range(count)
        for s in range(count)
    ]
    return lax.ppermute(array, ("tp", "sp"), pairs)


def swap_bits(count):
    bits = []
    bit = 1
    while bit < count:
        bits.append(bit)
        bit *= 2
    return bits


def gather_blocks(block, axis, count):
    held = {0: block}
    bits = swap_bits(count)
    for bit in bits[1:] + bits[:1]:
        held.update({d ^ bit: swap(held[d], axis, bit) for d in sorted(held)})
    return [held[d] for d in range(count)]


def other_halves(half, axis, count):
    firsts = {0: half}
    for bit in swap_bits(count)[1:]:
        firsts.update({d ^ bit: swap(firsts[d], axis, bit) for d in sorted(firsts)})
    del firsts[0]
    return firsts


def both_cores(held, axis):
    return {**held, **{d ^ 1: swap(held[d], axis, 1) for d in sorted(held)}}


def sum_blocks(blocks, axis, count):
    held = dict(enumerate(blocks))
    bits = swap_bits(count)
    for bit in bits:
        sent = [d for d in sorted(held) if d & bit]
        got = {d ^ bit: swap(held[d], axis, bit) for d in sent}
        if bit == bits[-1]:
            return held[0], got[0]
        held = {d: held[d] + got[d] for d in got}


def tables(positions, size):
    half = size // 2
    frequency = jnp.exp(jnp.arange(half, dtype=F32) * (-2.0 * math.log(1000000.0) / size))
    angles = positions.astype(F32)[:, None] * frequency[None, :]
    cosine = jnp.cos(angles)
    sine = jnp.sin(angles)
    return (
        jnp.concatenate([cosine, cosine], axis=1),
        jnp.concatenate([-sine, sine], axis=1),
    )


def on_device(
    hidden_cont,
    hidden_prompt,
    norm_gain,
    query_weight,
    keyval_weight,
    out_weight,
    query_gain,
    key_gain,
    sample_lengths,
):
    size = query_gain.shape[0]
    heads_here = query_weight.shape[1] // size
    cont_rows = hidden_cont.shape[0]
    prompt_rows = hidden_prompt.shape[0]
    sp_index = lax.axis_index("sp")
    sp_count = lax.axis_size("sp")
    tp_index = lax.axis_index("tp")
    assert lax.axis_size("tp") == sp_count and lax.axis_size("groups") == 2
    place = jnp.stack(
        [
            sp_index,
            tp_index,
            lax.axis_index("groups"),
            tp_index * heads_here // (QH // KVH),
        ]
    ).astype(jnp.int32)
    norm_gain = norm_gain[None, :]
    query_gain = query_gain[None, :]
    key_gain = key_gain[None, :]

    cont = norm_split(place, hidden_cont, norm_gain, sp_count)
    half, both = pick_columns(place, keyval_weight, size)
    cont_all = lax.all_to_all(cont, "sp", 0, 0, tiled=True)
    halves = other_halves(half, "sp", sp_count)
    partner = swap(both, "sp", 1)
    prompt, near_pair = near_keyval(place, hidden_prompt, norm_gain, cont, both, partner)

    index = sp_index * cont_rows + jnp.arange(cont_rows, dtype=jnp.int32)
    starts = jnp.cumsum(sample_lengths, dtype=jnp.int32) - sample_lengths
    start = jnp.max(jnp.where(index[:, None] >= starts[None, :], starts[None, :], 0), axis=1)
    prompt_pos = sp_index * prompt_rows + jnp.arange(prompt_rows, dtype=jnp.int32)
    positions = jnp.concatenate([prompt_pos, prompt_rows * sp_count + index - start])
    cosine, sine = tables(positions, size)

    others = {d: swap(half, "groups", 1) for d, half in halves.items()}
    halves = both_cores(halves, "sp")
    others = both_cores(others, "sp")
    width = out_weight.shape[1]
    side = tp_index % 2
    out_early = after(out_weight, near_pair)
    sent = lax.dynamic_slice_in_dim(out_early, (1 - side) * (width // 2), width // 2, 1)
    out_weights = [
        lax.dynamic_slice_in_dim(out_early, side * (width // 2), width // 2, 1),
        swap(sent, "tp", 1),
    ]

    parts = query_parts(place, after(cont_all, near_pair), query_weight)
    mine, other = sum_blocks(parts, "sp", sp_count)
    weights = [held[d] for d in range(2, sp_count) for held in (halves, others)]
    pair = keyval_rows(place, prompt, cont, cosine, sine, key_gain, near_pair, weights)
    pairs = gather_blocks(pair, "sp", sp_count)
    heads = attend(
        place,
        sample_lengths,
        mine,
        other,
        cosine[prompt_rows:],
        sine[prompt_rows:],
        query_gain,
        pairs,
        prompt_rows,
    )
    chips = range(0, sp_count, 2)
    near_heads = {d: swap(heads, "sp", d) if d else heads for d in chips}
    far_heads = {d: swap_both(heads, 1, d, sp_count) for d in chips}
    near_heads = both_cores(near_heads, "sp")
    far_heads = both_cores(far_heads, "sp")
    all_heads = [held[d] for held in (near_heads, far_heads) for d in range(sp_count)]
    parts = out_parts(place, all_heads, out_weights)
    parts = [
        lax.ppermute(
            part,
            ("tp", "sp"),
            [
                (t * sp_count + s, s * sp_count + (t ^ e))
                for t in range(sp_count)
                for s in range(sp_count)
            ],
        )
        for e, part in enumerate(parts)
    ]
    hidden = lax.dynamic_slice_in_dim(hidden_cont, tp_index * width, width, 1)
    return final_sum(place, parts, hidden)


def solution(mesh):
    placed = (
        P(("groups", "sp"), None),
        P(("groups", "sp"), None),
        P(),
        P("sp", "tp"),
        P("sp", None),
        P("tp", "sp"),
        P(),
        P(),
        P("groups"),
    )
    return jax.shard_map(
        on_device, mesh=mesh, in_specs=placed, out_specs=P(("groups", "sp"), "tp"), check_vma=False
    )
```

```python
import functools
import math

import jax
import jax.numpy as jnp
from jax import lax
from jax.experimental import pallas as pl
from jax.experimental.pallas import tpu as pltpu
from jax.sharding import PartitionSpec as P

QH = 32
KVH = 4
SP, TP, GROUP, HEAD = range(4)
BF16 = jnp.bfloat16
F32 = jnp.float32
ROOM = 24 * 1024 * 1024
ALL = 62 * 1024 * 1024


def call(kernel, place, grid, in_specs, out_specs, out_shape, args, cost, scratch=(), room=ROOM):
    flops, moved = cost
    return pl.pallas_call(
        kernel,
        out_shape=out_shape,
        grid_spec=pltpu.PrefetchScalarGridSpec(
            num_scalar_prefetch=1,
            grid=grid,
            in_specs=in_specs,
            out_specs=out_specs,
            scratch_shapes=scratch,
        ),
        compiler_params=pltpu.CompilerParams(vmem_limit_bytes=room),
        cost_estimate=pl.CostEstimate(flops=flops, bytes_accessed=moved, transcendentals=0),
    )(place, *args)


def whole(array):
    zeros = (0,) * array.ndim
    return pl.BlockSpec(array.shape, lambda i, place: zeros)


def shape_of(shape, dtype):
    return jax.ShapeDtypeStruct(shape, dtype)


def rms_rows(values, gain):
    return values * lax.rsqrt(jnp.mean(values * values, axis=-1, keepdims=True) + 1e-06) * gain


def split_normed(hidden, gain, out):
    count, _, depth = out.shape
    normed = rms_rows(hidden[...].astype(F32), gain[...]).astype(BF16)
    for j in range(count):
        out[j] = normed[:, j * depth : (j + 1) * depth]


def norm_kernel(place, hidden, gain, out):
    split_normed(hidden, gain, out)


def norm_split(place, hidden, gain, count):
    rows, width = hidden.shape
    step = min(rows, 64)
    out = (count, rows, width // count)
    return call(
        norm_kernel,
        place,
        (rows // step,),
        [pl.BlockSpec((step, width), lambda i, place: (i, 0)), whole(gain)],
        pl.BlockSpec((count, step, width // count), lambda i, place: (0, i, 0)),
        shape_of(out, BF16),
        (hidden, gain),
        (4 * rows * width, 4 * rows * width),
    )


def pick_kernel(place, first, key, value, half, both):
    size = half.shape[1]
    half[...] = first[...]
    both[:, :size] = key[...]
    both[:, size:] = value[...]


def pick_columns(place, weight, size):
    depth = weight.shape[0]
    block = (depth, size)
    outs = [shape_of(block, BF16), shape_of((depth, 2 * size), BF16)]
    return call(
        pick_kernel,
        place,
        (1,),
        [
            pl.BlockSpec(block, lambda i, place: (0, 2 * place[HEAD] + place[GROUP])),
            pl.BlockSpec(block, lambda i, place: (0, 2 * place[HEAD])),
            pl.BlockSpec(block, lambda i, place: (0, 2 * place[HEAD] + 1)),
        ],
        [whole(out) for out in outs],
        outs,
        (weight, weight, weight),
        (0, 12 * depth * size),
        room=ALL,
    )


def query_kernel(count, place, rows, weight, *outs):
    block = rows.shape[1]
    left = jnp.concatenate([rows[place[SP] ^ d] for d in range(count)], axis=0)
    part = jnp.dot(left, weight[...], preferred_element_type=F32)
    for d in range(count):
        outs[d][...] = part[d * block : (d + 1) * block]


def query_parts(place, rows, weight):
    count, block, depth = rows.shape
    width = weight.shape[1]
    step = min(width, 256)
    return call(
        functools.partial(query_kernel, count),
        place,
        (width // step,),
        [whole(rows), pl.BlockSpec((depth, step), lambda i, place: (0, i))],
        [pl.BlockSpec((block, step), lambda i, place: (0, i))] * count,
        [shape_of((block, width), F32)] * count,
        (rows, weight),
        (2 * count * block * depth * width, 2 * depth * width),
    )


def turn(values, cosine, sine):
    return values * cosine + pltpu.roll(values, values.shape[-1] // 2, 1) * sine


def near_kernel(place, hidden, norm_gain, cont, own, partner, prompt, out):
    split_normed(hidden, norm_gain, prompt)
    total = 0.0
    for d, weight in ((0, own), (1, partner)):
        left = jnp.concatenate([prompt[place[SP] ^ d], cont[place[SP] ^ d]], axis=0)
        total = total + jnp.dot(left, weight[...], preferred_element_type=F32)
    out[...] = total


def near_keyval(place, hidden, norm_gain, cont, own, partner):
    args = (hidden, norm_gain, cont, own, partner)
    count, cont_rows, depth = cont.shape
    prompt_rows = hidden.shape[0]
    rows = prompt_rows + cont_rows
    width = own.shape[1]
    outs = [shape_of((count, prompt_rows, depth), BF16), shape_of((rows, width), F32)]
    return call(
        near_kernel,
        place,
        (1,),
        [whole(a) for a in args],
        [whole(out) for out in outs],
        outs,
        args,
        (4 * rows * depth * width, 4 * depth * (rows * count + width)),
    )


def keyval_kernel(count, place, prompt, cont, cosine, sine, gain, near, *refs):
    weights, out = refs[:-1], refs[-1]
    size = gain.shape[1]
    total = 0.0
    for d in range(2, count):
        left = jnp.concatenate([prompt[place[SP] ^ d], cont[place[SP] ^ d]], axis=0)
        weight = jnp.concatenate([weights[2 * d - 4][...], weights[2 * d - 3][...]], axis=1)
        total = total + jnp.dot(left, weight, preferred_element_type=F32)
    swapped = place[GROUP] == 1
    first, second = total[:, :size], total[:, size:]
    key = near[:, :size] + jnp.where(swapped, second, first)
    value = near[:, size:] + jnp.where(swapped, first, second)
    out[:, :size] = turn(rms_rows(key, gain[...]), cosine[...], sine[...]).astype(BF16)
    out[:, size:] = value.astype(BF16)


def keyval_rows(place, prompt, cont, cosine, sine, gain, near, weights):
    count, prompt_rows, depth = prompt.shape
    rows = prompt_rows + cont.shape[1]
    size = gain.shape[1]
    args = (prompt, cont, cosine, sine, gain, near, *weights)
    out = shape_of((rows, 2 * size), BF16)
    return call(
        functools.partial(keyval_kernel, count),
        place,
        (1,),
        [whole(a) for a in args],
        whole(out),
        out,
        args,
        (2 * rows * count * depth * size, count * depth * (rows + 2 * size)),
    )


def attend_kernel(count, prompt_rows, place, lengths, mine, other, cosine, sine, gain, *refs):
    pairs, out = refs[:-1], refs[-1]
    rows, width = mine.shape
    size = gain.shape[1]
    heads = width // size
    queries = []
    for h in range(heads):
        part = slice(h * size, (h + 1) * size)
        value = rms_rows(mine[:, part] + other[:, part], gain[...])
        queries.append(turn(value, cosine[...], sine[...]).astype(BF16))
    queries = jnp.concatenate(queries, axis=0)
    prompt = jnp.concatenate([pair[:prompt_rows] for pair in pairs], axis=0)
    cont = jnp.concatenate([pair[prompt_rows:] for pair in pairs], axis=0)
    scale = 1.0 / math.sqrt(size)
    by_rows = (((1,), (1,)), ((), ()))
    to_prompt = (
        lax.dot_general(queries, prompt[:, :size], by_rows, preferred_element_type=F32) * scale
    )
    to_cont = (
        lax.dot_general(queries, cont[:, :size], by_rows, preferred_element_type=F32) * scale
    )
    shape = (rows, cont.shape[0])
    own = place[SP] * rows + lax.broadcasted_iota(jnp.int32, shape, 0)
    at = lax.broadcasted_iota(jnp.int32, shape, 1)
    key = jnp.zeros(shape, jnp.int32)
    for d in range(count):
        inside = (at >= d * rows) & (at < (d + 1) * rows)
        key = jnp.where(inside, (place[SP] ^ d) * rows + at - d * rows, key)
    start = jnp.zeros(shape, jnp.int32)
    total = jnp.int32(0)
    for c in range(lengths.shape[0]):
        start = jnp.where(own >= total, total, start)
        total = total + lengths[c]
    allowed = jnp.where((key >= start) & (key <= own), 0.0, -1e30)
    to_cont = to_cont + jnp.concatenate([allowed] * heads, axis=0)
    peak = jnp.maximum(
        jnp.max(to_prompt, axis=1, keepdims=True), jnp.max(to_cont, axis=1, keepdims=True)
    )
    to_prompt = jnp.exp(to_prompt - peak)
    to_cont = jnp.exp(to_cont - peak)
    divisor = jnp.sum(to_prompt, axis=1, keepdims=True) + jnp.sum(to_cont, axis=1, keepdims=True)
    result = jnp.dot(
        (to_prompt / divisor).astype(BF16), prompt[:, size:], preferred_element_type=F32
    ) + jnp.dot((to_cont / divisor).astype(BF16), cont[:, size:], preferred_element_type=F32)
    for h in range(heads):
        out[:, h * size : (h + 1) * size] = result[h * rows : (h + 1) * rows].astype(BF16)


def attend(place, lengths, mine, other, cosine, sine, gain, pairs, prompt_rows):
    rows, width = mine.shape
    args = (mine, other, cosine, sine, gain, *pairs)
    out = shape_of((rows, width), BF16)
    keys = len(pairs) * pairs[0].shape[0]
    return call(
        functools.partial(attend_kernel, len(pairs), prompt_rows),
        place,
        (1,),
        [pl.BlockSpec(memory_space=pltpu.SMEM)] + [whole(a) for a in args],
        whole(out),
        out,
        (lengths, *args),
        (4 * rows * width * keys, 10 * rows * width + 512 * keys),
    )


def out_kernel(count, place, *refs):
    heads, weights, outs, part = refs[: 2 * count], refs[-count - 3 : -count - 1], refs[-count - 1 : -1], refs[-1]
    rows = heads[0].shape[0]
    total = 0.0
    for side, weight in enumerate(weights):
        left = jnp.concatenate([h[...] for h in heads[side * count : (side + 1) * count]], axis=0)
        share = jnp.dot(left, weight[...], preferred_element_type=F32)
        total = total + share.astype(BF16).astype(F32)
    total = total.astype(BF16)
    for d in range(count):
        part[d] = total[d * rows : (d + 1) * rows]
    for e in range(count):
        outs[e][...] = part[place[TP] ^ e ^ place[SP]]


def out_parts(place, heads, weights):
    count = len(heads) // 2
    rows = heads[0].shape[0]
    depth, width = weights[0].shape
    args = (*heads, *weights)
    return call(
        functools.partial(out_kernel, count),
        place,
        (1,),
        [whole(a) for a in args],
        [pl.BlockSpec((rows, width), lambda i, place: (0, 0))] * count,
        [shape_of((rows, width), BF16)] * count,
        args,
        (4 * count * rows * depth * width, 4 * depth * width),
        [pltpu.VMEM((count, rows, width), BF16)],
    )


def final_kernel(count, place, hidden, *refs):
    parts, out = refs[:-1], refs[-1]
    width = parts[0].shape[1]
    sums = [0.0, 0.0]
    for e, part in enumerate(parts):
        sums[e % 2] = sums[e % 2] + part[...].astype(F32)
    odd = place[SP] % 2 == 1
    left = jnp.where(odd, sums[1], sums[0])
    right = jnp.where(odd, sums[0], sums[1])
    out[:, :width] = (hidden[:, :width].astype(F32) + left).astype(BF16)
    out[:, width:] = (hidden[:, width:].astype(F32) + right).astype(BF16)


def final_sum(place, parts, hidden):
    rows, width = hidden.shape
    count = len(parts)
    return call(
        functools.partial(final_kernel, count),
        place,
        (1,),
        [whole(a) for a in (hidden, *parts)],
        whole(hidden),
        shape_of((rows, width), BF16),
        (hidden, *parts),
        (count * rows * width, 12 * rows * width),
    )


def after(arrays, *others):
    return lax.optimization_barrier((arrays, others))[0]


def swap(array, axis, bits):
    return lax.ppermute(array, axis, [(i, i ^ bits) for i in range(lax.axis_size(axis))])


def swap_both(array, tp_bits, sp_bits, count):
    pairs = [
        (t * count + s, (t ^ tp_bits) * count + (s ^ sp_bits))
        for t in range(count)
        for s in range(count)
    ]
    return lax.ppermute(array, ("tp", "sp"), pairs)


def swap_bits(count):
    bits = []
    bit = 1
    while bit < count:
        bits.append(bit)
        bit *= 2
    return bits


def gather_blocks(block, axis, count):
    held = {0: block}
    bits = swap_bits(count)
    for bit in bits[1:] + bits[:1]:
        held.update({d ^ bit: swap(held[d], axis, bit) for d in sorted(held)})
    return [held[d] for d in range(count)]


def other_halves(half, axis, count):
    firsts = {0: half}
    for bit in swap_bits(count)[1:]:
        firsts.update({d ^ bit: swap(firsts[d], axis, bit) for d in sorted(firsts)})
    del firsts[0]
    return firsts


def both_cores(held, axis):
    return {**held, **{d ^ 1: swap(held[d], axis, 1) for d in sorted(held)}}


def sum_blocks(blocks, axis, count):
    held = dict(enumerate(blocks))
    bits = swap_bits(count)
    for bit in bits:
        sent = [d for d in sorted(held) if d & bit]
        got = {d ^ bit: swap(held[d], axis, bit) for d in sent}
        if bit == bits[-1]:
            return held[0], got[0]
        held = {d: held[d] + got[d] for d in got}


def tables(positions, size):
    half = size // 2
    frequency = jnp.exp(jnp.arange(half, dtype=F32) * (-2.0 * math.log(1000000.0) / size))
    angles = positions.astype(F32)[:, None] * frequency[None, :]
    cosine = jnp.cos(angles)
    sine = jnp.sin(angles)
    return (
        jnp.concatenate([cosine, cosine], axis=1),
        jnp.concatenate([-sine, sine], axis=1),
    )


def on_device(
    hidden_cont,
    hidden_prompt,
    norm_gain,
    query_weight,
    keyval_weight,
    out_weight,
    query_gain,
    key_gain,
    sample_lengths,
):
    size = query_gain.shape[0]
    heads_here = query_weight.shape[1] // size
    cont_rows = hidden_cont.shape[0]
    prompt_rows = hidden_prompt.shape[0]
    sp_index = lax.axis_index("sp")
    sp_count = lax.axis_size("sp")
    tp_index = lax.axis_index("tp")
    assert lax.axis_size("tp") == sp_count and lax.axis_size("groups") == 2
    place = jnp.stack(
        [
            sp_index,
            tp_index,
            lax.axis_index("groups"),
            tp_index * heads_here // (QH // KVH),
        ]
    ).astype(jnp.int32)
    norm_gain = norm_gain[None, :]
    query_gain = query_gain[None, :]
    key_gain = key_gain[None, :]

    cont = norm_split(place, hidden_cont, norm_gain, sp_count)
    half, both = pick_columns(place, keyval_weight, size)
    cont_all = lax.all_to_all(cont, "sp", 0, 0, tiled=True)
    halves = other_halves(half, "sp", sp_count)
    partner = swap(both, "sp", 1)
    width = out_weight.shape[1]
    side = tp_index % 2
    out_early = after(out_weight, cont)
    sent = lax.dynamic_slice_in_dim(out_early, (1 - side) * (width // 2), width // 2, 1)
    out_weights = [
        lax.dynamic_slice_in_dim(out_early, side * (width // 2), width // 2, 1),
        swap(sent, "tp", 1),
    ]
    others = {d: swap(half, "groups", 1) for d, half in halves.items()}
    halves = both_cores(halves, "sp")
    prompt, near_pair = near_keyval(
        place,
        hidden_prompt,
        norm_gain,
        cont,
        both,
        after(partner, halves, sent, out_weights[0]),
    )
    cont_all = after(cont_all, near_pair, others)
    others = both_cores(others, "sp")

    index = sp_index * cont_rows + jnp.arange(cont_rows, dtype=jnp.int32)
    starts = jnp.cumsum(sample_lengths, dtype=jnp.int32) - sample_lengths
    start = jnp.max(jnp.where(index[:, None] >= starts[None, :], starts[None, :], 0), axis=1)
    prompt_pos = sp_index * prompt_rows + jnp.arange(prompt_rows, dtype=jnp.int32)
    positions = jnp.concatenate([prompt_pos, prompt_rows * sp_count + index - start])
    cosine, sine = tables(positions, size)

    parts = query_parts(place, cont_all, query_weight)
    mine, other = sum_blocks(parts, "sp", sp_count)
    weights = [held[d] for d in range(2, sp_count) for held in (halves, others)]
    pair = keyval_rows(place, prompt, cont, cosine, sine, key_gain, near_pair, weights)
    pairs = gather_blocks(pair, "sp", sp_count)
    heads = attend(
        place,
        sample_lengths,
        mine,
        other,
        cosine[prompt_rows:],
        sine[prompt_rows:],
        query_gain,
        pairs,
        prompt_rows,
    )
    chips = range(0, sp_count, 2)
    near_heads = {d: swap(heads, "sp", d) if d else heads for d in chips}
    far_heads = {d: swap_both(heads, 1, d, sp_count) for d in chips}
    near_heads = both_cores(near_heads, "sp")
    far_heads = both_cores(far_heads, "sp")
    all_heads = [held[d] for held in (near_heads, far_heads) for d in range(sp_count)]
    parts = out_parts(place, all_heads, out_weights)
    parts = [
        lax.ppermute(
            part,
            ("tp", "sp"),
            [
                (t * sp_count + s, s * sp_count + (t ^ e))
                for t in range(sp_count)
                for s in range(sp_count)
            ],
        )
        for e, part in enumerate(parts)
    ]
    hidden = lax.dynamic_slice_in_dim(hidden_cont, tp_index * width, width, 1)
    return final_sum(place, parts, hidden)


def solution(mesh):
    placed = (
        P(("groups", "sp"), None),
        P(("groups", "sp"), None),
        P(),
        P("sp", "tp"),
        P("sp", None),
        P("tp", "sp"),
        P(),
        P(),
        P("groups"),
    )
    return jax.shard_map(
        on_device, mesh=mesh, in_specs=placed, out_specs=P(("groups", "sp"), "tp"), check_vma=False
    )
```

```python
import functools
import math

import jax
import jax.numpy as jnp
from jax import lax
from jax.experimental import pallas as pl
from jax.experimental.pallas import tpu as pltpu
from jax.sharding import PartitionSpec as P

QH = 32
KVH = 4
SP, TP, GROUP, HEAD = range(4)
BF16 = jnp.bfloat16
F32 = jnp.float32
ROOM = 14 * 1024 * 1024


def call(kernel, place, grid, in_specs, out_specs, out_shape, args, cost, scratch=(), room=ROOM):
    flops, moved = cost
    return pl.pallas_call(
        kernel,
        out_shape=out_shape,
        grid_spec=pltpu.PrefetchScalarGridSpec(
            num_scalar_prefetch=1,
            grid=grid,
            in_specs=in_specs,
            out_specs=out_specs,
            scratch_shapes=scratch,
        ),
        compiler_params=pltpu.CompilerParams(vmem_limit_bytes=room),
        cost_estimate=pl.CostEstimate(flops=flops, bytes_accessed=moved, transcendentals=0),
    )(place, *args)


def whole(array):
    zeros = (0,) * array.ndim
    return pl.BlockSpec(array.shape, lambda i, place: zeros)


def shape_of(shape, dtype):
    return jax.ShapeDtypeStruct(shape, dtype)


def rms_rows(values, gain):
    return values * lax.rsqrt(jnp.mean(values * values, axis=-1, keepdims=True) + 1e-06) * gain


def split_normed(hidden, gain, out):
    count, _, depth = out.shape
    normed = rms_rows(hidden[...].astype(F32), gain[...]).astype(BF16)
    for j in range(count):
        out[j] = normed[:, j * depth : (j + 1) * depth]


def norm_kernel(place, hidden, gain, out):
    split_normed(hidden, gain, out)


def norm_split(place, hidden, gain, count):
    rows, width = hidden.shape
    step = min(rows, 64)
    out = (count, rows, width // count)
    return call(
        norm_kernel,
        place,
        (rows // step,),
        [pl.BlockSpec((step, width), lambda i, place: (i, 0)), whole(gain)],
        pl.BlockSpec((count, step, width // count), lambda i, place: (0, i, 0)),
        shape_of(out, BF16),
        (hidden, gain),
        (4 * rows * width, 4 * rows * width),
    )


def pick_kernel(place, first, key, value, half, both):
    size = half.shape[1]
    half[...] = first[...]
    both[:, :size] = key[...]
    both[:, size:] = value[...]


def pick_columns(place, weight, size):
    depth = weight.shape[0]
    block = (depth, size)
    outs = [shape_of(block, BF16), shape_of((depth, 2 * size), BF16)]
    return call(
        pick_kernel,
        place,
        (1,),
        [
            pl.BlockSpec(block, lambda i, place: (0, 2 * place[HEAD] + place[GROUP])),
            pl.BlockSpec(block, lambda i, place: (0, 2 * place[HEAD])),
            pl.BlockSpec(block, lambda i, place: (0, 2 * place[HEAD] + 1)),
        ],
        [whole(out) for out in outs],
        outs,
        (weight, weight, weight),
        (0, 12 * depth * size),
    )


def query_kernel(count, place, rows, weight, *outs):
    block = rows.shape[1]
    left = jnp.concatenate([rows[place[SP] ^ d] for d in range(count)], axis=0)
    part = jnp.dot(left, weight[...], preferred_element_type=F32)
    for d in range(count):
        outs[d][...] = part[d * block : (d + 1) * block]


def query_parts(place, rows, weight):
    count, block, depth = rows.shape
    width = weight.shape[1]
    step = min(width, 256)
    return call(
        functools.partial(query_kernel, count),
        place,
        (width // step,),
        [whole(rows), pl.BlockSpec((depth, step), lambda i, place: (0, i))],
        [pl.BlockSpec((block, step), lambda i, place: (0, i))] * count,
        [shape_of((block, width), F32)] * count,
        (rows, weight),
        (2 * count * block * depth * width, 2 * depth * width),
    )


def turn(values, cosine, sine):
    return values * cosine + pltpu.roll(values, values.shape[-1] // 2, 1) * sine


def near_kernel(place, hidden, norm_gain, cont, own, partner, prompt, out):
    split_normed(hidden, norm_gain, prompt)
    total = 0.0
    for d, weight in ((0, own), (1, partner)):
        left = jnp.concatenate([prompt[place[SP] ^ d], cont[place[SP] ^ d]], axis=0)
        total = total + jnp.dot(left, weight[...], preferred_element_type=F32)
    out[...] = total


def near_keyval(place, hidden, norm_gain, cont, own, partner):
    args = (hidden, norm_gain, cont, own, partner)
    count, cont_rows, depth = cont.shape
    prompt_rows = hidden.shape[0]
    rows = prompt_rows + cont_rows
    width = own.shape[1]
    outs = [shape_of((count, prompt_rows, depth), BF16), shape_of((rows, width), F32)]
    return call(
        near_kernel,
        place,
        (1,),
        [whole(a) for a in args],
        [whole(out) for out in outs],
        outs,
        args,
        (4 * rows * depth * width, 4 * depth * (rows * count + width)),
    )


def keyval_kernel(count, place, prompt, cont, cosine, sine, gain, near, *refs):
    weights, out = refs[:-1], refs[-1]
    size = gain.shape[1]
    total = 0.0
    for d in range(2, count):
        left = jnp.concatenate([prompt[place[SP] ^ d], cont[place[SP] ^ d]], axis=0)
        weight = jnp.concatenate([weights[2 * d - 4][...], weights[2 * d - 3][...]], axis=1)
        total = total + jnp.dot(left, weight, preferred_element_type=F32)
    swapped = place[GROUP] == 1
    first, second = total[:, :size], total[:, size:]
    key = near[:, :size] + jnp.where(swapped, second, first)
    value = near[:, size:] + jnp.where(swapped, first, second)
    out[:, :size] = turn(rms_rows(key, gain[...]), cosine[...], sine[...]).astype(BF16)
    out[:, size:] = value.astype(BF16)


def keyval_rows(place, prompt, cont, cosine, sine, gain, near, weights):
    count, prompt_rows, depth = prompt.shape
    rows = prompt_rows + cont.shape[1]
    size = gain.shape[1]
    args = (prompt, cont, cosine, sine, gain, near, *weights)
    out = shape_of((rows, 2 * size), BF16)
    return call(
        functools.partial(keyval_kernel, count),
        place,
        (1,),
        [whole(a) for a in args],
        whole(out),
        out,
        args,
        (2 * rows * count * depth * size, count * depth * (rows + 2 * size)),
    )


def attend_kernel(count, prompt_rows, place, lengths, mine, other, cosine, sine, gain, *refs):
    pairs, out = refs[:-1], refs[-1]
    rows, width = mine.shape
    size = gain.shape[1]
    heads = width // size
    queries = []
    for h in range(heads):
        part = slice(h * size, (h + 1) * size)
        value = rms_rows(mine[:, part] + other[:, part], gain[...])
        queries.append(turn(value, cosine[...], sine[...]).astype(BF16))
    queries = jnp.concatenate(queries, axis=0)
    prompt = jnp.concatenate([pair[:prompt_rows] for pair in pairs], axis=0)
    cont = jnp.concatenate([pair[prompt_rows:] for pair in pairs], axis=0)
    scale = 1.0 / math.sqrt(size)
    by_rows = (((1,), (1,)), ((), ()))
    to_prompt = (
        lax.dot_general(queries, prompt[:, :size], by_rows, preferred_element_type=F32) * scale
    )
    to_cont = (
        lax.dot_general(queries, cont[:, :size], by_rows, preferred_element_type=F32) * scale
    )
    shape = (rows, cont.shape[0])
    own = place[SP] * rows + lax.broadcasted_iota(jnp.int32, shape, 0)
    at = lax.broadcasted_iota(jnp.int32, shape, 1)
    key = jnp.zeros(shape, jnp.int32)
    for d in range(count):
        inside = (at >= d * rows) & (at < (d + 1) * rows)
        key = jnp.where(inside, (place[SP] ^ d) * rows + at - d * rows, key)
    start = jnp.zeros(shape, jnp.int32)
    total = jnp.int32(0)
    for c in range(lengths.shape[0]):
        start = jnp.where(own >= total, total, start)
        total = total + lengths[c]
    allowed = jnp.where((key >= start) & (key <= own), 0.0, -1e30)
    to_cont = to_cont + jnp.concatenate([allowed] * heads, axis=0)
    peak = jnp.maximum(
        jnp.max(to_prompt, axis=1, keepdims=True), jnp.max(to_cont, axis=1, keepdims=True)
    )
    to_prompt = jnp.exp(to_prompt - peak)
    to_cont = jnp.exp(to_cont - peak)
    divisor = jnp.sum(to_prompt, axis=1, keepdims=True) + jnp.sum(to_cont, axis=1, keepdims=True)
    result = jnp.dot(
        (to_prompt / divisor).astype(BF16), prompt[:, size:], preferred_element_type=F32
    ) + jnp.dot((to_cont / divisor).astype(BF16), cont[:, size:], preferred_element_type=F32)
    for h in range(heads):
        out[:, h * size : (h + 1) * size] = result[h * rows : (h + 1) * rows].astype(BF16)


def attend(place, lengths, mine, other, cosine, sine, gain, pairs, prompt_rows):
    rows, width = mine.shape
    args = (mine, other, cosine, sine, gain, *pairs)
    out = shape_of((rows, width), BF16)
    keys = len(pairs) * pairs[0].shape[0]
    return call(
        functools.partial(attend_kernel, len(pairs), prompt_rows),
        place,
        (1,),
        [pl.BlockSpec(memory_space=pltpu.SMEM)] + [whole(a) for a in args],
        whole(out),
        out,
        (lengths, *args),
        (4 * rows * width * keys, 10 * rows * width + 512 * keys),
    )


def out_kernel(count, place, *refs):
    heads, weights, outs, part = refs[: 2 * count], refs[-count - 3 : -count - 1], refs[-count - 1 : -1], refs[-1]
    rows = heads[0].shape[0]
    total = 0.0
    for side, weight in enumerate(weights):
        left = jnp.concatenate([h[...] for h in heads[side * count : (side + 1) * count]], axis=0)
        share = jnp.dot(left, weight[...], preferred_element_type=F32)
        total = total + share.astype(BF16).astype(F32)
    total = total.astype(BF16)
    for d in range(count):
        part[d] = total[d * rows : (d + 1) * rows]
    for e in range(count):
        outs[e][...] = part[place[TP] ^ e ^ place[SP]]


def out_parts(place, heads, own, partner):
    count = len(heads) // 2
    rows = heads[0].shape[0]
    depth, width = partner.shape
    if width % 128:
        own = lax.dynamic_slice_in_dim(own, place[TP] % 2 * width, width, 1)
        half = whole(own)
    else:
        half = pl.BlockSpec((depth, width), lambda i, place: (0, place[TP] % 2))
    args = (*heads, own, partner)
    return call(
        functools.partial(out_kernel, count),
        place,
        (1,),
        [whole(h) for h in heads] + [half, whole(partner)],
        [pl.BlockSpec((rows, width), lambda i, place: (0, 0))] * count,
        [shape_of((rows, width), BF16)] * count,
        args,
        (4 * count * rows * depth * width, 4 * depth * width),
        [pltpu.VMEM((count, rows, width), BF16)],
    )


def final_kernel(count, place, hidden, *refs):
    parts, out = refs[:-1], refs[-1]
    width = parts[0].shape[1]
    sums = [0.0, 0.0]
    for e, part in enumerate(parts):
        sums[e % 2] = sums[e % 2] + part[...].astype(F32)
    odd = place[SP] % 2 == 1
    left = jnp.where(odd, sums[1], sums[0])
    right = jnp.where(odd, sums[0], sums[1])
    out[:, :width] = (hidden[:, :width].astype(F32) + left).astype(BF16)
    out[:, width:] = (hidden[:, width:].astype(F32) + right).astype(BF16)


def final_sum(place, parts, hidden):
    rows, width = hidden.shape
    count = len(parts)
    return call(
        functools.partial(final_kernel, count),
        place,
        (1,),
        [whole(a) for a in (hidden, *parts)],
        whole(hidden),
        shape_of((rows, width), BF16),
        (hidden, *parts),
        (count * rows * width, 12 * rows * width),
    )


def after(arrays, *others):
    return lax.optimization_barrier((arrays, others))[0]


def swap(array, axis, bits):
    return lax.ppermute(array, axis, [(i, i ^ bits) for i in range(lax.axis_size(axis))])


def swap_both(array, tp_bits, sp_bits, count):
    pairs = [
        (t * count + s, (t ^ tp_bits) * count + (s ^ sp_bits))
        for t in range(count)
        for s in range(count)
    ]
    return lax.ppermute(array, ("tp", "sp"), pairs)


def swap_bits(count):
    bits = []
    bit = 1
    while bit < count:
        bits.append(bit)
        bit *= 2
    return bits


def gather_blocks(block, axis, count):
    held = {0: block}
    bits = swap_bits(count)
    for bit in bits[1:] + bits[:1]:
        held.update({d ^ bit: swap(held[d], axis, bit) for d in sorted(held)})
    return [held[d] for d in range(count)]


def other_halves(half, axis, count):
    firsts = {0: half}
    for bit in swap_bits(count)[1:]:
        firsts.update({d ^ bit: swap(firsts[d], axis, bit) for d in sorted(firsts)})
    del firsts[0]
    return firsts


def both_cores(held, axis):
    return {**held, **{d ^ 1: swap(held[d], axis, 1) for d in sorted(held)}}


def sum_blocks(blocks, axis, count):
    held = dict(enumerate(blocks))
    bits = swap_bits(count)
    for bit in bits:
        sent = [d for d in sorted(held) if d & bit]
        got = {d ^ bit: swap(held[d], axis, bit) for d in sent}
        if bit == bits[-1]:
            return held[0], got[0]
        held = {d: held[d] + got[d] for d in got}


def tables(positions, size):
    half = size // 2
    frequency = jnp.exp(jnp.arange(half, dtype=F32) * (-2.0 * math.log(1000000.0) / size))
    angles = positions.astype(F32)[:, None] * frequency[None, :]
    cosine = jnp.cos(angles)
    sine = jnp.sin(angles)
    return (
        jnp.concatenate([cosine, cosine], axis=1),
        jnp.concatenate([-sine, sine], axis=1),
    )


def on_device(
    hidden_cont,
    hidden_prompt,
    norm_gain,
    query_weight,
    keyval_weight,
    out_weight,
    query_gain,
    key_gain,
    sample_lengths,
):
    size = query_gain.shape[0]
    heads_here = query_weight.shape[1] // size
    cont_rows = hidden_cont.shape[0]
    prompt_rows = hidden_prompt.shape[0]
    sp_index = lax.axis_index("sp")
    sp_count = lax.axis_size("sp")
    tp_index = lax.axis_index("tp")
    assert lax.axis_size("tp") == sp_count and lax.axis_size("groups") == 2
    place = jnp.stack(
        [
            sp_index,
            tp_index,
            lax.axis_index("groups"),
            tp_index * heads_here // (QH // KVH),
        ]
    ).astype(jnp.int32)
    norm_gain = norm_gain[None, :]
    query_gain = query_gain[None, :]
    key_gain = key_gain[None, :]

    cont = norm_split(place, hidden_cont, norm_gain, sp_count)
    half, both = pick_columns(place, keyval_weight, size)
    cont_all = lax.all_to_all(cont, "sp", 0, 0, tiled=True)
    halves = other_halves(half, "sp", sp_count)
    partner = swap(both, "sp", 1)
    width = out_weight.shape[1]
    side = tp_index % 2
    out_early = after(out_weight, cont)
    sent = lax.dynamic_slice_in_dim(out_early, (1 - side) * (width // 2), width // 2, 1)
    out_partner = swap(sent, "tp", 1)
    others = {d: swap(half, "groups", 1) for d, half in halves.items()}
    halves = both_cores(halves, "sp")
    prompt, near_pair = near_keyval(
        place,
        hidden_prompt,
        norm_gain,
        cont,
        both,
        after(partner, halves, sent),
    )
    cont_all = after(cont_all, near_pair, others)
    others = both_cores(others, "sp")

    index = sp_index * cont_rows + jnp.arange(cont_rows, dtype=jnp.int32)
    starts = jnp.cumsum(sample_lengths, dtype=jnp.int32) - sample_lengths
    start = jnp.max(jnp.where(index[:, None] >= starts[None, :], starts[None, :], 0), axis=1)
    prompt_pos = sp_index * prompt_rows + jnp.arange(prompt_rows, dtype=jnp.int32)
    positions = jnp.concatenate([prompt_pos, prompt_rows * sp_count + index - start])
    cosine, sine = tables(positions, size)

    parts = query_parts(place, cont_all, query_weight)
    mine, other = sum_blocks(parts, "sp", sp_count)
    weights = [held[d] for d in range(2, sp_count) for held in (halves, others)]
    pair = keyval_rows(place, prompt, cont, cosine, sine, key_gain, near_pair, weights)
    pairs = gather_blocks(pair, "sp", sp_count)
    heads = attend(
        place,
        sample_lengths,
        mine,
        other,
        cosine[prompt_rows:],
        sine[prompt_rows:],
        query_gain,
        pairs,
        prompt_rows,
    )
    chips = range(0, sp_count, 2)
    near_heads = {d: swap(heads, "sp", d) if d else heads for d in chips}
    far_heads = {d: swap_both(heads, 1, d, sp_count) for d in chips}
    near_heads = both_cores(near_heads, "sp")
    far_heads = both_cores(far_heads, "sp")
    all_heads = [held[d] for held in (near_heads, far_heads) for d in range(sp_count)]
    parts = out_parts(place, all_heads, out_weight, out_partner)
    parts = [
        lax.ppermute(
            part,
            ("tp", "sp"),
            [
                (t * sp_count + s, s * sp_count + (t ^ e))
                for t in range(sp_count)
                for s in range(sp_count)
            ],
        )
        for e, part in enumerate(parts)
    ]
    hidden = lax.dynamic_slice_in_dim(hidden_cont, tp_index * width, width, 1)
    return final_sum(place, parts, hidden)


def solution(mesh):
    placed = (
        P(("groups", "sp"), None),
        P(("groups", "sp"), None),
        P(),
        P("sp", "tp"),
        P("sp", None),
        P("tp", "sp"),
        P(),
        P(),
        P("groups"),
    )
    return jax.shard_map(
        on_device, mesh=mesh, in_specs=placed, out_specs=P(("groups", "sp"), "tp"), check_vma=False
    )
```

```python
import functools
import math

import jax
import jax.numpy as jnp
from jax import lax
from jax.experimental import pallas as pl
from jax.experimental.pallas import tpu as pltpu
from jax.sharding import PartitionSpec as P

QH = 32
KVH = 4
SP, TP, HEAD = range(3)
BF16 = jnp.bfloat16
F32 = jnp.float32
ROOM = 14 * 1024 * 1024


def call(kernel, place, grid, in_specs, out_specs, out_shape, args, cost, scratch=(), room=ROOM):
    flops, moved = cost
    return pl.pallas_call(
        kernel,
        out_shape=out_shape,
        grid_spec=pltpu.PrefetchScalarGridSpec(
            num_scalar_prefetch=1,
            grid=grid,
            in_specs=in_specs,
            out_specs=out_specs,
            scratch_shapes=scratch,
        ),
        compiler_params=pltpu.CompilerParams(vmem_limit_bytes=room),
        cost_estimate=pl.CostEstimate(flops=flops, bytes_accessed=moved, transcendentals=0),
    )(place, *args)


def whole(array):
    zeros = (0,) * array.ndim
    return pl.BlockSpec(array.shape, lambda i, place: zeros)


def shape_of(shape, dtype):
    return jax.ShapeDtypeStruct(shape, dtype)


def rms_rows(values, gain):
    return values * lax.rsqrt(jnp.mean(values * values, axis=-1, keepdims=True) + 1e-06) * gain


def split_normed(hidden, gain, out):
    count, _, depth = out.shape
    normed = rms_rows(hidden[...].astype(F32), gain[...]).astype(BF16)
    for j in range(count):
        out[j] = normed[:, j * depth : (j + 1) * depth]


def norm_kernel(place, hidden, gain, out):
    split_normed(hidden, gain, out)


def norm_split(place, hidden, gain, count):
    rows, width = hidden.shape
    step = min(rows, 64)
    out = (count, rows, width // count)
    return call(
        norm_kernel,
        place,
        (rows // step,),
        [pl.BlockSpec((step, width), lambda i, place: (i, 0)), whole(gain)],
        pl.BlockSpec((count, step, width // count), lambda i, place: (0, i, 0)),
        shape_of(out, BF16),
        (hidden, gain),
        (4 * rows * width, 4 * rows * width),
    )


def pick_kernel(place, columns, out):
    out[...] = columns[...]


def pick_columns(place, weight, size):
    block = (weight.shape[0], 2 * size)
    return call(
        pick_kernel,
        place,
        (1,),
        [pl.BlockSpec(block, lambda i, place: (0, place[HEAD]))],
        pl.BlockSpec(block, lambda i, place: (0, 0)),
        shape_of(block, BF16),
        (weight,),
        (0, 8 * block[0] * size),
    )


def query_kernel(count, place, rows, weight, *outs):
    block = rows.shape[1]
    left = jnp.concatenate([rows[place[SP] ^ d] for d in range(count)], axis=0)
    part = jnp.dot(left, weight[...], preferred_element_type=F32)
    for d in range(count):
        outs[d][...] = part[d * block : (d + 1) * block]


def query_parts(place, rows, weight):
    count, block, depth = rows.shape
    width = weight.shape[1]
    step = min(width, 256)
    return call(
        functools.partial(query_kernel, count),
        place,
        (width // step,),
        [whole(rows), pl.BlockSpec((depth, step), lambda i, place: (0, i))],
        [pl.BlockSpec((block, step), lambda i, place: (0, i))] * count,
        [shape_of((block, width), F32)] * count,
        (rows, weight),
        (2 * count * block * depth * width, 2 * depth * width),
    )


def turn(values, cosine, sine):
    return values * cosine + pltpu.roll(values, values.shape[-1] // 2, 1) * sine


def near_kernel(place, hidden, norm_gain, cont, own, partner, prompt, out):
    split_normed(hidden, norm_gain, prompt)
    total = 0.0
    for d, weight in ((0, own), (1, partner)):
        left = jnp.concatenate([prompt[place[SP] ^ d], cont[place[SP] ^ d]], axis=0)
        total = total + jnp.dot(left, weight[...], preferred_element_type=F32)
    out[...] = total


def near_keyval(place, hidden, norm_gain, cont, own, partner):
    args = (hidden, norm_gain, cont, own, partner)
    count, cont_rows, depth = cont.shape
    prompt_rows = hidden.shape[0]
    rows = prompt_rows + cont_rows
    width = own.shape[1]
    outs = [shape_of((count, prompt_rows, depth), BF16), shape_of((rows, width), F32)]
    return call(
        near_kernel,
        place,
        (1,),
        [whole(a) for a in args],
        [whole(out) for out in outs],
        outs,
        args,
        (4 * rows * depth * width, 4 * depth * (rows * count + width)),
    )


def keyval_kernel(count, place, prompt, cont, cosine, sine, gain, near, *refs):
    weights, out = refs[:-1], refs[-1]
    size = gain.shape[1]
    total = near[...]
    for d in range(2, count):
        left = jnp.concatenate([prompt[place[SP] ^ d], cont[place[SP] ^ d]], axis=0)
        total = total + jnp.dot(left, weights[d - 2][...], preferred_element_type=F32)
    key = rms_rows(total[:, :size], gain[...])
    out[:, :size] = turn(key, cosine[...], sine[...]).astype(BF16)
    out[:, size:] = total[:, size:].astype(BF16)


def keyval_rows(place, prompt, cont, cosine, sine, gain, near, weights):
    count, prompt_rows, depth = prompt.shape
    rows = prompt_rows + cont.shape[1]
    size = gain.shape[1]
    args = (prompt, cont, cosine, sine, gain, near, *weights)
    out = shape_of((rows, 2 * size), BF16)
    return call(
        functools.partial(keyval_kernel, count),
        place,
        (1,),
        [whole(a) for a in args],
        whole(out),
        out,
        args,
        (2 * rows * count * depth * size, count * depth * (rows + 2 * size)),
    )


def attend_kernel(count, prompt_rows, place, lengths, mine, other, cosine, sine, gain, *refs):
    pairs, out = refs[:-1], refs[-1]
    rows, width = mine.shape
    size = gain.shape[1]
    heads = width // size
    queries = []
    for h in range(heads):
        part = slice(h * size, (h + 1) * size)
        value = rms_rows(mine[:, part] + other[:, part], gain[...])
        queries.append(turn(value, cosine[...], sine[...]).astype(BF16))
    queries = jnp.concatenate(queries, axis=0)
    prompt = jnp.concatenate([pair[:prompt_rows] for pair in pairs], axis=0)
    cont = jnp.concatenate([pair[prompt_rows:] for pair in pairs], axis=0)
    scale = 1.0 / math.sqrt(size)
    by_rows = (((1,), (1,)), ((), ()))
    to_prompt = (
        lax.dot_general(queries, prompt[:, :size], by_rows, preferred_element_type=F32) * scale
    )
    to_cont = (
        lax.dot_general(queries, cont[:, :size], by_rows, preferred_element_type=F32) * scale
    )
    shape = (rows, cont.shape[0])
    own = place[SP] * rows + lax.broadcasted_iota(jnp.int32, shape, 0)
    at = lax.broadcasted_iota(jnp.int32, shape, 1)
    key = jnp.zeros(shape, jnp.int32)
    for d in range(count):
        inside = (at >= d * rows) & (at < (d + 1) * rows)
        key = jnp.where(inside, (place[SP] ^ d) * rows + at - d * rows, key)
    start = jnp.zeros(shape, jnp.int32)
    total = jnp.int32(0)
    for c in range(lengths.shape[0]):
        start = jnp.where(own >= total, total, start)
        total = total + lengths[c]
    allowed = jnp.where((key >= start) & (key <= own), 0.0, -1e30)
    to_cont = to_cont + jnp.concatenate([allowed] * heads, axis=0)
    peak = jnp.maximum(
        jnp.max(to_prompt, axis=1, keepdims=True), jnp.max(to_cont, axis=1, keepdims=True)
    )
    to_prompt = jnp.exp(to_prompt - peak)
    to_cont = jnp.exp(to_cont - peak)
    divisor = jnp.sum(to_prompt, axis=1, keepdims=True) + jnp.sum(to_cont, axis=1, keepdims=True)
    result = jnp.dot(
        (to_prompt / divisor).astype(BF16), prompt[:, size:], preferred_element_type=F32
    ) + jnp.dot((to_cont / divisor).astype(BF16), cont[:, size:], preferred_element_type=F32)
    for h in range(heads):
        out[:, h * size : (h + 1) * size] = result[h * rows : (h + 1) * rows].astype(BF16)


def attend(place, lengths, mine, other, cosine, sine, gain, pairs, prompt_rows):
    rows, width = mine.shape
    args = (mine, other, cosine, sine, gain, *pairs)
    out = shape_of((rows, width), BF16)
    keys = len(pairs) * pairs[0].shape[0]
    return call(
        functools.partial(attend_kernel, len(pairs), prompt_rows),
        place,
        (1,),
        [pl.BlockSpec(memory_space=pltpu.SMEM)] + [whole(a) for a in args],
        whole(out),
        out,
        (lengths, *args),
        (4 * rows * width * keys, 10 * rows * width + 512 * keys),
    )


def out_kernel(count, place, *refs):
    heads, weights, outs, part = refs[: 2 * count], refs[-count - 3 : -count - 1], refs[-count - 1 : -1], refs[-1]
    rows = heads[0].shape[0]
    total = 0.0
    for side, weight in enumerate(weights):
        left = jnp.concatenate([h[...] for h in heads[side * count : (side + 1) * count]], axis=0)
        share = jnp.dot(left, weight[...], preferred_element_type=F32)
        total = total + share.astype(BF16).astype(F32)
    total = total.astype(BF16)
    for d in range(count):
        part[d] = total[d * rows : (d + 1) * rows]
    for e in range(count):
        outs[e][...] = part[place[TP] ^ e ^ place[SP]]


def out_parts(place, heads, own, partner):
    count = len(heads) // 2
    rows = heads[0].shape[0]
    depth, width = partner.shape
    if width % 128:
        own = lax.dynamic_slice_in_dim(own, place[TP] % 2 * width, width, 1)
        half = whole(own)
    else:
        half = pl.BlockSpec((depth, width), lambda i, place: (0, place[TP] % 2))
    args = (*heads, own, partner)
    return call(
        functools.partial(out_kernel, count),
        place,
        (1,),
        [whole(h) for h in heads] + [half, whole(partner)],
        [pl.BlockSpec((rows, width), lambda i, place: (0, 0))] * count,
        [shape_of((rows, width), BF16)] * count,
        args,
        (4 * count * rows * depth * width, 4 * depth * width),
        [pltpu.VMEM((count, rows, width), BF16)],
    )


def final_kernel(count, place, hidden, *refs):
    parts, out = refs[:-1], refs[-1]
    width = parts[0].shape[1]
    sums = [0.0, 0.0]
    for e, part in enumerate(parts):
        sums[e % 2] = sums[e % 2] + part[...].astype(F32)
    odd = place[SP] % 2 == 1
    left = jnp.where(odd, sums[1], sums[0])
    right = jnp.where(odd, sums[0], sums[1])
    out[:, :width] = (hidden[:, :width].astype(F32) + left).astype(BF16)
    out[:, width:] = (hidden[:, width:].astype(F32) + right).astype(BF16)


def final_sum(place, parts, hidden):
    rows, width = hidden.shape
    count = len(parts)
    return call(
        functools.partial(final_kernel, count),
        place,
        (1,),
        [whole(a) for a in (hidden, *parts)],
        whole(hidden),
        shape_of((rows, width), BF16),
        (hidden, *parts),
        (count * rows * width, 12 * rows * width),
    )


def after(arrays, *others):
    return lax.optimization_barrier((arrays, others))[0]


def swap(array, axis, bits):
    return lax.ppermute(array, axis, [(i, i ^ bits) for i in range(lax.axis_size(axis))])


def swap_both(array, tp_bits, sp_bits, count):
    pairs = [
        (t * count + s, (t ^ tp_bits) * count + (s ^ sp_bits))
        for t in range(count)
        for s in range(count)
    ]
    return lax.ppermute(array, ("tp", "sp"), pairs)


def swap_bits(count):
    bits = []
    bit = 1
    while bit < count:
        bits.append(bit)
        bit *= 2
    return bits


def gather_blocks(block, axis, count):
    held = {0: block}
    bits = swap_bits(count)
    for bit in bits[1:] + bits[:1]:
        held.update({d ^ bit: swap(held[d], axis, bit) for d in sorted(held)})
    return [held[d] for d in range(count)]


def from_chips(block, axis, count):
    held = {0: block}
    for bit in swap_bits(count)[1:]:
        held.update({d ^ bit: swap(held[d], axis, bit) for d in sorted(held)})
    del held[0]
    return held


def both_cores(held, axis):
    return {**held, **{d ^ 1: swap(held[d], axis, 1) for d in sorted(held)}}


def sum_blocks(blocks, axis, count):
    held = dict(enumerate(blocks))
    bits = swap_bits(count)
    for bit in bits:
        sent = [d for d in sorted(held) if d & bit]
        got = {d ^ bit: swap(held[d], axis, bit) for d in sent}
        if bit == bits[-1]:
            return held[0], got[0]
        held = {d: held[d] + got[d] for d in got}


def tables(positions, size):
    half = size // 2
    frequency = jnp.exp(jnp.arange(half, dtype=F32) * (-2.0 * math.log(1000000.0) / size))
    angles = positions.astype(F32)[:, None] * frequency[None, :]
    cosine = jnp.cos(angles)
    sine = jnp.sin(angles)
    return (
        jnp.concatenate([cosine, cosine], axis=1),
        jnp.concatenate([-sine, sine], axis=1),
    )


def on_device(
    hidden_cont,
    hidden_prompt,
    norm_gain,
    query_weight,
    keyval_weight,
    out_weight,
    query_gain,
    key_gain,
    sample_lengths,
):
    size = query_gain.shape[0]
    heads_here = query_weight.shape[1] // size
    cont_rows = hidden_cont.shape[0]
    prompt_rows = hidden_prompt.shape[0]
    sp_index = lax.axis_index("sp")
    sp_count = lax.axis_size("sp")
    tp_index = lax.axis_index("tp")
    assert lax.axis_size("tp") == sp_count
    place = jnp.stack(
        [
            sp_index,
            tp_index,
            tp_index * heads_here // (QH // KVH),
        ]
    ).astype(jnp.int32)
    norm_gain = norm_gain[None, :]
    query_gain = query_gain[None, :]
    key_gain = key_gain[None, :]

    own = pick_columns(place, keyval_weight, size)
    weights = from_chips(own, "sp", sp_count)
    cont = norm_split(place, hidden_cont, norm_gain, sp_count)
    cont_all = lax.all_to_all(cont, "sp", 0, 0, tiled=True)
    partner = swap(own, "sp", 1)
    width = out_weight.shape[1]
    side = tp_index % 2
    out_early = after(out_weight, cont)
    sent = lax.dynamic_slice_in_dim(out_early, (1 - side) * (width // 2), width // 2, 1)
    out_partner = swap(sent, "tp", 1)
    prompt, near_pair = near_keyval(
        place, hidden_prompt, norm_gain, cont, own, after(partner, sent)
    )
    cont_all = after(cont_all, near_pair)

    index = sp_index * cont_rows + jnp.arange(cont_rows, dtype=jnp.int32)
    starts = jnp.cumsum(sample_lengths, dtype=jnp.int32) - sample_lengths
    start = jnp.max(jnp.where(index[:, None] >= starts[None, :], starts[None, :], 0), axis=1)
    prompt_pos = sp_index * prompt_rows + jnp.arange(prompt_rows, dtype=jnp.int32)
    positions = jnp.concatenate([prompt_pos, prompt_rows * sp_count + index - start])
    cosine, sine = tables(positions, size)

    parts = query_parts(place, cont_all, query_weight)
    mine, other = sum_blocks(parts, "sp", sp_count)
    weights = both_cores(after(weights, parts), "sp")
    weights = [weights[d] for d in range(2, sp_count)]
    pair = keyval_rows(place, prompt, cont, cosine, sine, key_gain, near_pair, weights)
    pairs = gather_blocks(pair, "sp", sp_count)
    heads = attend(
        place,
        sample_lengths,
        mine,
        other,
        cosine[prompt_rows:],
        sine[prompt_rows:],
        query_gain,
        pairs,
        prompt_rows,
    )
    chips = range(0, sp_count, 2)
    near_heads = {d: swap(heads, "sp", d) if d else heads for d in chips}
    far_heads = {d: swap_both(heads, 1, d, sp_count) for d in chips}
    near_heads = both_cores(near_heads, "sp")
    far_heads = both_cores(far_heads, "sp")
    all_heads = [held[d] for held in (near_heads, far_heads) for d in range(sp_count)]
    parts = out_parts(place, all_heads, out_weight, out_partner)
    parts = [
        lax.ppermute(
            part,
            ("tp", "sp"),
            [
                (t * sp_count + s, s * sp_count + (t ^ e))
                for t in range(sp_count)
                for s in range(sp_count)
            ],
        )
        for e, part in enumerate(parts)
    ]
    hidden = lax.dynamic_slice_in_dim(hidden_cont, tp_index * width, width, 1)
    return final_sum(place, parts, hidden)


def solution(mesh):
    placed = (
        P(("groups", "sp"), None),
        P(("groups", "sp"), None),
        P(),
        P("sp", "tp"),
        P("sp", None),
        P("tp", "sp"),
        P(),
        P(),
        P("groups"),
    )
    return jax.shard_map(
        on_device, mesh=mesh, in_specs=placed, out_specs=P(("groups", "sp"), "tp"), check_vma=False
    )
```

```python
import functools
import math

import jax
import jax.numpy as jnp
from jax import lax
from jax.experimental import pallas as pl
from jax.experimental.pallas import tpu as pltpu
from jax.sharding import PartitionSpec as P

QH = 32
KVH = 4
SP, TP, GROUP, HEAD = range(4)
BF16 = jnp.bfloat16
F32 = jnp.float32
ROOM = 14 * 1024 * 1024
ALL = 62 * 1024 * 1024


def call(kernel, place, grid, in_specs, out_specs, out_shape, args, cost, scratch=(), room=ROOM):
    flops, moved = cost
    return pl.pallas_call(
        kernel,
        out_shape=out_shape,
        grid_spec=pltpu.PrefetchScalarGridSpec(
            num_scalar_prefetch=1,
            grid=grid,
            in_specs=in_specs,
            out_specs=out_specs,
            scratch_shapes=scratch,
        ),
        compiler_params=pltpu.CompilerParams(vmem_limit_bytes=room),
        cost_estimate=pl.CostEstimate(flops=flops, bytes_accessed=moved, transcendentals=0),
    )(place, *args)


def whole(array):
    zeros = (0,) * array.ndim
    return pl.BlockSpec(array.shape, lambda i, place: zeros)


def shape_of(shape, dtype):
    return jax.ShapeDtypeStruct(shape, dtype)


def rms_rows(values, gain):
    return values * lax.rsqrt(jnp.mean(values * values, axis=-1, keepdims=True) + 1e-06) * gain


def split_normed(hidden, gain, out):
    count, _, depth = out.shape
    normed = rms_rows(hidden[...].astype(F32), gain[...]).astype(BF16)
    for j in range(count):
        out[j] = normed[:, j * depth : (j + 1) * depth]


def norm_kernel(place, hidden, gain, out):
    split_normed(hidden, gain, out)


def norm_split(place, hidden, gain, count):
    rows, width = hidden.shape
    step = min(rows, 64)
    out = (count, rows, width // count)
    return call(
        norm_kernel,
        place,
        (rows // step,),
        [pl.BlockSpec((step, width), lambda i, place: (i, 0)), whole(gain)],
        pl.BlockSpec((count, step, width // count), lambda i, place: (0, i, 0)),
        shape_of(out, BF16),
        (hidden, gain),
        (4 * rows * width, 4 * rows * width),
    )


def pick_kernel(place, weight, upper, lower, both, sems):
    rows, size = upper.shape
    half = pl.multiple_of((2 * place[HEAD] + place[GROUP]) * size, size)
    head = pl.multiple_of(2 * place[HEAD] * size, size)
    copies = [
        pltpu.make_async_copy(weight.at[0:rows, pl.ds(half, size)], upper, sems.at[0]),
        pltpu.make_async_copy(weight.at[rows : 2 * rows, pl.ds(half, size)], lower, sems.at[1]),
        pltpu.make_async_copy(weight.at[:, pl.ds(head, 2 * size)], both, sems.at[2]),
    ]
    for copy in copies:
        copy.start()
    for copy in copies:
        copy.wait()


def pick_columns(place, weight, size):
    depth = weight.shape[0]
    outs = [shape_of((depth // 2, size), BF16)] * 2 + [shape_of((depth, 2 * size), BF16)]
    return call(
        pick_kernel,
        place,
        (1,),
        [pl.BlockSpec(memory_space=pl.ANY)],
        [pl.BlockSpec(memory_space=pl.ANY)] * 3,
        outs,
        (weight,),
        (0, 12 * depth * size),
        [pltpu.SemaphoreType.DMA((3,))],
        ALL,
    )


def query_kernel(count, place, rows, weight, *outs):
    block = rows.shape[1]
    left = jnp.concatenate([rows[place[SP] ^ d] for d in range(count)], axis=0)
    part = jnp.dot(left, weight[...], preferred_element_type=F32)
    for d in range(count):
        outs[d][...] = part[d * block : (d + 1) * block]


def query_parts(place, rows, weight):
    count, block, depth = rows.shape
    width = weight.shape[1]
    step = min(width, 256)
    return call(
        functools.partial(query_kernel, count),
        place,
        (width // step,),
        [whole(rows), pl.BlockSpec((depth, step), lambda i, place: (0, i))],
        [pl.BlockSpec((block, step), lambda i, place: (0, i))] * count,
        [shape_of((block, width), F32)] * count,
        (rows, weight),
        (2 * count * block * depth * width, 2 * depth * width),
    )


def turn(values, cosine, sine):
    return values * cosine + pltpu.roll(values, values.shape[-1] // 2, 1) * sine


def near_kernel(place, hidden, norm_gain, cont, own, partner, prompt, out):
    split_normed(hidden, norm_gain, prompt)
    total = 0.0
    for d, weight in ((0, own), (1, partner)):
        left = jnp.concatenate([prompt[place[SP] ^ d], cont[place[SP] ^ d]], axis=0)
        total = total + jnp.dot(left, weight[...], preferred_element_type=F32)
    out[...] = total


def near_keyval(place, hidden, norm_gain, cont, own, partner):
    args = (hidden, norm_gain, cont, own, partner)
    count, cont_rows, depth = cont.shape
    prompt_rows = hidden.shape[0]
    rows = prompt_rows + cont_rows
    width = own.shape[1]
    outs = [shape_of((count, prompt_rows, depth), BF16), shape_of((rows, width), F32)]
    return call(
        near_kernel,
        place,
        (1,),
        [whole(a) for a in args],
        [whole(out) for out in outs],
        outs,
        args,
        (4 * rows * depth * width, 4 * depth * (rows * count + width)),
    )


def keyval_kernel(count, place, prompt, cont, cosine, sine, gain, near, *refs):
    weights, out = refs[:-1], refs[-1]
    size = gain.shape[1]
    total = 0.0
    for d in range(2, count):
        left = jnp.concatenate([prompt[place[SP] ^ d], cont[place[SP] ^ d]], axis=0)
        four = [weight[...] for weight in weights[4 * d - 8 : 4 * d - 4]]
        weight = jnp.concatenate(
            [jnp.concatenate(four[i : i + 2], axis=0) for i in (0, 2)], axis=1
        )
        total = total + jnp.dot(left, weight, preferred_element_type=F32)
    swapped = place[GROUP] == 1
    first, second = total[:, :size], total[:, size:]
    key = near[:, :size] + jnp.where(swapped, second, first)
    value = near[:, size:] + jnp.where(swapped, first, second)
    out[:, :size] = turn(rms_rows(key, gain[...]), cosine[...], sine[...]).astype(BF16)
    out[:, size:] = value.astype(BF16)


def keyval_rows(place, prompt, cont, cosine, sine, gain, near, weights):
    count, prompt_rows, depth = prompt.shape
    rows = prompt_rows + cont.shape[1]
    size = gain.shape[1]
    args = (prompt, cont, cosine, sine, gain, near, *weights)
    out = shape_of((rows, 2 * size), BF16)
    return call(
        functools.partial(keyval_kernel, count),
        place,
        (1,),
        [whole(a) for a in args],
        whole(out),
        out,
        args,
        (2 * rows * count * depth * size, count * depth * (rows + 2 * size)),
    )


def attend_kernel(count, prompt_rows, place, lengths, mine, other, cosine, sine, gain, *refs):
    pairs, out = refs[:-1], refs[-1]
    rows, width = mine.shape
    size = gain.shape[1]
    heads = width // size
    queries = []
    for h in range(heads):
        part = slice(h * size, (h + 1) * size)
        value = rms_rows(mine[:, part] + other[:, part], gain[...])
        queries.append(turn(value, cosine[...], sine[...]).astype(BF16))
    queries = jnp.concatenate(queries, axis=0)
    prompt = jnp.concatenate([pair[:prompt_rows] for pair in pairs], axis=0)
    cont = jnp.concatenate([pair[prompt_rows:] for pair in pairs], axis=0)
    scale = 1.0 / math.sqrt(size)
    by_rows = (((1,), (1,)), ((), ()))
    to_prompt = (
        lax.dot_general(queries, prompt[:, :size], by_rows, preferred_element_type=F32) * scale
    )
    to_cont = (
        lax.dot_general(queries, cont[:, :size], by_rows, preferred_element_type=F32) * scale
    )
    shape = (rows, cont.shape[0])
    own = place[SP] * rows + lax.broadcasted_iota(jnp.int32, shape, 0)
    at = lax.broadcasted_iota(jnp.int32, shape, 1)
    key = jnp.zeros(shape, jnp.int32)
    for d in range(count):
        inside = (at >= d * rows) & (at < (d + 1) * rows)
        key = jnp.where(inside, (place[SP] ^ d) * rows + at - d * rows, key)
    start = jnp.zeros(shape, jnp.int32)
    total = jnp.int32(0)
    for c in range(lengths.shape[0]):
        start = jnp.where(own >= total, total, start)
        total = total + lengths[c]
    allowed = jnp.where((key >= start) & (key <= own), 0.0, -1e30)
    to_cont = to_cont + jnp.concatenate([allowed] * heads, axis=0)
    peak = jnp.maximum(
        jnp.max(to_prompt, axis=1, keepdims=True), jnp.max(to_cont, axis=1, keepdims=True)
    )
    to_prompt = jnp.exp(to_prompt - peak)
    to_cont = jnp.exp(to_cont - peak)
    divisor = jnp.sum(to_prompt, axis=1, keepdims=True) + jnp.sum(to_cont, axis=1, keepdims=True)
    result = jnp.dot(
        (to_prompt / divisor).astype(BF16), prompt[:, size:], preferred_element_type=F32
    ) + jnp.dot((to_cont / divisor).astype(BF16), cont[:, size:], preferred_element_type=F32)
    for h in range(heads):
        out[:, h * size : (h + 1) * size] = result[h * rows : (h + 1) * rows].astype(BF16)


def attend(place, lengths, mine, other, cosine, sine, gain, pairs, prompt_rows):
    rows, width = mine.shape
    args = (mine, other, cosine, sine, gain, *pairs)
    out = shape_of((rows, width), BF16)
    keys = len(pairs) * pairs[0].shape[0]
    return call(
        functools.partial(attend_kernel, len(pairs), prompt_rows),
        place,
        (1,),
        [pl.BlockSpec(memory_space=pltpu.SMEM)] + [whole(a) for a in args],
        whole(out),
        out,
        (lengths, *args),
        (4 * rows * width * keys, 10 * rows * width + 512 * keys),
    )


def out_kernel(count, place, *refs):
    heads, weights, outs, part = refs[: 2 * count], refs[-count - 3 : -count - 1], refs[-count - 1 : -1], refs[-1]
    rows = heads[0].shape[0]
    total = 0.0
    for side, weight in enumerate(weights):
        left = jnp.concatenate([h[...] for h in heads[side * count : (side + 1) * count]], axis=0)
        share = jnp.dot(left, weight[...], preferred_element_type=F32)
        total = total + share.astype(BF16).astype(F32)
    total = total.astype(BF16)
    for d in range(count):
        part[d] = total[d * rows : (d + 1) * rows]
    for e in range(count):
        outs[e][...] = part[place[TP] ^ e ^ place[SP]]


def out_parts(place, heads, own, partner):
    count = len(heads) // 2
    rows = heads[0].shape[0]
    depth, width = partner.shape
    if width % 128:
        own = lax.dynamic_slice_in_dim(own, place[TP] % 2 * width, width, 1)
        half = whole(own)
    else:
        half = pl.BlockSpec((depth, width), lambda i, place: (0, place[TP] % 2))
    args = (*heads, own, partner)
    return call(
        functools.partial(out_kernel, count),
        place,
        (1,),
        [whole(h) for h in heads] + [half, whole(partner)],
        [pl.BlockSpec((rows, width), lambda i, place: (0, 0))] * count,
        [shape_of((rows, width), BF16)] * count,
        args,
        (4 * count * rows * depth * width, 4 * depth * width),
        [pltpu.VMEM((count, rows, width), BF16)],
    )


def final_kernel(count, place, hidden, *refs):
    parts, out = refs[:-1], refs[-1]
    width = parts[0].shape[1]
    sums = [0.0, 0.0]
    for e, part in enumerate(parts):
        sums[e % 2] = sums[e % 2] + part[...].astype(F32)
    odd = place[SP] % 2 == 1
    left = jnp.where(odd, sums[1], sums[0])
    right = jnp.where(odd, sums[0], sums[1])
    out[:, :width] = (hidden[:, :width].astype(F32) + left).astype(BF16)
    out[:, width:] = (hidden[:, width:].astype(F32) + right).astype(BF16)


def final_sum(place, parts, hidden):
    rows, width = hidden.shape
    count = len(parts)
    return call(
        functools.partial(final_kernel, count),
        place,
        (1,),
        [whole(a) for a in (hidden, *parts)],
        whole(hidden),
        shape_of((rows, width), BF16),
        (hidden, *parts),
        (count * rows * width, 12 * rows * width),
    )


def after(arrays, *others):
    return lax.optimization_barrier((arrays, others))[0]


def swap(array, axis, bits):
    return lax.ppermute(array, axis, [(i, i ^ bits) for i in range(lax.axis_size(axis))])


def swap_both(array, tp_bits, sp_bits, count):
    pairs = [
        (t * count + s, (t ^ tp_bits) * count + (s ^ sp_bits))
        for t in range(count)
        for s in range(count)
    ]
    return lax.ppermute(array, ("tp", "sp"), pairs)


def swap_bits(count):
    bits = []
    bit = 1
    while bit < count:
        bits.append(bit)
        bit *= 2
    return bits


def gather_blocks(block, axis, count):
    held = {0: block}
    bits = swap_bits(count)
    for bit in bits[1:] + bits[:1]:
        held.update({d ^ bit: swap(held[d], axis, bit) for d in sorted(held)})
    return [held[d] for d in range(count)]


def other_halves(half, axis, count):
    firsts = {0: half}
    for bit in swap_bits(count)[1:]:
        firsts.update({d ^ bit: swap(firsts[d], axis, bit) for d in sorted(firsts)})
    del firsts[0]
    return firsts


def both_cores(held, axis):
    return {**held, **{d ^ 1: swap(held[d], axis, 1) for d in sorted(held)}}


def sum_blocks(blocks, axis, count):
    held = dict(enumerate(blocks))
    bits = swap_bits(count)
    for bit in bits:
        sent = [d for d in sorted(held) if d & bit]
        got = {d ^ bit: swap(held[d], axis, bit) for d in sent}
        if bit == bits[-1]:
            return held[0], got[0]
        held = {d: held[d] + got[d] for d in got}


def tables(positions, size):
    half = size // 2
    frequency = jnp.exp(jnp.arange(half, dtype=F32) * (-2.0 * math.log(1000000.0) / size))
    angles = positions.astype(F32)[:, None] * frequency[None, :]
    cosine = jnp.cos(angles)
    sine = jnp.sin(angles)
    return (
        jnp.concatenate([cosine, cosine], axis=1),
        jnp.concatenate([-sine, sine], axis=1),
    )


def on_device(
    hidden_cont,
    hidden_prompt,
    norm_gain,
    query_weight,
    keyval_weight,
    out_weight,
    query_gain,
    key_gain,
    sample_lengths,
):
    size = query_gain.shape[0]
    heads_here = query_weight.shape[1] // size
    cont_rows = hidden_cont.shape[0]
    prompt_rows = hidden_prompt.shape[0]
    sp_index = lax.axis_index("sp")
    sp_count = lax.axis_size("sp")
    tp_index = lax.axis_index("tp")
    assert lax.axis_size("tp") == sp_count and lax.axis_size("groups") == 2
    place = jnp.stack(
        [
            sp_index,
            tp_index,
            lax.axis_index("groups"),
            tp_index * heads_here // (QH // KVH),
        ]
    ).astype(jnp.int32)
    norm_gain = norm_gain[None, :]
    query_gain = query_gain[None, :]
    key_gain = key_gain[None, :]

    upper, lower, both = pick_columns(place, keyval_weight, size)
    upper = other_halves(upper, "sp", sp_count)
    lower = other_halves(lower, "sp", sp_count)
    cont = norm_split(place, hidden_cont, norm_gain, sp_count)
    cont_all = lax.all_to_all(cont, "sp", 0, 0, tiled=True)
    partner = swap(both, "sp", 1)
    others = [{d: swap(a, "groups", 1) for d, a in held.items()} for held in (upper, lower)]
    upper = both_cores(upper, "sp")
    lower = both_cores(lower, "sp")
    width = out_weight.shape[1]
    side = tp_index % 2
    out_early = after(out_weight, others[0], lower)
    sent = lax.dynamic_slice_in_dim(out_early, (1 - side) * (width // 2), width // 2, 1)
    out_partner = swap(sent, "tp", 1)
    prompt, near_pair = near_keyval(
        place, hidden_prompt, norm_gain, cont, both, after(partner, lower)
    )
    cont_all = after(cont_all, near_pair, others, sent)
    others = [both_cores(held, "sp") for held in others]

    index = sp_index * cont_rows + jnp.arange(cont_rows, dtype=jnp.int32)
    starts = jnp.cumsum(sample_lengths, dtype=jnp.int32) - sample_lengths
    start = jnp.max(jnp.where(index[:, None] >= starts[None, :], starts[None, :], 0), axis=1)
    prompt_pos = sp_index * prompt_rows + jnp.arange(prompt_rows, dtype=jnp.int32)
    positions = jnp.concatenate([prompt_pos, prompt_rows * sp_count + index - start])
    cosine, sine = tables(positions, size)

    parts = query_parts(place, cont_all, query_weight)
    mine, other = sum_blocks(parts, "sp", sp_count)
    weights = [held[d] for d in range(2, sp_count) for held in (upper, lower, *others)]
    pair = keyval_rows(place, prompt, cont, cosine, sine, key_gain, near_pair, weights)
    pairs = gather_blocks(pair, "sp", sp_count)
    heads = attend(
        place,
        sample_lengths,
        mine,
        other,
        cosine[prompt_rows:],
        sine[prompt_rows:],
        query_gain,
        pairs,
        prompt_rows,
    )
    chips = range(0, sp_count, 2)
    near_heads = {d: swap(heads, "sp", d) if d else heads for d in chips}
    far_heads = {d: swap_both(heads, 1, d, sp_count) for d in chips}
    near_heads = both_cores(near_heads, "sp")
    far_heads = both_cores(far_heads, "sp")
    all_heads = [held[d] for held in (near_heads, far_heads) for d in range(sp_count)]
    parts = out_parts(place, all_heads, out_weight, out_partner)
    parts = [
        lax.ppermute(
            part,
            ("tp", "sp"),
            [
                (t * sp_count + s, s * sp_count + (t ^ e))
                for t in range(sp_count)
                for s in range(sp_count)
            ],
        )
        for e, part in enumerate(parts)
    ]
    hidden = lax.dynamic_slice_in_dim(hidden_cont, tp_index * width, width, 1)
    return final_sum(place, parts, hidden)


def solution(mesh):
    placed = (
        P(("groups", "sp"), None),
        P(("groups", "sp"), None),
        P(),
        P("sp", "tp"),
        P("sp", None),
        P("tp", "sp"),
        P(),
        P(),
        P("groups"),
    )
    return jax.shard_map(
        on_device, mesh=mesh, in_specs=placed, out_specs=P(("groups", "sp"), "tp"), check_vma=False
    )
```

```python
import functools
import math

import jax
import jax.numpy as jnp
from jax import lax
from jax.experimental import pallas as pl
from jax.experimental.pallas import tpu as pltpu
from jax.sharding import PartitionSpec as P

QH = 32
KVH = 4
SP, TP, GROUP, HEAD = range(4)
BF16 = jnp.bfloat16
F32 = jnp.float32
ROOM = 14 * 1024 * 1024


def call(kernel, place, grid, in_specs, out_specs, out_shape, args, cost, scratch=(), room=ROOM):
    flops, moved = cost
    return pl.pallas_call(
        kernel,
        out_shape=out_shape,
        grid_spec=pltpu.PrefetchScalarGridSpec(
            num_scalar_prefetch=1,
            grid=grid,
            in_specs=in_specs,
            out_specs=out_specs,
            scratch_shapes=scratch,
        ),
        compiler_params=pltpu.CompilerParams(vmem_limit_bytes=room),
        cost_estimate=pl.CostEstimate(flops=flops, bytes_accessed=moved, transcendentals=0),
    )(place, *args)


def whole(array):
    zeros = (0,) * array.ndim
    return pl.BlockSpec(array.shape, lambda i, place: zeros)


def shape_of(shape, dtype):
    return jax.ShapeDtypeStruct(shape, dtype)


def rms_rows(values, gain):
    return values * lax.rsqrt(jnp.mean(values * values, axis=-1, keepdims=True) + 1e-06) * gain


def split_normed(hidden, gain, out):
    count, _, depth = out.shape
    normed = rms_rows(hidden[...].astype(F32), gain[...]).astype(BF16)
    for j in range(count):
        out[j] = normed[:, j * depth : (j + 1) * depth]


def norm_kernel(place, hidden, gain, out):
    split_normed(hidden, gain, out)


def norm_split(place, hidden, gain, count):
    rows, width = hidden.shape
    step = min(rows, 64)
    out = (count, rows, width // count)
    return call(
        norm_kernel,
        place,
        (rows // step,),
        [pl.BlockSpec((step, width), lambda i, place: (i, 0)), whole(gain)],
        pl.BlockSpec((count, step, width // count), lambda i, place: (0, i, 0)),
        shape_of(out, BF16),
        (hidden, gain),
        (4 * rows * width, 4 * rows * width),
    )


def pick_kernel(place, first, key, value, half, both):
    size = half.shape[1]
    half[...] = first[...]
    both[:, :size] = key[...]
    both[:, size:] = value[...]


def pick_columns(place, weight, size):
    depth = weight.shape[0]
    block = (depth, size)
    outs = [shape_of(block, BF16), shape_of((depth, 2 * size), BF16)]
    return call(
        pick_kernel,
        place,
        (1,),
        [
            pl.BlockSpec(block, lambda i, place: (0, 2 * place[HEAD] + place[GROUP])),
            pl.BlockSpec(block, lambda i, place: (0, 2 * place[HEAD])),
            pl.BlockSpec(block, lambda i, place: (0, 2 * place[HEAD] + 1)),
        ],
        [whole(out) for out in outs],
        outs,
        (weight, weight, weight),
        (0, 12 * depth * size),
    )


def query_kernel(count, place, rows, weight, keep, send):
    block = rows.shape[1]
    left = jnp.concatenate([rows[place[SP] ^ d] for d in range(count)], axis=0)
    part = jnp.dot(left, weight[...], preferred_element_type=F32)
    for d in range(count):
        at = d // 2 * block
        (keep, send)[d % 2][at : at + block, :] = part[d * block : (d + 1) * block]


def query_parts(place, rows, weight):
    count, block, depth = rows.shape
    width = weight.shape[1]
    step = min(width, 256)
    half = count // 2 * block
    return call(
        functools.partial(query_kernel, count),
        place,
        (width // step,),
        [whole(rows), pl.BlockSpec((depth, step), lambda i, place: (0, i))],
        [pl.BlockSpec((half, step), lambda i, place: (0, i))] * 2,
        [shape_of((half, width), F32)] * 2,
        (rows, weight),
        (2 * count * block * depth * width, 2 * depth * width),
    )


def turn(values, cosine, sine):
    return values * cosine + pltpu.roll(values, values.shape[-1] // 2, 1) * sine


def near_kernel(place, hidden, norm_gain, cont, own, partner, prompt, out):
    split_normed(hidden, norm_gain, prompt)
    total = 0.0
    for d, weight in ((0, own), (1, partner)):
        left = jnp.concatenate([prompt[place[SP] ^ d], cont[place[SP] ^ d]], axis=0)
        total = total + jnp.dot(left, weight[...], preferred_element_type=F32)
    out[...] = total


def near_keyval(place, hidden, norm_gain, cont, own, partner):
    args = (hidden, norm_gain, cont, own, partner)
    count, cont_rows, depth = cont.shape
    prompt_rows = hidden.shape[0]
    rows = prompt_rows + cont_rows
    width = own.shape[1]
    outs = [shape_of((count, prompt_rows, depth), BF16), shape_of((rows, width), F32)]
    return call(
        near_kernel,
        place,
        (1,),
        [whole(a) for a in args],
        [whole(out) for out in outs],
        outs,
        args,
        (4 * rows * depth * width, 4 * depth * (rows * count + width)),
    )


def keyval_kernel(count, place, prompt, cont, cosine, sine, gain, near, *refs):
    weights, out = refs[:-1], refs[-1]
    size = gain.shape[1]
    total = 0.0
    for d in range(2, count):
        left = jnp.concatenate([prompt[place[SP] ^ d], cont[place[SP] ^ d]], axis=0)
        weight = jnp.concatenate([weights[2 * d - 4][...], weights[2 * d - 3][...]], axis=1)
        total = total + jnp.dot(left, weight, preferred_element_type=F32)
    swapped = place[GROUP] == 1
    first, second = total[:, :size], total[:, size:]
    key = near[:, :size] + jnp.where(swapped, second, first)
    value = near[:, size:] + jnp.where(swapped, first, second)
    out[:, :size] = turn(rms_rows(key, gain[...]), cosine[...], sine[...]).astype(BF16)
    out[:, size:] = value.astype(BF16)


def keyval_rows(place, prompt, cont, cosine, sine, gain, near, weights):
    count, prompt_rows, depth = prompt.shape
    rows = prompt_rows + cont.shape[1]
    size = gain.shape[1]
    args = (prompt, cont, cosine, sine, gain, near, *weights)
    out = shape_of((rows, 2 * size), BF16)
    return call(
        functools.partial(keyval_kernel, count),
        place,
        (1,),
        [whole(a) for a in args],
        whole(out),
        out,
        args,
        (2 * rows * count * depth * size, count * depth * (rows + 2 * size)),
    )


def starts_of(lengths, index):
    start = jnp.zeros(index.shape, jnp.int32)
    total = jnp.int32(0)
    for c in range(lengths.shape[0]):
        start = jnp.where(index >= total, total, start)
        total = total + lengths[c]
    return start


def attend_kernel(count, prompt_rows, place, lengths, mine, near, far, cosine, sine, gain, *refs):
    pairs, out = refs[:-1], refs[-1]
    rows, width = far.shape
    size = gain.shape[1]
    heads = width // size
    cosine, sine = cosine[prompt_rows:, :], sine[prompt_rows:, :]
    queries = []
    for h in range(heads):
        part = slice(h * size, (h + 1) * size)
        value = rms_rows(mine[:rows, part] + near[:rows, part] + far[:, part], gain[...])
        queries.append(turn(value, cosine, sine).astype(BF16))
    queries = jnp.concatenate(queries, axis=0)
    prompt = jnp.concatenate([pair[:prompt_rows] for pair in pairs], axis=0)
    cont = jnp.concatenate([pair[prompt_rows:] for pair in pairs], axis=0)
    scale = 1.0 / math.sqrt(size)
    by_rows = (((1,), (1,)), ((), ()))
    to_prompt = (
        lax.dot_general(queries, prompt[:, :size], by_rows, preferred_element_type=F32) * scale
    )
    to_cont = (
        lax.dot_general(queries, cont[:, :size], by_rows, preferred_element_type=F32) * scale
    )
    shape = (rows, cont.shape[0])
    own = place[SP] * rows + lax.broadcasted_iota(jnp.int32, shape, 0)
    at = lax.broadcasted_iota(jnp.int32, shape, 1)
    key = jnp.zeros(shape, jnp.int32)
    for d in range(count):
        inside = (at >= d * rows) & (at < (d + 1) * rows)
        key = jnp.where(inside, (place[SP] ^ d) * rows + at - d * rows, key)
    allowed = jnp.where((key >= starts_of(lengths, own)) & (key <= own), 0.0, -1e30)
    to_cont = to_cont + jnp.concatenate([allowed] * heads, axis=0)
    peak = jnp.maximum(
        jnp.max(to_prompt, axis=1, keepdims=True), jnp.max(to_cont, axis=1, keepdims=True)
    )
    to_prompt = jnp.exp(to_prompt - peak)
    to_cont = jnp.exp(to_cont - peak)
    divisor = jnp.sum(to_prompt, axis=1, keepdims=True) + jnp.sum(to_cont, axis=1, keepdims=True)
    result = jnp.dot(
        (to_prompt / divisor).astype(BF16), prompt[:, size:], preferred_element_type=F32
    ) + jnp.dot((to_cont / divisor).astype(BF16), cont[:, size:], preferred_element_type=F32)
    for h in range(heads):
        out[:, h * size : (h + 1) * size] = result[h * rows : (h + 1) * rows].astype(BF16)


def attend(place, lengths, mine, near, far, cosine, sine, gain, pairs, prompt_rows):
    rows, width = far.shape
    args = (mine, near, far, cosine, sine, gain, *pairs)
    out = shape_of((rows, width), BF16)
    keys = len(pairs) * pairs[0].shape[0]
    return call(
        functools.partial(attend_kernel, len(pairs), prompt_rows),
        place,
        (1,),
        [pl.BlockSpec(memory_space=pltpu.SMEM)] + [whole(a) for a in args],
        whole(out),
        out,
        (lengths, *args),
        (4 * rows * width * keys, 10 * rows * width + 512 * keys),
    )


def out_kernel(count, place, *refs):
    heads, weights, outs, part = refs[: 2 * count], refs[-count - 3 : -count - 1], refs[-count - 1 : -1], refs[-1]
    rows = heads[0].shape[0]
    total = 0.0
    for side, weight in enumerate(weights):
        left = jnp.concatenate([h[...] for h in heads[side * count : (side + 1) * count]], axis=0)
        share = jnp.dot(left, weight[...], preferred_element_type=F32)
        total = total + share.astype(BF16).astype(F32)
    total = total.astype(BF16)
    for d in range(count):
        part[d] = total[d * rows : (d + 1) * rows]
    for e in range(count):
        outs[e][...] = part[place[TP] ^ e ^ place[SP]]


def out_parts(place, heads, own, partner):
    count = len(heads) // 2
    rows = heads[0].shape[0]
    depth, width = partner.shape
    if width % 128:
        own = column_half(place, own, False)
        half = whole(own)
    else:
        half = pl.BlockSpec((depth, width), lambda i, place: (0, place[TP] % 2))
    args = (*heads, own, partner)
    return call(
        functools.partial(out_kernel, count),
        place,
        (1,),
        [whole(h) for h in heads] + [half, whole(partner)],
        [pl.BlockSpec((rows, width), lambda i, place: (0, 0))] * count,
        [shape_of((rows, width), BF16)] * count,
        args,
        (4 * count * rows * depth * width, 4 * depth * width),
        [pltpu.VMEM((count, rows, width), BF16)],
    )


def final_kernel(count, place, hidden, *refs):
    parts, out = refs[:-1], refs[-1]
    width = parts[0].shape[1]
    sums = [0.0, 0.0]
    for e, part in enumerate(parts):
        sums[e % 2] = sums[e % 2] + part[...].astype(F32)
    odd = place[SP] % 2 == 1
    left = jnp.where(odd, sums[1], sums[0])
    right = jnp.where(odd, sums[0], sums[1])
    out[:, :width] = (hidden[:, :width].astype(F32) + left).astype(BF16)
    out[:, width:] = (hidden[:, width:].astype(F32) + right).astype(BF16)


def final_sum(place, parts, hidden):
    rows, width = parts[0].shape
    width *= 2
    count = len(parts)
    if width % 128:
        hidden = lax.dynamic_slice_in_dim(hidden, place[TP] * width, width, 1)
        residual = whole(hidden)
    else:
        residual = pl.BlockSpec((rows, width), lambda i, place: (0, place[TP]))
    return call(
        functools.partial(final_kernel, count),
        place,
        (1,),
        [residual] + [whole(a) for a in parts],
        pl.BlockSpec((rows, width), lambda i, place: (0, 0)),
        shape_of((rows, width), BF16),
        (hidden, *parts),
        (count * rows * width, 12 * rows * width),
    )


def after(arrays, *others):
    return lax.optimization_barrier((arrays, others))[0]


def swap(array, axis, bits):
    return lax.ppermute(array, axis, [(i, i ^ bits) for i in range(lax.axis_size(axis))])


def swap_both(array, tp_bits, sp_bits, count):
    pairs = [
        (t * count + s, (t ^ tp_bits) * count + (s ^ sp_bits))
        for t in range(count)
        for s in range(count)
    ]
    return lax.ppermute(array, ("tp", "sp"), pairs)


def swap_bits(count):
    bits = []
    bit = 1
    while bit < count:
        bits.append(bit)
        bit *= 2
    return bits


def gather_blocks(block, axis, count):
    held = {0: block}
    bits = swap_bits(count)
    for bit in bits[1:] + bits[:1]:
        held.update({d ^ bit: swap(held[d], axis, bit) for d in sorted(held)})
    return [held[d] for d in range(count)]


def other_halves(half, axis, count):
    firsts = {0: half}
    for bit in swap_bits(count)[1:]:
        firsts.update({d ^ bit: swap(firsts[d], axis, bit) for d in sorted(firsts)})
    del firsts[0]
    return firsts


def both_cores(held, axis):
    return {**held, **{d ^ 1: swap(held[d], axis, 1) for d in sorted(held)}}


def sum_blocks(place, keep, send, axis, count):
    near = swap(send, axis, 1)
    rows = keep.shape[0] // (count // 2)
    held = {d: add_rows(place, keep, near, d // 2 * rows, rows) for d in range(2, count, 2)}
    far = 0.0
    for bit in swap_bits(count)[1:]:
        sent = [d for d in sorted(held) if d & bit]
        got = {d ^ bit: swap(held[d], axis, bit) for d in sent}
        far = far + got.pop(0)
        held = {d: held[d] + got[d] for d in got}
    return keep, near, far


def table_kernel(prompt_rows, prompt_total, place, lengths, cosine, sine):
    rows, size = cosine.shape
    shape = cosine.shape
    row = lax.broadcasted_iota(jnp.int32, shape, 0)
    lane = lax.broadcasted_iota(jnp.int32, shape, 1)
    index = place[SP] * (rows - prompt_rows) + row - prompt_rows
    position = jnp.where(
        row < prompt_rows,
        place[SP] * prompt_rows + row,
        prompt_total + index - starts_of(lengths, index),
    )
    half = size // 2
    step = jnp.where(lane < half, lane, lane - half).astype(F32)
    angle = position.astype(F32) * jnp.exp(step * (-2.0 * math.log(1000000.0) / size))
    cosine[...] = jnp.cos(angle)
    angle = jnp.sin(angle)
    sine[...] = jnp.where(lane < half, -angle, angle)


def tables(place, lengths, prompt_rows, prompt_total, cont_rows, size):
    out = shape_of((prompt_rows + cont_rows, size), F32)
    return call(
        functools.partial(table_kernel, prompt_rows, prompt_total),
        place,
        (1,),
        [pl.BlockSpec(memory_space=pltpu.SMEM)],
        [whole(out)] * 2,
        [out] * 2,
        (lengths,),
        (100 * out.size, 8 * out.size),
    )


def slice_kernel(place, array, out):
    out[...] = array[...]


def column_half(place, array, other):
    rows, width = array.shape
    width //= 2
    side = 1 if other else 0
    if width % 128:
        at = (place[TP] + side) % 2 * width
        return lax.dynamic_slice_in_dim(array, at, width, 1)
    return call(
        slice_kernel,
        place,
        (4,),
        [pl.BlockSpec((rows // 4, width), lambda i, place: (i, (place[TP] + side) % 2))],
        pl.BlockSpec((rows // 4, width), lambda i, place: (i, 0)),
        shape_of((rows, width), BF16),
        (array,),
        (0, 4 * rows * width),
    )


def add_kernel(place, left, right, out):
    out[...] = left[...] + right[...]


def add_rows(place, left, right, at, rows):
    width = left.shape[1]
    spec = pl.BlockSpec((rows, width), lambda i, place: (at // rows, 0))
    return call(
        add_kernel,
        place,
        (1,),
        [spec, spec],
        pl.BlockSpec((rows, width), lambda i, place: (0, 0)),
        shape_of((rows, width), F32),
        (left, right),
        (rows * width, 12 * rows * width),
    )


def on_device(
    hidden_cont,
    hidden_prompt,
    norm_gain,
    query_weight,
    keyval_weight,
    out_weight,
    query_gain,
    key_gain,
    sample_lengths,
):
    size = query_gain.shape[0]
    heads_here = query_weight.shape[1] // size
    cont_rows = hidden_cont.shape[0]
    prompt_rows = hidden_prompt.shape[0]
    sp_index = lax.axis_index("sp")
    sp_count = lax.axis_size("sp")
    tp_index = lax.axis_index("tp")
    assert lax.axis_size("tp") == sp_count and lax.axis_size("groups") == 2
    place = jnp.stack(
        [
            sp_index,
            tp_index,
            lax.axis_index("groups"),
            tp_index * heads_here // (QH // KVH),
        ]
    ).astype(jnp.int32)
    norm_gain = norm_gain[None, :]
    query_gain = query_gain[None, :]
    key_gain = key_gain[None, :]

    cont = norm_split(place, hidden_cont, norm_gain, sp_count)
    half, both = pick_columns(place, keyval_weight, size)
    cont_all = lax.all_to_all(cont, "sp", 0, 0, tiled=True)
    halves = other_halves(half, "sp", sp_count)
    partner = swap(both, "sp", 1)
    halves = after(halves, cont)
    others = {d: swap(half, "groups", 1) for d, half in halves.items()}
    halves = both_cores(halves, "sp")
    sent = column_half(place, after(out_weight, halves), True)
    out_partner = swap(sent, "tp", 1)
    prompt, near_pair = near_keyval(
        place, hidden_prompt, norm_gain, cont, both, after(partner, halves)
    )
    cosine, sine = tables(
        place, sample_lengths, prompt_rows, prompt_rows * sp_count, cont_rows, size
    )
    cont_all = after(cont_all, near_pair, others, sent, cosine)
    others = both_cores(others, "sp")

    keep, send = query_parts(place, cont_all, query_weight)
    mine, near, far = sum_blocks(place, keep, send, "sp", sp_count)
    weights = [held[d] for d in range(2, sp_count) for held in (halves, others)]
    pair = keyval_rows(place, prompt, cont, cosine, sine, key_gain, near_pair, weights)
    pairs = gather_blocks(pair, "sp", sp_count)
    heads = attend(
        place,
        sample_lengths,
        mine,
        near,
        far,
        cosine,
        sine,
        query_gain,
        pairs,
        prompt_rows,
    )
    chips = range(0, sp_count, 2)
    near_heads = {d: swap(heads, "sp", d) if d else heads for d in chips}
    far_heads = {d: swap_both(heads, 1, d, sp_count) for d in chips}
    near_heads = both_cores(near_heads, "sp")
    far_heads = both_cores(far_heads, "sp")
    all_heads = [held[d] for held in (near_heads, far_heads) for d in range(sp_count)]
    parts = out_parts(place, all_heads, out_weight, out_partner)
    parts = [
        lax.ppermute(
            part,
            ("tp", "sp"),
            [
                (t * sp_count + s, s * sp_count + (t ^ e))
                for t in range(sp_count)
                for s in range(sp_count)
            ],
        )
        for e, part in enumerate(parts)
    ]
    return final_sum(place, parts, hidden_cont)


def solution(mesh):
    placed = (
        P(("groups", "sp"), None),
        P(("groups", "sp"), None),
        P(),
        P("sp", "tp"),
        P("sp", None),
        P("tp", "sp"),
        P(),
        P(),
        P("groups"),
    )
    return jax.shard_map(
        on_device, mesh=mesh, in_specs=placed, out_specs=P(("groups", "sp"), "tp"), check_vma=False
    )
```

```python
import functools
import math

import jax
import jax.numpy as jnp
from jax import lax
from jax.experimental import pallas as pl
from jax.experimental.pallas import tpu as pltpu
from jax.sharding import PartitionSpec as P

QH = 32
KVH = 4
SP, TP, GROUP, HEAD = range(4)
BF16 = jnp.bfloat16
F32 = jnp.float32
ROOM = 14 * 1024 * 1024


def call(kernel, place, grid, in_specs, out_specs, out_shape, args, cost, scratch=(), room=ROOM):
    flops, moved = cost
    return pl.pallas_call(
        kernel,
        out_shape=out_shape,
        grid_spec=pltpu.PrefetchScalarGridSpec(
            num_scalar_prefetch=1,
            grid=grid,
            in_specs=in_specs,
            out_specs=out_specs,
            scratch_shapes=scratch,
        ),
        compiler_params=pltpu.CompilerParams(vmem_limit_bytes=room),
        cost_estimate=pl.CostEstimate(flops=flops, bytes_accessed=moved, transcendentals=0),
    )(place, *args)


def whole(array):
    zeros = (0,) * array.ndim
    return pl.BlockSpec(array.shape, lambda i, place: zeros)


def shape_of(shape, dtype):
    return jax.ShapeDtypeStruct(shape, dtype)


def rms_rows(values, gain):
    return values * lax.rsqrt(jnp.mean(values * values, axis=-1, keepdims=True) + 1e-06) * gain


def split_normed(hidden, gain, out):
    count, _, depth = out.shape
    normed = rms_rows(hidden[...].astype(F32), gain[...]).astype(BF16)
    for j in range(count):
        out[j] = normed[:, j * depth : (j + 1) * depth]


def norm_kernel(place, hidden, gain, out, split):
    split_normed(hidden, gain, split)
    for d in range(out.shape[0]):
        out[d] = split[place[SP] ^ 1 ^ 2 * d]


def norm_split(place, hidden, gain, count):
    rows, width = hidden.shape
    step = rows if rows % 32 else 32
    depth = width // count
    return call(
        norm_kernel,
        place,
        (rows // step,),
        [pl.BlockSpec((step, width), lambda i, place: (i, 0)), whole(gain)],
        [
            pl.BlockSpec((n, step, depth), lambda i, place: (0, i, 0))
            for n in (count // 2, count)
        ],
        [shape_of((n, rows, depth), BF16) for n in (count // 2, count)],
        (hidden, gain),
        (4 * rows * width, 4 * rows * width),
    )


def pack_kernel(place, cont, other, *outs):
    for d, out in enumerate(outs, 1):
        out[0] = cont[place[SP] ^ 2 * d]
        out[1] = other[d]


def pack(place, cont, other):
    count, rows, depth = cont.shape
    block = (2, rows, depth)
    sent = count // 2 - 1
    return call(
        pack_kernel,
        place,
        (1,),
        [whole(cont), whole(other)],
        [pl.BlockSpec(block, lambda i, place: (0, 0, 0))] * sent,
        [shape_of(block, BF16)] * sent,
        (cont, other),
        (0, 8 * sent * rows * depth),
    )


def pick_kernel(place, first, key, value, half, both):
    size = half.shape[1]
    half[...] = first[...]
    both[:, :size] = key[...]
    both[:, size:] = value[...]


def pick_columns(place, weight, size):
    depth = weight.shape[0]
    block = (depth, size)
    outs = [shape_of(block, BF16), shape_of((depth, 2 * size), BF16)]
    return call(
        pick_kernel,
        place,
        (1,),
        [
            pl.BlockSpec(block, lambda i, place: (0, 2 * place[HEAD] + place[GROUP])),
            pl.BlockSpec(block, lambda i, place: (0, 2 * place[HEAD])),
            pl.BlockSpec(block, lambda i, place: (0, 2 * place[HEAD] + 1)),
        ],
        [whole(out) for out in outs],
        outs,
        (weight, weight, weight),
        (0, 12 * depth * size),
    )


def query_kernel(count, place, *refs):
    cont, other, chips, (weight, keep, send) = refs[0], refs[1], refs[2:-3], refs[-3:]
    block = cont.shape[1]
    rows = [cont[place[SP]], other[0]]
    for chip in chips:
        rows += [chip[0], chip[1]]
    part = jnp.dot(jnp.concatenate(rows, axis=0), weight[...], preferred_element_type=F32)
    for d in range(count):
        at = d // 2 * block
        (keep, send)[d % 2][at : at + block, :] = part[d * block : (d + 1) * block]


def query_parts(place, cont, got, weight):
    count, block, depth = cont.shape
    width = weight.shape[1]
    step = min(width, 256)
    half = count // 2 * block
    return call(
        functools.partial(query_kernel, count),
        place,
        (width // step,),
        [whole(a) for a in (cont, *got)]
        + [pl.BlockSpec((depth, step), lambda i, place: (0, i))],
        [pl.BlockSpec((half, step), lambda i, place: (0, i))] * 2,
        [shape_of((half, width), F32)] * 2,
        (cont, *got, weight),
        (2 * count * block * depth * width, 2 * depth * width),
    )


def turn(values, cosine, sine):
    return values * cosine + pltpu.roll(values, values.shape[-1] // 2, 1) * sine


def near_kernel(place, hidden, norm_gain, cont, own, partner, prompt, out):
    split_normed(hidden, norm_gain, prompt)
    total = 0.0
    for d, weight in ((0, own), (1, partner)):
        left = jnp.concatenate([prompt[place[SP] ^ d], cont[place[SP] ^ d]], axis=0)
        total = total + jnp.dot(left, weight[...], preferred_element_type=F32)
    out[...] = total


def near_keyval(place, hidden, norm_gain, cont, own, partner):
    args = (hidden, norm_gain, cont, own, partner)
    count, cont_rows, depth = cont.shape
    prompt_rows = hidden.shape[0]
    rows = prompt_rows + cont_rows
    width = own.shape[1]
    outs = [shape_of((count, prompt_rows, depth), BF16), shape_of((rows, width), F32)]
    return call(
        near_kernel,
        place,
        (1,),
        [whole(a) for a in args],
        [whole(out) for out in outs],
        outs,
        args,
        (4 * rows * depth * width, 4 * depth * (rows * count + width)),
    )


def keyval_kernel(count, place, prompt, cont, cosine, sine, gain, near, *refs):
    weights, out = refs[:-1], refs[-1]
    size = gain.shape[1]
    total = 0.0
    for d in range(2, count):
        left = jnp.concatenate([prompt[place[SP] ^ d], cont[place[SP] ^ d]], axis=0)
        weight = jnp.concatenate([weights[2 * d - 4][...], weights[2 * d - 3][...]], axis=1)
        total = total + jnp.dot(left, weight, preferred_element_type=F32)
    swapped = place[GROUP] == 1
    first, second = total[:, :size], total[:, size:]
    key = near[:, :size] + jnp.where(swapped, second, first)
    value = near[:, size:] + jnp.where(swapped, first, second)
    out[:, :size] = turn(rms_rows(key, gain[...]), cosine[...], sine[...]).astype(BF16)
    out[:, size:] = value.astype(BF16)


def keyval_rows(place, prompt, cont, cosine, sine, gain, near, weights):
    count, prompt_rows, depth = prompt.shape
    rows = prompt_rows + cont.shape[1]
    size = gain.shape[1]
    args = (prompt, cont, cosine, sine, gain, near, *weights)
    out = shape_of((rows, 2 * size), BF16)
    return call(
        functools.partial(keyval_kernel, count),
        place,
        (1,),
        [whole(a) for a in args],
        whole(out),
        out,
        args,
        (2 * rows * count * depth * size, count * depth * (rows + 2 * size)),
    )


def starts_of(lengths, index):
    start = jnp.zeros(index.shape, jnp.int32)
    total = jnp.int32(0)
    for c in range(lengths.shape[0]):
        start = jnp.where(index >= total, total, start)
        total = total + lengths[c]
    return start


def attend_kernel(count, prompt_rows, place, lengths, mine, near, far, cosine, sine, gain, *refs):
    pairs, out = refs[:-1], refs[-1]
    rows, width = far.shape
    size = gain.shape[1]
    heads = width // size
    cosine, sine = cosine[prompt_rows:, :], sine[prompt_rows:, :]
    queries = []
    for h in range(heads):
        part = slice(h * size, (h + 1) * size)
        value = rms_rows(mine[:rows, part] + near[:rows, part] + far[:, part], gain[...])
        queries.append(turn(value, cosine, sine).astype(BF16))
    queries = jnp.concatenate(queries, axis=0)
    prompt = jnp.concatenate([pair[:prompt_rows] for pair in pairs], axis=0)
    cont = jnp.concatenate([pair[prompt_rows:] for pair in pairs], axis=0)
    scale = 1.0 / math.sqrt(size)
    by_rows = (((1,), (1,)), ((), ()))
    to_prompt = (
        lax.dot_general(queries, prompt[:, :size], by_rows, preferred_element_type=F32) * scale
    )
    to_cont = (
        lax.dot_general(queries, cont[:, :size], by_rows, preferred_element_type=F32) * scale
    )
    shape = (rows, cont.shape[0])
    own = place[SP] * rows + lax.broadcasted_iota(jnp.int32, shape, 0)
    at = lax.broadcasted_iota(jnp.int32, shape, 1)
    key = jnp.zeros(shape, jnp.int32)
    for d in range(count):
        inside = (at >= d * rows) & (at < (d + 1) * rows)
        key = jnp.where(inside, (place[SP] ^ d) * rows + at - d * rows, key)
    allowed = jnp.where((key >= starts_of(lengths, own)) & (key <= own), 0.0, -1e30)
    to_cont = to_cont + jnp.concatenate([allowed] * heads, axis=0)
    peak = jnp.maximum(
        jnp.max(to_prompt, axis=1, keepdims=True), jnp.max(to_cont, axis=1, keepdims=True)
    )
    to_prompt = jnp.exp(to_prompt - peak)
    to_cont = jnp.exp(to_cont - peak)
    divisor = jnp.sum(to_prompt, axis=1, keepdims=True) + jnp.sum(to_cont, axis=1, keepdims=True)
    result = jnp.dot(
        (to_prompt / divisor).astype(BF16), prompt[:, size:], preferred_element_type=F32
    ) + jnp.dot((to_cont / divisor).astype(BF16), cont[:, size:], preferred_element_type=F32)
    for h in range(heads):
        out[:, h * size : (h + 1) * size] = result[h * rows : (h + 1) * rows].astype(BF16)


def attend(place, lengths, mine, near, far, cosine, sine, gain, pairs, prompt_rows):
    rows, width = far.shape
    args = (mine, near, far, cosine, sine, gain, *pairs)
    out = shape_of((rows, width), BF16)
    keys = len(pairs) * pairs[0].shape[0]
    return call(
        functools.partial(attend_kernel, len(pairs), prompt_rows),
        place,
        (1,),
        [pl.BlockSpec(memory_space=pltpu.SMEM)] + [whole(a) for a in args],
        whole(out),
        out,
        (lengths, *args),
        (4 * rows * width * keys, 10 * rows * width + 512 * keys),
    )


def out_kernel(count, place, *refs):
    heads, weights, outs, part = refs[: 2 * count], refs[-count - 3 : -count - 1], refs[-count - 1 : -1], refs[-1]
    rows = heads[0].shape[0]
    total = 0.0
    for side, weight in enumerate(weights):
        left = jnp.concatenate([h[...] for h in heads[side * count : (side + 1) * count]], axis=0)
        share = jnp.dot(left, weight[...], preferred_element_type=F32)
        total = total + share.astype(BF16).astype(F32)
    total = total.astype(BF16)
    for d in range(count):
        part[d] = total[d * rows : (d + 1) * rows]
    for e in range(count):
        outs[e][...] = part[place[TP] ^ e ^ place[SP]]


def out_parts(place, heads, own, partner):
    count = len(heads) // 2
    rows = heads[0].shape[0]
    depth, width = partner.shape
    if width % 128:
        own = column_half(place, own, False)
        half = whole(own)
    else:
        half = pl.BlockSpec((depth, width), lambda i, place: (0, place[TP] % 2))
    args = (*heads, own, partner)
    return call(
        functools.partial(out_kernel, count),
        place,
        (1,),
        [whole(h) for h in heads] + [half, whole(partner)],
        [pl.BlockSpec((rows, width), lambda i, place: (0, 0))] * count,
        [shape_of((rows, width), BF16)] * count,
        args,
        (4 * count * rows * depth * width, 4 * depth * width),
        [pltpu.VMEM((count, rows, width), BF16)],
    )


def final_kernel(count, place, hidden, *refs):
    parts, out = refs[:-1], refs[-1]
    width = parts[0].shape[1]
    sums = [0.0, 0.0]
    for e, part in enumerate(parts):
        sums[e % 2] = sums[e % 2] + part[...].astype(F32)
    odd = place[SP] % 2 == 1
    left = jnp.where(odd, sums[1], sums[0])
    right = jnp.where(odd, sums[0], sums[1])
    out[:, :width] = (hidden[:, :width].astype(F32) + left).astype(BF16)
    out[:, width:] = (hidden[:, width:].astype(F32) + right).astype(BF16)


def final_sum(place, parts, hidden):
    rows, width = parts[0].shape
    width *= 2
    count = len(parts)
    if width % 128:
        hidden = lax.dynamic_slice_in_dim(hidden, place[TP] * width, width, 1)
        residual = whole(hidden)
    else:
        residual = pl.BlockSpec((rows, width), lambda i, place: (0, place[TP]))
    return call(
        functools.partial(final_kernel, count),
        place,
        (1,),
        [residual] + [whole(a) for a in parts],
        pl.BlockSpec((rows, width), lambda i, place: (0, 0)),
        shape_of((rows, width), BF16),
        (hidden, *parts),
        (count * rows * width, 12 * rows * width),
    )


def after(arrays, *others):
    return lax.optimization_barrier((arrays, others))[0]


def swap(array, axis, bits):
    return lax.ppermute(array, axis, [(i, i ^ bits) for i in range(lax.axis_size(axis))])


def swap_both(array, tp_bits, sp_bits, count):
    pairs = [
        (t * count + s, (t ^ tp_bits) * count + (s ^ sp_bits))
        for t in range(count)
        for s in range(count)
    ]
    return lax.ppermute(array, ("tp", "sp"), pairs)


def swap_bits(count):
    bits = []
    bit = 1
    while bit < count:
        bits.append(bit)
        bit *= 2
    return bits


def gather_blocks(block, axis, count):
    held = {0: block}
    bits = swap_bits(count)
    for bit in bits[1:] + bits[:1]:
        held.update({d ^ bit: swap(held[d], axis, bit) for d in sorted(held)})
    return [held[d] for d in range(count)]


def other_halves(half, axis, count):
    firsts = {0: half}
    for bit in swap_bits(count)[1:]:
        firsts.update({d ^ bit: swap(firsts[d], axis, bit) for d in sorted(firsts)})
    del firsts[0]
    return firsts


def both_cores(held, axis):
    return {**held, **{d ^ 1: swap(held[d], axis, 1) for d in sorted(held)}}


def sum_blocks(place, keep, send, axis, count):
    near = swap(send, axis, 1)
    rows = keep.shape[0] // (count // 2)
    held = {d: add_rows(place, keep, near, d // 2 * rows, rows) for d in range(2, count, 2)}
    far = 0.0
    for bit in swap_bits(count)[1:]:
        sent = [d for d in sorted(held) if d & bit]
        got = {d ^ bit: swap(held[d], axis, bit) for d in sent}
        far = far + got.pop(0)
        held = {d: held[d] + got[d] for d in got}
    return keep, near, far


def table_kernel(prompt_rows, prompt_total, place, lengths, cosine, sine):
    rows, size = cosine.shape
    shape = cosine.shape
    row = lax.broadcasted_iota(jnp.int32, shape, 0)
    lane = lax.broadcasted_iota(jnp.int32, shape, 1)
    index = place[SP] * (rows - prompt_rows) + row - prompt_rows
    position = jnp.where(
        row < prompt_rows,
        place[SP] * prompt_rows + row,
        prompt_total + index - starts_of(lengths, index),
    )
    half = size // 2
    step = jnp.where(lane < half, lane, lane - half).astype(F32)
    angle = position.astype(F32) * jnp.exp(step * (-2.0 * math.log(1000000.0) / size))
    cosine[...] = jnp.cos(angle)
    angle = jnp.sin(angle)
    sine[...] = jnp.where(lane < half, -angle, angle)


def tables(place, lengths, prompt_rows, prompt_total, cont_rows, size):
    out = shape_of((prompt_rows + cont_rows, size), F32)
    return call(
        functools.partial(table_kernel, prompt_rows, prompt_total),
        place,
        (1,),
        [pl.BlockSpec(memory_space=pltpu.SMEM)],
        [whole(out)] * 2,
        [out] * 2,
        (lengths,),
        (100 * out.size, 8 * out.size),
    )


def slice_kernel(place, array, out):
    out[...] = array[...]


def column_half(place, array, other):
    rows, width = array.shape
    width //= 2
    side = 1 if other else 0
    if width % 128:
        at = (place[TP] + side) % 2 * width
        return lax.dynamic_slice_in_dim(array, at, width, 1)
    return call(
        slice_kernel,
        place,
        (4,),
        [pl.BlockSpec((rows // 4, width), lambda i, place: (i, (place[TP] + side) % 2))],
        pl.BlockSpec((rows // 4, width), lambda i, place: (i, 0)),
        shape_of((rows, width), BF16),
        (array,),
        (0, 4 * rows * width),
    )


def add_kernel(place, left, right, out):
    out[...] = left[...] + right[...]


def add_rows(place, left, right, at, rows):
    width = left.shape[1]
    spec = pl.BlockSpec((rows, width), lambda i, place: (at // rows, 0))
    return call(
        add_kernel,
        place,
        (1,),
        [spec, spec],
        pl.BlockSpec((rows, width), lambda i, place: (0, 0)),
        shape_of((rows, width), F32),
        (left, right),
        (rows * width, 12 * rows * width),
    )


def on_device(
    hidden_cont,
    hidden_prompt,
    norm_gain,
    query_weight,
    keyval_weight,
    out_weight,
    query_gain,
    key_gain,
    sample_lengths,
):
    size = query_gain.shape[0]
    heads_here = query_weight.shape[1] // size
    cont_rows = hidden_cont.shape[0]
    prompt_rows = hidden_prompt.shape[0]
    sp_index = lax.axis_index("sp")
    sp_count = lax.axis_size("sp")
    tp_index = lax.axis_index("tp")
    assert lax.axis_size("tp") == sp_count and lax.axis_size("groups") == 2
    place = jnp.stack(
        [
            sp_index,
            tp_index,
            lax.axis_index("groups"),
            tp_index * heads_here // (QH // KVH),
        ]
    ).astype(jnp.int32)
    norm_gain = norm_gain[None, :]
    query_gain = query_gain[None, :]
    key_gain = key_gain[None, :]

    half, both = pick_columns(place, keyval_weight, size)
    halves = other_halves(half, "sp", sp_count)
    block, cont = norm_split(after(place, half), hidden_cont, norm_gain, sp_count)
    other = swap(block, "sp", 1)
    packed = pack(place, cont, other)
    got = [swap(block, "sp", 2 * d) for d, block in enumerate(packed, 1)]
    partner = swap(both, "sp", 1)
    halves = after(halves, packed)
    others = {d: swap(half, "groups", 1) for d, half in halves.items()}
    halves = both_cores(halves, "sp")
    sent = column_half(place, after(out_weight, halves), True)
    out_partner = swap(sent, "tp", 1)
    prompt, near_pair = near_keyval(
        place, hidden_prompt, norm_gain, cont, both, after(partner, halves)
    )
    cosine, sine = tables(
        place, sample_lengths, prompt_rows, prompt_rows * sp_count, cont_rows, size
    )
    got = after(got, near_pair, others, sent, cosine)
    others = both_cores(others, "sp")

    keep, send = query_parts(place, cont, [other] + got, query_weight)
    mine, near, far = sum_blocks(place, keep, send, "sp", sp_count)
    weights = [held[d] for d in range(2, sp_count) for held in (halves, others)]
    pair = keyval_rows(place, prompt, cont, cosine, sine, key_gain, near_pair, weights)
    pairs = gather_blocks(pair, "sp", sp_count)
    heads = attend(
        place,
        sample_lengths,
        mine,
        near,
        far,
        cosine,
        sine,
        query_gain,
        pairs,
        prompt_rows,
    )
    chips = range(0, sp_count, 2)
    near_heads = {d: swap(heads, "sp", d) if d else heads for d in chips}
    far_heads = {d: swap_both(heads, 1, d, sp_count) for d in chips}
    near_heads = both_cores(near_heads, "sp")
    far_heads = both_cores(far_heads, "sp")
    all_heads = [held[d] for held in (near_heads, far_heads) for d in range(sp_count)]
    parts = out_parts(place, all_heads, out_weight, out_partner)
    parts = [
        lax.ppermute(
            part,
            ("tp", "sp"),
            [
                (t * sp_count + s, s * sp_count + (t ^ e))
                for t in range(sp_count)
                for s in range(sp_count)
            ],
        )
        for e, part in enumerate(parts)
    ]
    return final_sum(place, parts, hidden_cont)


def solution(mesh):
    placed = (
        P(("groups", "sp"), None),
        P(("groups", "sp"), None),
        P(),
        P("sp", "tp"),
        P("sp", None),
        P("tp", "sp"),
        P(),
        P(),
        P("groups"),
    )
    return jax.shard_map(
        on_device, mesh=mesh, in_specs=placed, out_specs=P(("groups", "sp"), "tp"), check_vma=False
    )
```

```python
import functools
import math

import jax
import jax.numpy as jnp
from jax import lax
from jax.experimental import pallas as pl
from jax.experimental.pallas import tpu as pltpu
from jax.sharding import PartitionSpec as P

QH = 32
KVH = 4
SP, TP, GROUP, HEAD = range(4)
BF16 = jnp.bfloat16
F32 = jnp.float32
ROOM = 14 * 1024 * 1024


def call(kernel, place, grid, in_specs, out_specs, out_shape, args, cost, scratch=(), room=ROOM):
    flops, moved = cost
    return pl.pallas_call(
        kernel,
        out_shape=out_shape,
        grid_spec=pltpu.PrefetchScalarGridSpec(
            num_scalar_prefetch=1,
            grid=grid,
            in_specs=in_specs,
            out_specs=out_specs,
            scratch_shapes=scratch,
        ),
        compiler_params=pltpu.CompilerParams(vmem_limit_bytes=room),
        cost_estimate=pl.CostEstimate(flops=flops, bytes_accessed=moved, transcendentals=0),
    )(place, *args)


def whole(array):
    zeros = (0,) * array.ndim
    return pl.BlockSpec(array.shape, lambda i, place: zeros)


def shape_of(shape, dtype):
    return jax.ShapeDtypeStruct(shape, dtype)


def rms_rows(values, gain):
    return values * lax.rsqrt(jnp.mean(values * values, axis=-1, keepdims=True) + 1e-06) * gain


def split_normed(hidden, gain, out):
    count, _, depth = out.shape
    normed = rms_rows(hidden[...].astype(F32), gain[...]).astype(BF16)
    for j in range(count):
        out[j] = normed[:, j * depth : (j + 1) * depth]


def norm_kernel(place, hidden, gain, out, split):
    split_normed(hidden, gain, split)
    for d in range(out.shape[0]):
        out[d] = split[place[SP] ^ 1 ^ 2 * d]


def norm_split(place, hidden, gain, count):
    rows, width = hidden.shape
    step = rows if rows % 32 else 32
    depth = width // count
    return call(
        norm_kernel,
        place,
        (rows // step,),
        [pl.BlockSpec((step, width), lambda i, place: (i, 0)), whole(gain)],
        [
            pl.BlockSpec((n, step, depth), lambda i, place: (0, i, 0))
            for n in (count // 2, count)
        ],
        [shape_of((n, rows, depth), BF16) for n in (count // 2, count)],
        (hidden, gain),
        (4 * rows * width, 4 * rows * width),
    )


def pack_kernel(place, cont, other, *outs):
    for d, out in enumerate(outs, 1):
        out[0] = cont[place[SP] ^ 2 * d]
        out[1] = other[d]


def pack(place, cont, other):
    count, rows, depth = cont.shape
    block = (2, rows, depth)
    sent = count // 2 - 1
    return call(
        pack_kernel,
        place,
        (1,),
        [whole(cont), whole(other)],
        [pl.BlockSpec(block, lambda i, place: (0, 0, 0))] * sent,
        [shape_of(block, BF16)] * sent,
        (cont, other),
        (0, 8 * sent * rows * depth),
    )


def pick_kernel(place, first, key, value, half, both):
    size = half.shape[1]
    half[...] = first[...]
    both[:, :size] = key[...]
    both[:, size:] = value[...]


def pick_columns(place, weight, size):
    depth = weight.shape[0]
    block = (depth, size)
    outs = [shape_of(block, BF16), shape_of((depth, 2 * size), BF16)]
    return call(
        pick_kernel,
        place,
        (1,),
        [
            pl.BlockSpec(block, lambda i, place: (0, 2 * place[HEAD] + place[GROUP])),
            pl.BlockSpec(block, lambda i, place: (0, 2 * place[HEAD])),
            pl.BlockSpec(block, lambda i, place: (0, 2 * place[HEAD] + 1)),
        ],
        [whole(out) for out in outs],
        outs,
        (weight, weight, weight),
        (0, 12 * depth * size),
    )


def query_kernel(count, place, *refs):
    cont, other, chips, (weight, keep, send) = refs[0], refs[1], refs[2:-3], refs[-3:]
    block = cont.shape[1]
    rows = [cont[place[SP]], other[0]]
    for chip in chips:
        rows += [chip[0], chip[1]]
    part = jnp.dot(jnp.concatenate(rows, axis=0), weight[...], preferred_element_type=F32)
    for d in range(count):
        at = d // 2 * block
        (keep, send)[d % 2][at : at + block, :] = part[d * block : (d + 1) * block]


def query_parts(place, cont, got, weight):
    count, block, depth = cont.shape
    width = weight.shape[1]
    step = min(width, 256)
    half = count // 2 * block
    return call(
        functools.partial(query_kernel, count),
        place,
        (width // step,),
        [whole(a) for a in (cont, *got)]
        + [pl.BlockSpec((depth, step), lambda i, place: (0, i))],
        [pl.BlockSpec((half, step), lambda i, place: (0, i))] * 2,
        [shape_of((half, width), F32)] * 2,
        (cont, *got, weight),
        (2 * count * block * depth * width, 2 * depth * width),
    )


def turn(values, cosine, sine):
    return values * cosine + pltpu.roll(values, values.shape[-1] // 2, 1) * sine


def near_kernel(place, hidden, norm_gain, cont, own, partner, prompt, out):
    split_normed(hidden, norm_gain, prompt)
    total = 0.0
    for d, weight in ((0, own), (1, partner)):
        left = jnp.concatenate([prompt[place[SP] ^ d], cont[place[SP] ^ d]], axis=0)
        total = total + jnp.dot(left, weight[...], preferred_element_type=F32)
    out[...] = total


def near_keyval(place, hidden, norm_gain, cont, own, partner):
    args = (hidden, norm_gain, cont, own, partner)
    count, cont_rows, depth = cont.shape
    prompt_rows = hidden.shape[0]
    rows = prompt_rows + cont_rows
    width = own.shape[1]
    outs = [shape_of((count, prompt_rows, depth), BF16), shape_of((rows, width), F32)]
    return call(
        near_kernel,
        place,
        (1,),
        [whole(a) for a in args],
        [whole(out) for out in outs],
        outs,
        args,
        (4 * rows * depth * width, 4 * depth * (rows * count + width)),
    )


def keyval_kernel(count, place, prompt, cont, cosine, sine, gain, near, *refs):
    weights, out = refs[:-1], refs[-1]
    size = gain.shape[1]
    total = 0.0
    for d in range(2, count):
        left = jnp.concatenate([prompt[place[SP] ^ d], cont[place[SP] ^ d]], axis=0)
        weight = jnp.concatenate([weights[2 * d - 4][...], weights[2 * d - 3][...]], axis=1)
        total = total + jnp.dot(left, weight, preferred_element_type=F32)
    swapped = place[GROUP] == 1
    first, second = total[:, :size], total[:, size:]
    key = near[:, :size] + jnp.where(swapped, second, first)
    value = near[:, size:] + jnp.where(swapped, first, second)
    out[:, :size] = turn(rms_rows(key, gain[...]), cosine[...], sine[...]).astype(BF16)
    out[:, size:] = value.astype(BF16)


def keyval_rows(place, prompt, cont, cosine, sine, gain, near, weights):
    count, prompt_rows, depth = prompt.shape
    rows = prompt_rows + cont.shape[1]
    size = gain.shape[1]
    args = (prompt, cont, cosine, sine, gain, near, *weights)
    out = shape_of((rows, 2 * size), BF16)
    return call(
        functools.partial(keyval_kernel, count),
        place,
        (1,),
        [whole(a) for a in args],
        whole(out),
        out,
        args,
        (2 * rows * count * depth * size, count * depth * (rows + 2 * size)),
    )


def starts_of(lengths, index):
    start = jnp.zeros(index.shape, jnp.int32)
    total = jnp.int32(0)
    for c in range(lengths.shape[0]):
        start = jnp.where(index >= total, total, start)
        total = total + lengths[c]
    return start


def attend_kernel(count, prompt_rows, place, lengths, mine, near, cosine, sine, gain, *refs):
    pairs, far, out = refs[:count], refs[count:-1], refs[-1]
    rows, width = out.shape
    size = gain.shape[1]
    heads = width // size
    cosine, sine = cosine[prompt_rows:, :], sine[prompt_rows:, :]
    queries = []
    for h in range(heads):
        part = slice(h * size, (h + 1) * size)
        value = mine[:rows, part] + near[:rows, part]
        for block in far:
            value = value + block[:, part].astype(F32)
        value = rms_rows(value, gain[...])
        queries.append(turn(value, cosine, sine).astype(BF16))
    queries = jnp.concatenate(queries, axis=0)
    prompt = jnp.concatenate([pair[:prompt_rows] for pair in pairs], axis=0)
    cont = jnp.concatenate([pair[prompt_rows:] for pair in pairs], axis=0)
    scale = 1.0 / math.sqrt(size)
    by_rows = (((1,), (1,)), ((), ()))
    to_prompt = (
        lax.dot_general(queries, prompt[:, :size], by_rows, preferred_element_type=F32) * scale
    )
    to_cont = (
        lax.dot_general(queries, cont[:, :size], by_rows, preferred_element_type=F32) * scale
    )
    shape = (rows, cont.shape[0])
    own = place[SP] * rows + lax.broadcasted_iota(jnp.int32, shape, 0)
    at = lax.broadcasted_iota(jnp.int32, shape, 1)
    key = jnp.zeros(shape, jnp.int32)
    for d in range(count):
        inside = (at >= d * rows) & (at < (d + 1) * rows)
        key = jnp.where(inside, (place[SP] ^ d) * rows + at - d * rows, key)
    allowed = jnp.where((key >= starts_of(lengths, own)) & (key <= own), 0.0, -1e30)
    to_cont = to_cont + jnp.concatenate([allowed] * heads, axis=0)
    peak = jnp.maximum(
        jnp.max(to_prompt, axis=1, keepdims=True), jnp.max(to_cont, axis=1, keepdims=True)
    )
    to_prompt = jnp.exp(to_prompt - peak)
    to_cont = jnp.exp(to_cont - peak)
    divisor = jnp.sum(to_prompt, axis=1, keepdims=True) + jnp.sum(to_cont, axis=1, keepdims=True)
    result = jnp.dot(
        (to_prompt / divisor).astype(BF16), prompt[:, size:], preferred_element_type=F32
    ) + jnp.dot((to_cont / divisor).astype(BF16), cont[:, size:], preferred_element_type=F32)
    for h in range(heads):
        out[:, h * size : (h + 1) * size] = result[h * rows : (h + 1) * rows].astype(BF16)


def attend(place, lengths, mine, near, far, cosine, sine, gain, pairs, prompt_rows):
    rows, width = far[0].shape
    args = (mine, near, cosine, sine, gain, *pairs, *far)
    out = shape_of((rows, width), BF16)
    keys = len(pairs) * pairs[0].shape[0]
    return call(
        functools.partial(attend_kernel, len(pairs), prompt_rows),
        place,
        (1,),
        [pl.BlockSpec(memory_space=pltpu.SMEM)] + [whole(a) for a in args],
        whole(out),
        out,
        (lengths, *args),
        (4 * rows * width * keys, 10 * rows * width + 512 * keys),
    )


def out_kernel(count, place, *refs):
    heads, weights, outs, part = refs[: 2 * count], refs[-count - 3 : -count - 1], refs[-count - 1 : -1], refs[-1]
    rows = heads[0].shape[0]
    total = 0.0
    for side, weight in enumerate(weights):
        left = jnp.concatenate([h[...] for h in heads[side * count : (side + 1) * count]], axis=0)
        share = jnp.dot(left, weight[...], preferred_element_type=F32)
        total = total + share.astype(BF16).astype(F32)
    total = total.astype(BF16)
    for d in range(count):
        part[d] = total[d * rows : (d + 1) * rows]
    for e in range(count):
        outs[e][...] = part[place[TP] ^ e ^ place[SP]]


def out_parts(place, heads, own, partner):
    count = len(heads) // 2
    rows = heads[0].shape[0]
    depth, width = partner.shape
    if width % 128:
        own = column_half(place, own, False)
        half = whole(own)
    else:
        half = pl.BlockSpec((depth, width), lambda i, place: (0, place[TP] % 2))
    args = (*heads, own, partner)
    return call(
        functools.partial(out_kernel, count),
        place,
        (1,),
        [whole(h) for h in heads] + [half, whole(partner)],
        [pl.BlockSpec((rows, width), lambda i, place: (0, 0))] * count,
        [shape_of((rows, width), BF16)] * count,
        args,
        (4 * count * rows * depth * width, 4 * depth * width),
        [pltpu.VMEM((count, rows, width), BF16)],
    )


def final_kernel(count, place, hidden, *refs):
    parts, out = refs[:-1], refs[-1]
    width = parts[0].shape[1]
    sums = [0.0, 0.0]
    for e, part in enumerate(parts):
        sums[e % 2] = sums[e % 2] + part[...].astype(F32)
    odd = place[SP] % 2 == 1
    left = jnp.where(odd, sums[1], sums[0])
    right = jnp.where(odd, sums[0], sums[1])
    out[:, :width] = (hidden[:, :width].astype(F32) + left).astype(BF16)
    out[:, width:] = (hidden[:, width:].astype(F32) + right).astype(BF16)


def final_sum(place, parts, hidden):
    rows, width = parts[0].shape
    width *= 2
    count = len(parts)
    if width % 128:
        hidden = lax.dynamic_slice_in_dim(hidden, place[TP] * width, width, 1)
        residual = whole(hidden)
    else:
        residual = pl.BlockSpec((rows, width), lambda i, place: (0, place[TP]))
    return call(
        functools.partial(final_kernel, count),
        place,
        (1,),
        [residual] + [whole(a) for a in parts],
        pl.BlockSpec((rows, width), lambda i, place: (0, 0)),
        shape_of((rows, width), BF16),
        (hidden, *parts),
        (count * rows * width, 12 * rows * width),
    )


def after(arrays, *others):
    return lax.optimization_barrier((arrays, others))[0]


def swap(array, axis, bits):
    return lax.ppermute(array, axis, [(i, i ^ bits) for i in range(lax.axis_size(axis))])


def swap_both(array, tp_bits, sp_bits, count):
    pairs = [
        (t * count + s, (t ^ tp_bits) * count + (s ^ sp_bits))
        for t in range(count)
        for s in range(count)
    ]
    return lax.ppermute(array, ("tp", "sp"), pairs)


def swap_bits(count):
    bits = []
    bit = 1
    while bit < count:
        bits.append(bit)
        bit *= 2
    return bits


def gather_blocks(block, axis, count):
    held = {0: block}
    bits = swap_bits(count)
    for bit in bits[1:] + bits[:1]:
        held.update({d ^ bit: swap(held[d], axis, bit) for d in sorted(held)})
    return [held[d] for d in range(count)]


def other_halves(half, axis, count):
    firsts = {0: half}
    for bit in swap_bits(count)[1:]:
        firsts.update({d ^ bit: swap(firsts[d], axis, bit) for d in sorted(firsts)})
    del firsts[0]
    return firsts


def both_cores(held, axis):
    return {**held, **{d ^ 1: swap(held[d], axis, 1) for d in sorted(held)}}


def sum_blocks(place, keep, send, axis, count):
    near = swap(send, axis, 1)
    rows = keep.shape[0] // (count // 2)
    held = {d: add_rows(place, keep, near, d // 2 * rows, rows) for d in range(2, count, 2)}
    far = []
    for bit in swap_bits(count)[1:]:
        sent = [d for d in sorted(held) if d & bit]
        got = {d ^ bit: swap(held[d], axis, bit) for d in sent}
        far.append(got.pop(0))
        held = {d: (held[d].astype(F32) + got[d].astype(F32)).astype(BF16) for d in got}
    return keep, near, far


def table_kernel(prompt_rows, prompt_total, place, lengths, cosine, sine):
    rows, size = cosine.shape
    shape = cosine.shape
    row = lax.broadcasted_iota(jnp.int32, shape, 0)
    lane = lax.broadcasted_iota(jnp.int32, shape, 1)
    index = place[SP] * (rows - prompt_rows) + row - prompt_rows
    position = jnp.where(
        row < prompt_rows,
        place[SP] * prompt_rows + row,
        prompt_total + index - starts_of(lengths, index),
    )
    half = size // 2
    step = jnp.where(lane < half, lane, lane - half).astype(F32)
    angle = position.astype(F32) * jnp.exp(step * (-2.0 * math.log(1000000.0) / size))
    cosine[...] = jnp.cos(angle)
    angle = jnp.sin(angle)
    sine[...] = jnp.where(lane < half, -angle, angle)


def tables(place, lengths, prompt_rows, prompt_total, cont_rows, size):
    out = shape_of((prompt_rows + cont_rows, size), F32)
    return call(
        functools.partial(table_kernel, prompt_rows, prompt_total),
        place,
        (1,),
        [pl.BlockSpec(memory_space=pltpu.SMEM)],
        [whole(out)] * 2,
        [out] * 2,
        (lengths,),
        (100 * out.size, 8 * out.size),
    )


def slice_kernel(place, array, out):
    out[...] = array[...]


def column_half(place, array, other):
    rows, width = array.shape
    width //= 2
    side = 1 if other else 0
    if width % 128:
        at = (place[TP] + side) % 2 * width
        return lax.dynamic_slice_in_dim(array, at, width, 1)
    return call(
        slice_kernel,
        place,
        (4,),
        [pl.BlockSpec((rows // 4, width), lambda i, place: (i, (place[TP] + side) % 2))],
        pl.BlockSpec((rows // 4, width), lambda i, place: (i, 0)),
        shape_of((rows, width), BF16),
        (array,),
        (0, 4 * rows * width),
    )


def add_kernel(place, left, right, out):
    out[...] = (left[...] + right[...]).astype(BF16)


def add_rows(place, left, right, at, rows):
    width = left.shape[1]
    spec = pl.BlockSpec((rows, width), lambda i, place: (at // rows, 0))
    return call(
        add_kernel,
        place,
        (1,),
        [spec, spec],
        pl.BlockSpec((rows, width), lambda i, place: (0, 0)),
        shape_of((rows, width), BF16),
        (left, right),
        (rows * width, 10 * rows * width),
    )


def on_device(
    hidden_cont,
    hidden_prompt,
    norm_gain,
    query_weight,
    keyval_weight,
    out_weight,
    query_gain,
    key_gain,
    sample_lengths,
):
    size = query_gain.shape[0]
    heads_here = query_weight.shape[1] // size
    cont_rows = hidden_cont.shape[0]
    prompt_rows = hidden_prompt.shape[0]
    sp_index = lax.axis_index("sp")
    sp_count = lax.axis_size("sp")
    tp_index = lax.axis_index("tp")
    assert lax.axis_size("tp") == sp_count and lax.axis_size("groups") == 2
    place = jnp.stack(
        [
            sp_index,
            tp_index,
            lax.axis_index("groups"),
            tp_index * heads_here // (QH // KVH),
        ]
    ).astype(jnp.int32)
    norm_gain = norm_gain[None, :]
    query_gain = query_gain[None, :]
    key_gain = key_gain[None, :]

    half, both = pick_columns(place, keyval_weight, size)
    halves = other_halves(half, "sp", sp_count)
    block, cont = norm_split(after(place, half), hidden_cont, norm_gain, sp_count)
    other = swap(block, "sp", 1)
    packed = pack(place, cont, other)
    got = [swap(block, "sp", 2 * d) for d, block in enumerate(packed, 1)]
    partner = swap(both, "sp", 1)
    halves = after(halves, packed)
    others = {d: swap(half, "groups", 1) for d, half in halves.items()}
    halves = both_cores(halves, "sp")
    sent = column_half(place, after(out_weight, halves), True)
    out_partner = swap(sent, "tp", 1)
    prompt, near_pair = near_keyval(
        place, hidden_prompt, norm_gain, cont, both, after(partner, halves)
    )
    cosine, sine = tables(
        place, sample_lengths, prompt_rows, prompt_rows * sp_count, cont_rows, size
    )
    got = after(got, near_pair, others, sent, cosine)
    others = both_cores(others, "sp")

    keep, send = query_parts(place, cont, [other] + got, query_weight)
    mine, near, far = sum_blocks(place, keep, send, "sp", sp_count)
    weights = [held[d] for d in range(2, sp_count) for held in (halves, others)]
    pair = keyval_rows(place, prompt, cont, cosine, sine, key_gain, near_pair, weights)
    pairs = gather_blocks(pair, "sp", sp_count)
    heads = attend(
        place,
        sample_lengths,
        mine,
        near,
        far,
        cosine,
        sine,
        query_gain,
        pairs,
        prompt_rows,
    )
    chips = range(0, sp_count, 2)
    near_heads = {d: swap(heads, "sp", d) if d else heads for d in chips}
    far_heads = {d: swap_both(heads, 1, d, sp_count) for d in chips}
    near_heads = both_cores(near_heads, "sp")
    far_heads = both_cores(far_heads, "sp")
    all_heads = [held[d] for held in (near_heads, far_heads) for d in range(sp_count)]
    parts = out_parts(place, all_heads, out_weight, out_partner)
    parts = [
        lax.ppermute(
            part,
            ("tp", "sp"),
            [
                (t * sp_count + s, s * sp_count + (t ^ e))
                for t in range(sp_count)
                for s in range(sp_count)
            ],
        )
        for e, part in enumerate(parts)
    ]
    return final_sum(place, parts, hidden_cont)


def solution(mesh):
    placed = (
        P(("groups", "sp"), None),
        P(("groups", "sp"), None),
        P(),
        P("sp", "tp"),
        P("sp", None),
        P("tp", "sp"),
        P(),
        P(),
        P("groups"),
    )
    return jax.shard_map(
        on_device, mesh=mesh, in_specs=placed, out_specs=P(("groups", "sp"), "tp"), check_vma=False
    )
```

```python
import functools
import math

import jax
import jax.numpy as jnp
from jax import lax
from jax.experimental import pallas as pl
from jax.experimental.pallas import tpu as pltpu
from jax.sharding import PartitionSpec as P

QH = 32
KVH = 4
SP, TP, GROUP, HEAD = range(4)
BF16 = jnp.bfloat16
F32 = jnp.float32
ROOM = 14 * 1024 * 1024


def call(kernel, place, grid, in_specs, out_specs, out_shape, args, cost, scratch=(), room=ROOM):
    flops, moved = cost
    return pl.pallas_call(
        kernel,
        out_shape=out_shape,
        grid_spec=pltpu.PrefetchScalarGridSpec(
            num_scalar_prefetch=1,
            grid=grid,
            in_specs=in_specs,
            out_specs=out_specs,
            scratch_shapes=scratch,
        ),
        compiler_params=pltpu.CompilerParams(vmem_limit_bytes=room),
        cost_estimate=pl.CostEstimate(flops=flops, bytes_accessed=moved, transcendentals=0),
    )(place, *args)


def whole(array):
    zeros = (0,) * array.ndim
    return pl.BlockSpec(array.shape, lambda i, place: zeros)


def shape_of(shape, dtype):
    return jax.ShapeDtypeStruct(shape, dtype)


def rms_rows(values, gain):
    return values * lax.rsqrt(jnp.mean(values * values, axis=-1, keepdims=True) + 1e-06) * gain


def split_normed(hidden, gain, out):
    count, _, depth = out.shape
    normed = rms_rows(hidden[...].astype(F32), gain[...]).astype(BF16)
    for j in range(count):
        out[j] = normed[:, j * depth : (j + 1) * depth]


def pack_kernel(place, cont, other, *outs):
    for d, out in enumerate(outs, 1):
        out[0] = cont[place[SP] ^ 2 * d]
        out[1] = other[d]


def pack(place, cont, other):
    count, rows, depth = cont.shape
    block = (2, rows, depth)
    sent = count // 2 - 1
    return call(
        pack_kernel,
        place,
        (1,),
        [whole(cont), whole(other)],
        [pl.BlockSpec(block, lambda i, place: (0, 0, 0))] * sent,
        [shape_of(block, BF16)] * sent,
        (cont, other),
        (0, 8 * sent * rows * depth),
    )


def first_kernel(place, first, key, value, hidden, gain, half, both, out, split):
    size = half.shape[1]
    half[...] = first[...]
    both[:, :size] = key[...]
    both[:, size:] = value[...]
    split_normed(hidden, gain, split)
    for d in range(out.shape[0]):
        out[d] = split[place[SP] ^ 1 ^ 2 * d]


def first_step(place, weight, hidden, gain, size, count):
    depth = weight.shape[0]
    rows = hidden.shape[0]
    block = (depth, size)
    outs = [shape_of(block, BF16), shape_of((depth, 2 * size), BF16)]
    outs += [shape_of((n, rows, depth), BF16) for n in (count // 2, count)]
    return call(
        first_kernel,
        place,
        (1,),
        [
            pl.BlockSpec(block, lambda i, place: (0, 2 * place[HEAD] + place[GROUP])),
            pl.BlockSpec(block, lambda i, place: (0, 2 * place[HEAD])),
            pl.BlockSpec(block, lambda i, place: (0, 2 * place[HEAD] + 1)),
            whole(hidden),
            whole(gain),
        ],
        [whole(out) for out in outs],
        outs,
        (weight, weight, weight, hidden, gain),
        (4 * rows * depth * count, 12 * depth * size + 6 * rows * depth * count),
    )


def query_kernel(count, place, *refs):
    cont, other, chips, (weight, keep, send) = refs[0], refs[1], refs[2:-3], refs[-3:]
    block = cont.shape[1]
    rows = [cont[place[SP]], other[0]]
    for chip in chips:
        rows += [chip[0], chip[1]]
    part = jnp.dot(jnp.concatenate(rows, axis=0), weight[...], preferred_element_type=F32)
    for d in range(count):
        at = d // 2 * block
        (keep, send)[d % 2][at : at + block, :] = part[d * block : (d + 1) * block]


def query_parts(place, cont, got, weight):
    count, block, depth = cont.shape
    width = weight.shape[1]
    step = min(width, 256)
    half = count // 2 * block
    return call(
        functools.partial(query_kernel, count),
        place,
        (width // step,),
        [whole(a) for a in (cont, *got)]
        + [pl.BlockSpec((depth, step), lambda i, place: (0, i))],
        [pl.BlockSpec((half, step), lambda i, place: (0, i))] * 2,
        [shape_of((half, width), F32)] * 2,
        (cont, *got, weight),
        (2 * count * block * depth * width, 2 * depth * width),
    )


def turn(values, cosine, sine):
    return values * cosine + pltpu.roll(values, values.shape[-1] // 2, 1) * sine


def near_kernel(place, hidden, norm_gain, cont, own, partner, prompt, out):
    split_normed(hidden, norm_gain, prompt)
    total = 0.0
    for d, weight in ((0, own), (1, partner)):
        left = jnp.concatenate([prompt[place[SP] ^ d], cont[place[SP] ^ d]], axis=0)
        total = total + jnp.dot(left, weight[...], preferred_element_type=F32)
    out[...] = total


def near_keyval(place, hidden, norm_gain, cont, own, partner):
    args = (hidden, norm_gain, cont, own, partner)
    count, cont_rows, depth = cont.shape
    prompt_rows = hidden.shape[0]
    rows = prompt_rows + cont_rows
    width = own.shape[1]
    outs = [shape_of((count, prompt_rows, depth), BF16), shape_of((rows, width), F32)]
    return call(
        near_kernel,
        place,
        (1,),
        [whole(a) for a in args],
        [whole(out) for out in outs],
        outs,
        args,
        (4 * rows * depth * width, 4 * depth * (rows * count + width)),
    )


def keyval_kernel(count, place, prompt, cont, cosine, sine, gain, near, *refs):
    weights, out = refs[:-1], refs[-1]
    size = gain.shape[1]
    total = 0.0
    for d in range(2, count):
        left = jnp.concatenate([prompt[place[SP] ^ d], cont[place[SP] ^ d]], axis=0)
        weight = jnp.concatenate([weights[2 * d - 4][...], weights[2 * d - 3][...]], axis=1)
        total = total + jnp.dot(left, weight, preferred_element_type=F32)
    swapped = place[GROUP] == 1
    first, second = total[:, :size], total[:, size:]
    key = near[:, :size] + jnp.where(swapped, second, first)
    value = near[:, size:] + jnp.where(swapped, first, second)
    out[:, :size] = turn(rms_rows(key, gain[...]), cosine[...], sine[...]).astype(BF16)
    out[:, size:] = value.astype(BF16)


def keyval_rows(place, prompt, cont, cosine, sine, gain, near, weights):
    count, prompt_rows, depth = prompt.shape
    rows = prompt_rows + cont.shape[1]
    size = gain.shape[1]
    args = (prompt, cont, cosine, sine, gain, near, *weights)
    out = shape_of((rows, 2 * size), BF16)
    return call(
        functools.partial(keyval_kernel, count),
        place,
        (1,),
        [whole(a) for a in args],
        whole(out),
        out,
        args,
        (2 * rows * count * depth * size, count * depth * (rows + 2 * size)),
    )


def starts_of(lengths, index):
    start = jnp.zeros(index.shape, jnp.int32)
    total = jnp.int32(0)
    for c in range(lengths.shape[0]):
        start = jnp.where(index >= total, total, start)
        total = total + lengths[c]
    return start


def attend_kernel(count, prompt_rows, place, lengths, mine, near, far, cosine, sine, gain, *refs):
    pairs, out = refs[:-1], refs[-1]
    rows, width = far.shape
    size = gain.shape[1]
    heads = width // size
    cosine, sine = cosine[prompt_rows:, :], sine[prompt_rows:, :]
    queries = []
    for h in range(heads):
        part = slice(h * size, (h + 1) * size)
        value = rms_rows(mine[:rows, part] + near[:rows, part] + far[:, part], gain[...])
        queries.append(turn(value, cosine, sine).astype(BF16))
    queries = jnp.concatenate(queries, axis=0)
    prompt = jnp.concatenate([pair[:prompt_rows] for pair in pairs], axis=0)
    cont = jnp.concatenate([pair[prompt_rows:] for pair in pairs], axis=0)
    scale = 1.0 / math.sqrt(size)
    by_rows = (((1,), (1,)), ((), ()))
    to_prompt = (
        lax.dot_general(queries, prompt[:, :size], by_rows, preferred_element_type=F32) * scale
    )
    to_cont = (
        lax.dot_general(queries, cont[:, :size], by_rows, preferred_element_type=F32) * scale
    )
    shape = (rows, cont.shape[0])
    own = place[SP] * rows + lax.broadcasted_iota(jnp.int32, shape, 0)
    at = lax.broadcasted_iota(jnp.int32, shape, 1)
    key = jnp.zeros(shape, jnp.int32)
    for d in range(count):
        inside = (at >= d * rows) & (at < (d + 1) * rows)
        key = jnp.where(inside, (place[SP] ^ d) * rows + at - d * rows, key)
    allowed = jnp.where((key >= starts_of(lengths, own)) & (key <= own), 0.0, -1e30)
    to_cont = to_cont + jnp.concatenate([allowed] * heads, axis=0)
    peak = jnp.maximum(
        jnp.max(to_prompt, axis=1, keepdims=True), jnp.max(to_cont, axis=1, keepdims=True)
    )
    to_prompt = jnp.exp(to_prompt - peak)
    to_cont = jnp.exp(to_cont - peak)
    factor = 1.0 / (
        jnp.sum(to_prompt, axis=1, keepdims=True) + jnp.sum(to_cont, axis=1, keepdims=True)
    )
    result = jnp.dot(
        (to_prompt * factor).astype(BF16), prompt[:, size:], preferred_element_type=F32
    ) + jnp.dot((to_cont * factor).astype(BF16), cont[:, size:], preferred_element_type=F32)
    for h in range(heads):
        out[:, h * size : (h + 1) * size] = result[h * rows : (h + 1) * rows].astype(BF16)


def attend(place, lengths, mine, near, far, cosine, sine, gain, pairs, prompt_rows):
    rows, width = far.shape
    args = (mine, near, far, cosine, sine, gain, *pairs)
    out = shape_of((rows, width), BF16)
    keys = len(pairs) * pairs[0].shape[0]
    return call(
        functools.partial(attend_kernel, len(pairs), prompt_rows),
        place,
        (1,),
        [pl.BlockSpec(memory_space=pltpu.SMEM)] + [whole(a) for a in args],
        whole(out),
        out,
        (lengths, *args),
        (4 * rows * width * keys, 10 * rows * width + 512 * keys),
    )


def out_kernel(count, place, *refs):
    heads, weights, outs, part = refs[: 2 * count], refs[-count - 3 : -count - 1], refs[-count - 1 : -1], refs[-1]
    rows = heads[0].shape[0]
    total = 0.0
    for side, weight in enumerate(weights):
        left = jnp.concatenate([h[...] for h in heads[side * count : (side + 1) * count]], axis=0)
        share = jnp.dot(left, weight[...], preferred_element_type=F32)
        total = total + share.astype(BF16).astype(F32)
    total = total.astype(BF16)
    for d in range(count):
        part[d] = total[d * rows : (d + 1) * rows]
    for e in range(count):
        outs[e][...] = part[place[TP] ^ e ^ place[SP]]


def out_parts(place, heads, own, partner):
    count = len(heads) // 2
    rows = heads[0].shape[0]
    depth, width = partner.shape
    if width % 128:
        own = column_half(place, own, False)
        half = whole(own)
    else:
        half = pl.BlockSpec((depth, width), lambda i, place: (0, place[TP] % 2))
    args = (*heads, own, partner)
    return call(
        functools.partial(out_kernel, count),
        place,
        (1,),
        [whole(h) for h in heads] + [half, whole(partner)],
        [pl.BlockSpec((rows, width), lambda i, place: (0, 0))] * count,
        [shape_of((rows, width), BF16)] * count,
        args,
        (4 * count * rows * depth * width, 4 * depth * width),
        [pltpu.VMEM((count, rows, width), BF16)],
    )


def final_kernel(count, place, hidden, *refs):
    parts, out = refs[:-1], refs[-1]
    width = parts[0].shape[1]
    sums = [0.0, 0.0]
    for e, part in enumerate(parts):
        sums[e % 2] = sums[e % 2] + part[...].astype(F32)
    odd = place[SP] % 2 == 1
    left = jnp.where(odd, sums[1], sums[0])
    right = jnp.where(odd, sums[0], sums[1])
    out[:, :width] = (hidden[:, :width].astype(F32) + left).astype(BF16)
    out[:, width:] = (hidden[:, width:].astype(F32) + right).astype(BF16)


def final_sum(place, parts, hidden):
    rows, width = hidden.shape
    count = len(parts)
    return call(
        functools.partial(final_kernel, count),
        place,
        (1,),
        [whole(a) for a in (hidden, *parts)],
        whole(hidden),
        shape_of((rows, width), BF16),
        (hidden, *parts),
        (count * rows * width, 12 * rows * width),
    )


def after(arrays, *others):
    return lax.optimization_barrier((arrays, others))[0]


def swap(array, axis, bits):
    return lax.ppermute(array, axis, [(i, i ^ bits) for i in range(lax.axis_size(axis))])


def swap_both(array, tp_bits, sp_bits, count):
    pairs = [
        (t * count + s, (t ^ tp_bits) * count + (s ^ sp_bits))
        for t in range(count)
        for s in range(count)
    ]
    return lax.ppermute(array, ("tp", "sp"), pairs)


def swap_bits(count):
    bits = []
    bit = 1
    while bit < count:
        bits.append(bit)
        bit *= 2
    return bits


def gather_blocks(block, axis, count):
    held = {0: block}
    bits = swap_bits(count)
    for bit in bits[1:] + bits[:1]:
        held.update({d ^ bit: swap(held[d], axis, bit) for d in sorted(held)})
    return [held[d] for d in range(count)]


def other_halves(half, axis, count):
    firsts = {0: half}
    for bit in swap_bits(count)[1:]:
        firsts.update({d ^ bit: swap(firsts[d], axis, bit) for d in sorted(firsts)})
    del firsts[0]
    return firsts


def both_cores(held, axis):
    return {**held, **{d ^ 1: swap(held[d], axis, 1) for d in sorted(held)}}


def sum_blocks(place, keep, send, axis, count):
    near = swap(send, axis, 1)
    rows = keep.shape[0] // (count // 2)
    held = {d: add_rows(place, keep, near, d // 2 * rows, rows) for d in range(2, count, 2)}
    far = 0.0
    for bit in swap_bits(count)[1:]:
        sent = [d for d in sorted(held) if d & bit]
        got = {d ^ bit: swap(held[d], axis, bit) for d in sent}
        far = far + got.pop(0)
        held = {d: held[d] + got[d] for d in got}
    return keep, near, far


def table_kernel(prompt_rows, prompt_total, place, lengths, cosine, sine):
    rows, size = cosine.shape
    shape = cosine.shape
    row = lax.broadcasted_iota(jnp.int32, shape, 0)
    lane = lax.broadcasted_iota(jnp.int32, shape, 1)
    index = place[SP] * (rows - prompt_rows) + row - prompt_rows
    position = jnp.where(
        row < prompt_rows,
        place[SP] * prompt_rows + row,
        prompt_total + index - starts_of(lengths, index),
    )
    half = size // 2
    step = jnp.where(lane < half, lane, lane - half).astype(F32)
    angle = position.astype(F32) * jnp.exp(step * (-2.0 * math.log(1000000.0) / size))
    cosine[...] = jnp.cos(angle)
    angle = jnp.sin(angle)
    sine[...] = jnp.where(lane < half, -angle, angle)


def tables(place, lengths, prompt_rows, prompt_total, cont_rows, size):
    out = shape_of((prompt_rows + cont_rows, size), F32)
    return call(
        functools.partial(table_kernel, prompt_rows, prompt_total),
        place,
        (1,),
        [pl.BlockSpec(memory_space=pltpu.SMEM)],
        [whole(out)] * 2,
        [out] * 2,
        (lengths,),
        (100 * out.size, 8 * out.size),
    )


def slice_kernel(place, array, out):
    out[...] = array[...]


def column_half(place, array, other):
    rows, width = array.shape
    width //= 2
    side = 1 if other else 0
    if width % 128:
        at = (place[TP] + side) % 2 * width
        return lax.dynamic_slice_in_dim(array, at, width, 1)
    return call(
        slice_kernel,
        place,
        (4,),
        [pl.BlockSpec((rows // 4, width), lambda i, place: (i, (place[TP] + side) % 2))],
        pl.BlockSpec((rows // 4, width), lambda i, place: (i, 0)),
        shape_of((rows, width), BF16),
        (array,),
        (0, 4 * rows * width),
    )


def own_columns(place, array, width):
    rows = array.shape[0]
    if width % 128:
        return lax.dynamic_slice_in_dim(array, place[TP] * width, width, 1)
    return call(
        slice_kernel,
        place,
        (1,),
        [pl.BlockSpec((rows, width), lambda i, place: (0, place[TP]))],
        pl.BlockSpec((rows, width), lambda i, place: (0, 0)),
        shape_of((rows, width), BF16),
        (array,),
        (0, 4 * rows * width),
    )


def add_kernel(place, left, right, out):
    out[...] = left[...] + right[...]


def add_rows(place, left, right, at, rows):
    width = left.shape[1]
    spec = pl.BlockSpec((rows, width), lambda i, place: (at // rows, 0))
    return call(
        add_kernel,
        place,
        (1,),
        [spec, spec],
        pl.BlockSpec((rows, width), lambda i, place: (0, 0)),
        shape_of((rows, width), F32),
        (left, right),
        (rows * width, 12 * rows * width),
    )


def on_device(
    hidden_cont,
    hidden_prompt,
    norm_gain,
    query_weight,
    keyval_weight,
    out_weight,
    query_gain,
    key_gain,
    sample_lengths,
):
    size = query_gain.shape[0]
    heads_here = query_weight.shape[1] // size
    cont_rows = hidden_cont.shape[0]
    prompt_rows = hidden_prompt.shape[0]
    sp_index = lax.axis_index("sp")
    sp_count = lax.axis_size("sp")
    tp_index = lax.axis_index("tp")
    assert lax.axis_size("tp") == sp_count and lax.axis_size("groups") == 2
    place = jnp.stack(
        [
            sp_index,
            tp_index,
            lax.axis_index("groups"),
            tp_index * heads_here // (QH // KVH),
        ]
    ).astype(jnp.int32)
    norm_gain = norm_gain[None, :]
    query_gain = query_gain[None, :]
    key_gain = key_gain[None, :]

    half, both, block, cont = first_step(
        place, keyval_weight, hidden_cont, norm_gain, size, sp_count
    )
    halves = other_halves(half, "sp", sp_count)
    partner = swap(both, "sp", 1)
    other = swap(block, "sp", 1)
    packed = pack(place, cont, other)
    got = [swap(block, "sp", 2 * d) for d, block in enumerate(packed, 1)]
    halves = after(halves, packed)
    others = {d: swap(half, "groups", 1) for d, half in halves.items()}
    halves = both_cores(halves, "sp")
    sent = column_half(place, after(out_weight, halves), True)
    out_partner = swap(sent, "tp", 1)
    prompt, near_pair = near_keyval(
        place, hidden_prompt, norm_gain, cont, both, after(partner, halves)
    )
    cosine, sine = tables(
        place, sample_lengths, prompt_rows, prompt_rows * sp_count, cont_rows, size
    )
    hidden = own_columns(place, after(hidden_cont, cosine), out_weight.shape[1])
    got = after(got, near_pair, others, sent, cosine, hidden)
    others = both_cores(others, "sp")

    keep, send = query_parts(place, cont, [other] + got, query_weight)
    mine, near, far = sum_blocks(place, keep, send, "sp", sp_count)
    weights = [held[d] for d in range(2, sp_count) for held in (halves, others)]
    pair = keyval_rows(place, prompt, cont, cosine, sine, key_gain, near_pair, weights)
    pairs = gather_blocks(pair, "sp", sp_count)
    heads = attend(
        place,
        sample_lengths,
        mine,
        near,
        far,
        cosine,
        sine,
        query_gain,
        pairs,
        prompt_rows,
    )
    chips = range(0, sp_count, 2)
    near_heads = {d: swap(heads, "sp", d) if d else heads for d in chips}
    far_heads = {d: swap_both(heads, 1, d, sp_count) for d in chips}
    near_heads = both_cores(near_heads, "sp")
    far_heads = both_cores(far_heads, "sp")
    all_heads = [held[d] for held in (near_heads, far_heads) for d in range(sp_count)]
    parts = out_parts(place, all_heads, out_weight, out_partner)
    parts = [
        lax.ppermute(
            part,
            ("tp", "sp"),
            [
                (t * sp_count + s, s * sp_count + (t ^ e))
                for t in range(sp_count)
                for s in range(sp_count)
            ],
        )
        for e, part in enumerate(parts)
    ]
    return final_sum(place, parts, hidden)


def solution(mesh):
    placed = (
        P(("groups", "sp"), None),
        P(("groups", "sp"), None),
        P(),
        P("sp", "tp"),
        P("sp", None),
        P("tp", "sp"),
        P(),
        P(),
        P("groups"),
    )
    return jax.shard_map(
        on_device, mesh=mesh, in_specs=placed, out_specs=P(("groups", "sp"), "tp"), check_vma=False
    )
```

```python
import functools
import math

import jax
import jax.numpy as jnp
from jax import lax
from jax.experimental import pallas as pl
from jax.experimental.pallas import tpu as pltpu
from jax.sharding import PartitionSpec as P

QH = 32
KVH = 4
SP, TP, GROUP, HEAD = range(4)
BF16 = jnp.bfloat16
F32 = jnp.float32
ROOM = 14 * 1024 * 1024


def call(kernel, place, grid, in_specs, out_specs, out_shape, args, cost, scratch=(), room=ROOM):
    flops, moved = cost
    return pl.pallas_call(
        kernel,
        out_shape=out_shape,
        grid_spec=pltpu.PrefetchScalarGridSpec(
            num_scalar_prefetch=1,
            grid=grid,
            in_specs=in_specs,
            out_specs=out_specs,
            scratch_shapes=scratch,
        ),
        compiler_params=pltpu.CompilerParams(vmem_limit_bytes=room),
        cost_estimate=pl.CostEstimate(flops=flops, bytes_accessed=moved, transcendentals=0),
    )(place, *args)


def whole(array):
    zeros = (0,) * array.ndim
    return pl.BlockSpec(array.shape, lambda i, place: zeros)


def shape_of(shape, dtype):
    return jax.ShapeDtypeStruct(shape, dtype)


def rms_rows(values, gain):
    return values * lax.rsqrt(jnp.mean(values * values, axis=-1, keepdims=True) + 1e-06) * gain


def split_normed(hidden, gain, out):
    count, _, depth = out.shape
    normed = rms_rows(hidden[...].astype(F32), gain[...]).astype(BF16)
    for j in range(count):
        out[j] = normed[:, j * depth : (j + 1) * depth]


def norm_kernel(place, hidden, gain, out, split):
    split_normed(hidden, gain, split)
    for d in range(out.shape[0]):
        out[d] = split[place[SP] ^ 1 ^ 2 * d]


def norm_split(place, hidden, gain, count):
    rows, width = hidden.shape
    step = rows if rows % 32 else 32
    depth = width // count
    return call(
        norm_kernel,
        place,
        (rows // step,),
        [pl.BlockSpec((step, width), lambda i, place: (i, 0)), whole(gain)],
        [
            pl.BlockSpec((n, step, depth), lambda i, place: (0, i, 0))
            for n in (count // 2, count)
        ],
        [shape_of((n, rows, depth), BF16) for n in (count // 2, count)],
        (hidden, gain),
        (4 * rows * width, 4 * rows * width),
    )


def pack_kernel(place, cont, other, *outs):
    for d, out in enumerate(outs, 1):
        out[0] = cont[place[SP] ^ 2 * d]
        out[1] = other[d]


def pack(place, cont, other):
    count, rows, depth = cont.shape
    block = (2, rows, depth)
    sent = count // 2 - 1
    return call(
        pack_kernel,
        place,
        (1,),
        [whole(cont), whole(other)],
        [pl.BlockSpec(block, lambda i, place: (0, 0, 0))] * sent,
        [shape_of(block, BF16)] * sent,
        (cont, other),
        (0, 8 * sent * rows * depth),
    )


def pick_kernel(place, first, key, value, half, both):
    size = half.shape[1]
    half[...] = first[...]
    both[:, :size] = key[...]
    both[:, size:] = value[...]


def pick_columns(place, weight, size):
    depth = weight.shape[0]
    block = (depth, size)
    outs = [shape_of(block, BF16), shape_of((depth, 2 * size), BF16)]
    return call(
        pick_kernel,
        place,
        (1,),
        [
            pl.BlockSpec(block, lambda i, place: (0, 2 * place[HEAD] + place[GROUP])),
            pl.BlockSpec(block, lambda i, place: (0, 2 * place[HEAD])),
            pl.BlockSpec(block, lambda i, place: (0, 2 * place[HEAD] + 1)),
        ],
        [whole(out) for out in outs],
        outs,
        (weight, weight, weight),
        (0, 12 * depth * size),
    )


def query_kernel(count, place, *refs):
    cont, other, chips, (weight, keep, send) = refs[0], refs[1], refs[2:-3], refs[-3:]
    block = cont.shape[1]
    rows = [cont[place[SP]], other[0]]
    for chip in chips:
        rows += [chip[0], chip[1]]
    part = jnp.dot(jnp.concatenate(rows, axis=0), weight[...], preferred_element_type=F32)
    for d in range(count):
        at = d // 2 * block
        (keep, send)[d % 2][at : at + block, :] = part[d * block : (d + 1) * block]


def query_parts(place, cont, got, weight):
    count, block, depth = cont.shape
    width = weight.shape[1]
    step = min(width, 256)
    half = count // 2 * block
    return call(
        functools.partial(query_kernel, count),
        place,
        (width // step,),
        [whole(a) for a in (cont, *got)]
        + [pl.BlockSpec((depth, step), lambda i, place: (0, i))],
        [pl.BlockSpec((half, step), lambda i, place: (0, i))] * 2,
        [shape_of((half, width), F32)] * 2,
        (cont, *got, weight),
        (2 * count * block * depth * width, 2 * depth * width),
    )


def turn(values, cosine, sine):
    return values * cosine + pltpu.roll(values, values.shape[-1] // 2, 1) * sine


def near_kernel(place, hidden, norm_gain, cont, own, partner, prompt, out):
    split_normed(hidden, norm_gain, prompt)
    total = 0.0
    for d, weight in ((0, own), (1, partner)):
        left = jnp.concatenate([prompt[place[SP] ^ d], cont[place[SP] ^ d]], axis=0)
        total = total + jnp.dot(left, weight[...], preferred_element_type=F32)
    out[...] = total


def near_keyval(place, hidden, norm_gain, cont, own, partner):
    args = (hidden, norm_gain, cont, own, partner)
    count, cont_rows, depth = cont.shape
    prompt_rows = hidden.shape[0]
    rows = prompt_rows + cont_rows
    width = own.shape[1]
    outs = [shape_of((count, prompt_rows, depth), BF16), shape_of((rows, width), F32)]
    return call(
        near_kernel,
        place,
        (1,),
        [whole(a) for a in args],
        [whole(out) for out in outs],
        outs,
        args,
        (4 * rows * depth * width, 4 * depth * (rows * count + width)),
    )


def keyval_kernel(count, place, prompt, cont, cosine, sine, gain, near, *refs):
    weights, out = refs[:-1], refs[-1]
    size = gain.shape[1]
    total = 0.0
    for d in range(2, count):
        left = jnp.concatenate([prompt[place[SP] ^ d], cont[place[SP] ^ d]], axis=0)
        weight = jnp.concatenate([weights[2 * d - 4][...], weights[2 * d - 3][...]], axis=1)
        total = total + jnp.dot(left, weight, preferred_element_type=F32)
    swapped = place[GROUP] == 1
    first, second = total[:, :size], total[:, size:]
    key = near[:, :size] + jnp.where(swapped, second, first)
    value = near[:, size:] + jnp.where(swapped, first, second)
    out[:, :size] = turn(rms_rows(key, gain[...]), cosine[...], sine[...]).astype(BF16)
    out[:, size:] = value.astype(BF16)


def keyval_rows(place, prompt, cont, cosine, sine, gain, near, weights):
    count, prompt_rows, depth = prompt.shape
    rows = prompt_rows + cont.shape[1]
    size = gain.shape[1]
    args = (prompt, cont, cosine, sine, gain, near, *weights)
    out = shape_of((rows, 2 * size), BF16)
    return call(
        functools.partial(keyval_kernel, count),
        place,
        (1,),
        [whole(a) for a in args],
        whole(out),
        out,
        args,
        (2 * rows * count * depth * size, count * depth * (rows + 2 * size)),
    )


def starts_of(lengths, index):
    start = jnp.zeros(index.shape, jnp.int32)
    total = jnp.int32(0)
    for c in range(lengths.shape[0]):
        start = jnp.where(index >= total, total, start)
        total = total + lengths[c]
    return start


def attend_kernel(count, prompt_rows, place, lengths, mine, near, far, cosine, sine, gain, *refs):
    pairs, out = refs[:-1], refs[-1]
    rows, width = far.shape
    size = gain.shape[1]
    heads = width // size
    cosine, sine = cosine[prompt_rows:, :], sine[prompt_rows:, :]
    queries = []
    for h in range(heads):
        part = slice(h * size, (h + 1) * size)
        value = rms_rows(mine[:rows, part] + near[:rows, part] + far[:, part], gain[...])
        queries.append(turn(value, cosine, sine).astype(BF16))
    queries = jnp.concatenate(queries, axis=0)
    prompt = jnp.concatenate([pair[:prompt_rows] for pair in pairs], axis=0)
    cont = jnp.concatenate([pair[prompt_rows:] for pair in pairs], axis=0)
    scale = 1.0 / math.sqrt(size)
    by_rows = (((1,), (1,)), ((), ()))
    to_prompt = (
        lax.dot_general(queries, prompt[:, :size], by_rows, preferred_element_type=F32) * scale
    )
    to_cont = (
        lax.dot_general(queries, cont[:, :size], by_rows, preferred_element_type=F32) * scale
    )
    shape = (rows, cont.shape[0])
    own = place[SP] * rows + lax.broadcasted_iota(jnp.int32, shape, 0)
    at = lax.broadcasted_iota(jnp.int32, shape, 1)
    key = jnp.zeros(shape, jnp.int32)
    for d in range(count):
        inside = (at >= d * rows) & (at < (d + 1) * rows)
        key = jnp.where(inside, (place[SP] ^ d) * rows + at - d * rows, key)
    allowed = jnp.where((key >= starts_of(lengths, own)) & (key <= own), 0.0, -1e30)
    to_cont = to_cont + jnp.concatenate([allowed] * heads, axis=0)
    peak = jnp.maximum(
        jnp.max(to_prompt, axis=1, keepdims=True), jnp.max(to_cont, axis=1, keepdims=True)
    )
    to_prompt = jnp.exp(to_prompt - peak)
    to_cont = jnp.exp(to_cont - peak)
    divisor = jnp.sum(to_prompt, axis=1, keepdims=True) + jnp.sum(to_cont, axis=1, keepdims=True)
    result = jnp.dot(
        (to_prompt / divisor).astype(BF16), prompt[:, size:], preferred_element_type=F32
    ) + jnp.dot((to_cont / divisor).astype(BF16), cont[:, size:], preferred_element_type=F32)
    for h in range(heads):
        out[:, h * size : (h + 1) * size] = result[h * rows : (h + 1) * rows].astype(BF16)


def attend(place, lengths, mine, near, far, cosine, sine, gain, pairs, prompt_rows):
    rows, width = far.shape
    args = (mine, near, far, cosine, sine, gain, *pairs)
    out = shape_of((rows, width), BF16)
    keys = len(pairs) * pairs[0].shape[0]
    return call(
        functools.partial(attend_kernel, len(pairs), prompt_rows),
        place,
        (1,),
        [pl.BlockSpec(memory_space=pltpu.SMEM)] + [whole(a) for a in args],
        whole(out),
        out,
        (lengths, *args),
        (4 * rows * width * keys, 10 * rows * width + 512 * keys),
    )


def out_kernel(count, place, *refs):
    heads, weights, outs, part = refs[: 2 * count], refs[-count - 3 : -count - 1], refs[-count - 1 : -1], refs[-1]
    rows = heads[0].shape[0]
    total = 0.0
    for side, weight in enumerate(weights):
        left = jnp.concatenate([h[...] for h in heads[side * count : (side + 1) * count]], axis=0)
        share = jnp.dot(left, weight[...], preferred_element_type=F32)
        total = total + share.astype(BF16).astype(F32)
    total = total.astype(BF16)
    for d in range(count):
        part[d] = total[d * rows : (d + 1) * rows]
    for e in range(count):
        outs[e][...] = part[place[TP] ^ e ^ place[SP]]


def out_parts(place, heads, own, partner):
    count = len(heads) // 2
    rows = heads[0].shape[0]
    depth, width = partner.shape
    if width % 128:
        own = column_half(place, own, False)
        half = whole(own)
    else:
        half = pl.BlockSpec((depth, width), lambda i, place: (0, place[TP] % 2))
    args = (*heads, own, partner)
    return call(
        functools.partial(out_kernel, count),
        place,
        (1,),
        [whole(h) for h in heads] + [half, whole(partner)],
        [pl.BlockSpec((rows, width), lambda i, place: (0, 0))] * count,
        [shape_of((rows, width), BF16)] * count,
        args,
        (4 * count * rows * depth * width, 4 * depth * width),
        [pltpu.VMEM((count, rows, width), BF16)],
    )


def final_kernel(count, place, hidden, *refs):
    parts, out = refs[:-1], refs[-1]
    width = parts[0].shape[1]
    sums = [0.0, 0.0]
    for e, part in enumerate(parts):
        sums[e % 2] = sums[e % 2] + part[...].astype(F32)
    odd = place[SP] % 2 == 1
    left = jnp.where(odd, sums[1], sums[0])
    right = jnp.where(odd, sums[0], sums[1])
    out[:, :width] = (hidden[:, :width].astype(F32) + left).astype(BF16)
    out[:, width:] = (hidden[:, width:].astype(F32) + right).astype(BF16)


def final_sum(place, parts, hidden):
    rows, width = parts[0].shape
    width *= 2
    count = len(parts)
    if width % 128:
        hidden = lax.dynamic_slice_in_dim(hidden, place[TP] * width, width, 1)
        residual = whole(hidden)
    else:
        residual = pl.BlockSpec((rows, width), lambda i, place: (0, place[TP]))
    return call(
        functools.partial(final_kernel, count),
        place,
        (1,),
        [residual] + [whole(a) for a in parts],
        pl.BlockSpec((rows, width), lambda i, place: (0, 0)),
        shape_of((rows, width), BF16),
        (hidden, *parts),
        (count * rows * width, 12 * rows * width),
    )


def after(arrays, *others):
    return lax.optimization_barrier((arrays, others))[0]


def swap(array, axis, bits):
    return lax.ppermute(array, axis, [(i, i ^ bits) for i in range(lax.axis_size(axis))])


def swap_both(array, tp_bits, sp_bits, count):
    pairs = [
        (t * count + s, (t ^ tp_bits) * count + (s ^ sp_bits))
        for t in range(count)
        for s in range(count)
    ]
    return lax.ppermute(array, ("tp", "sp"), pairs)


def swap_bits(count):
    bits = []
    bit = 1
    while bit < count:
        bits.append(bit)
        bit *= 2
    return bits


def gather_blocks(block, axis, count):
    held = {0: block}
    bits = swap_bits(count)
    for bit in bits[1:] + bits[:1]:
        held.update({d ^ bit: swap(held[d], axis, bit) for d in sorted(held)})
    return [held[d] for d in range(count)]


def other_halves(half, axis, count):
    firsts = {0: half}
    for bit in swap_bits(count)[1:]:
        firsts.update({d ^ bit: swap(firsts[d], axis, bit) for d in sorted(firsts)})
    del firsts[0]
    return firsts


def both_cores(held, axis):
    return {**held, **{d ^ 1: swap(held[d], axis, 1) for d in sorted(held)}}


def sum_blocks(place, keep, send, axis, count):
    near = swap(send, axis, 1)
    rows = keep.shape[0] // (count // 2)
    held = {d: add_rows(place, keep, near, d // 2 * rows, rows) for d in range(2, count, 2)}
    far = 0.0
    for bit in swap_bits(count)[1:]:
        sent = [d for d in sorted(held) if d & bit]
        got = {d ^ bit: swap(held[d], axis, bit) for d in sent}
        far = far + got.pop(0)
        held = {d: held[d] + got[d] for d in got}
    return keep, near, far


def table_kernel(prompt_rows, prompt_total, place, lengths, cosine, sine):
    rows, size = cosine.shape
    shape = cosine.shape
    row = lax.broadcasted_iota(jnp.int32, shape, 0)
    lane = lax.broadcasted_iota(jnp.int32, shape, 1)
    index = place[SP] * (rows - prompt_rows) + row - prompt_rows
    position = jnp.where(
        row < prompt_rows,
        place[SP] * prompt_rows + row,
        prompt_total + index - starts_of(lengths, index),
    )
    half = size // 2
    step = jnp.where(lane < half, lane, lane - half).astype(F32)
    angle = position.astype(F32) * jnp.exp(step * (-2.0 * math.log(1000000.0) / size))
    cosine[...] = jnp.cos(angle)
    angle = jnp.sin(angle)
    sine[...] = jnp.where(lane < half, -angle, angle)


def tables(place, lengths, prompt_rows, prompt_total, cont_rows, size):
    out = shape_of((prompt_rows + cont_rows, size), F32)
    return call(
        functools.partial(table_kernel, prompt_rows, prompt_total),
        place,
        (1,),
        [pl.BlockSpec(memory_space=pltpu.SMEM)],
        [whole(out)] * 2,
        [out] * 2,
        (lengths,),
        (100 * out.size, 8 * out.size),
    )


def slice_kernel(place, array, out):
    out[...] = array[...]


def column_half(place, array, other):
    rows, width = array.shape
    width //= 2
    side = 1 if other else 0
    if width % 128:
        at = (place[TP] + side) % 2 * width
        return lax.dynamic_slice_in_dim(array, at, width, 1)
    return call(
        slice_kernel,
        place,
        (4,),
        [pl.BlockSpec((rows // 4, width), lambda i, place: (i, (place[TP] + side) % 2))],
        pl.BlockSpec((rows // 4, width), lambda i, place: (i, 0)),
        shape_of((rows, width), BF16),
        (array,),
        (0, 4 * rows * width),
    )


def add_kernel(place, left, right, out):
    out[...] = left[...] + right[...]


def add_rows(place, left, right, at, rows):
    width = left.shape[1]
    spec = pl.BlockSpec((rows, width), lambda i, place: (at // rows, 0))
    return call(
        add_kernel,
        place,
        (1,),
        [spec, spec],
        pl.BlockSpec((rows, width), lambda i, place: (0, 0)),
        shape_of((rows, width), F32),
        (left, right),
        (rows * width, 12 * rows * width),
    )


def on_device(
    hidden_cont,
    hidden_prompt,
    norm_gain,
    query_weight,
    keyval_weight,
    out_weight,
    query_gain,
    key_gain,
    sample_lengths,
):
    size = query_gain.shape[0]
    heads_here = query_weight.shape[1] // size
    cont_rows = hidden_cont.shape[0]
    prompt_rows = hidden_prompt.shape[0]
    sp_index = lax.axis_index("sp")
    sp_count = lax.axis_size("sp")
    tp_index = lax.axis_index("tp")
    assert lax.axis_size("tp") == sp_count and lax.axis_size("groups") == 2
    place = jnp.stack(
        [
            sp_index,
            tp_index,
            lax.axis_index("groups"),
            tp_index * heads_here // (QH // KVH),
        ]
    ).astype(jnp.int32)
    norm_gain = norm_gain[None, :]
    query_gain = query_gain[None, :]
    key_gain = key_gain[None, :]

    half, both = pick_columns(place, keyval_weight, size)
    halves = other_halves(half, "sp", sp_count)
    block, cont = norm_split(after(place, half), hidden_cont, norm_gain, sp_count)
    other = swap(block, "sp", 1)
    packed = pack(place, cont, other)
    got = [swap(block, "sp", 2 * d) for d, block in enumerate(packed, 1)]
    partner = swap(both, "sp", 1)
    sent = column_half(place, after(out_weight, packed), True)
    out_partner = swap(sent, "tp", 1)
    cosine, sine = tables(
        place, sample_lengths, prompt_rows, prompt_rows * sp_count, cont_rows, size
    )
    halves = after(halves, packed, sent, cosine)
    others = {d: swap(half, "groups", 1) for d, half in halves.items()}
    halves = both_cores(halves, "sp")
    prompt, near_pair = near_keyval(
        place, hidden_prompt, norm_gain, cont, both, after(partner, halves)
    )
    got = after(got, near_pair, sent, cosine)
    others = both_cores(others, "sp")

    keep, send = query_parts(place, cont, [other] + got, query_weight)
    mine, near, far = sum_blocks(place, keep, send, "sp", sp_count)
    weights = [held[d] for d in range(2, sp_count) for held in (halves, others)]
    pair = keyval_rows(place, prompt, cont, cosine, sine, key_gain, near_pair, weights)
    pairs = gather_blocks(pair, "sp", sp_count)
    heads = attend(
        place,
        sample_lengths,
        mine,
        near,
        far,
        cosine,
        sine,
        query_gain,
        pairs,
        prompt_rows,
    )
    chips = range(0, sp_count, 2)
    near_heads = {d: swap(heads, "sp", d) if d else heads for d in chips}
    far_heads = {d: swap_both(heads, 1, d, sp_count) for d in chips}
    near_heads = both_cores(near_heads, "sp")
    far_heads = both_cores(far_heads, "sp")
    all_heads = [held[d] for held in (near_heads, far_heads) for d in range(sp_count)]
    parts = out_parts(place, all_heads, out_weight, out_partner)
    parts = [
        lax.ppermute(
            part,
            ("tp", "sp"),
            [
                (t * sp_count + s, s * sp_count + (t ^ e))
                for t in range(sp_count)
                for s in range(sp_count)
            ],
        )
        for e, part in enumerate(parts)
    ]
    return final_sum(place, parts, hidden_cont)


def solution(mesh):
    placed = (
        P(("groups", "sp"), None),
        P(("groups", "sp"), None),
        P(),
        P("sp", "tp"),
        P("sp", None),
        P("tp", "sp"),
        P(),
        P(),
        P("groups"),
    )
    return jax.shard_map(
        on_device, mesh=mesh, in_specs=placed, out_specs=P(("groups", "sp"), "tp"), check_vma=False
    )
```

```python
import functools
import math

import jax
import jax.numpy as jnp
from jax import lax
from jax.experimental import pallas as pl
from jax.experimental.pallas import tpu as pltpu
from jax.sharding import PartitionSpec as P

QH = 32
KVH = 4
SP, TP, GROUP, HEAD = range(4)
BF16 = jnp.bfloat16
F32 = jnp.float32
ROOM = 14 * 1024 * 1024


def call(kernel, place, grid, in_specs, out_specs, out_shape, args, cost, scratch=(), room=ROOM):
    flops, moved = cost
    return pl.pallas_call(
        kernel,
        out_shape=out_shape,
        grid_spec=pltpu.PrefetchScalarGridSpec(
            num_scalar_prefetch=1,
            grid=grid,
            in_specs=in_specs,
            out_specs=out_specs,
            scratch_shapes=scratch,
        ),
        compiler_params=pltpu.CompilerParams(vmem_limit_bytes=room),
        cost_estimate=pl.CostEstimate(flops=flops, bytes_accessed=moved, transcendentals=0),
    )(place, *args)


def whole(array):
    zeros = (0,) * array.ndim
    return pl.BlockSpec(array.shape, lambda i, place: zeros)


def shape_of(shape, dtype):
    return jax.ShapeDtypeStruct(shape, dtype)


def rms_rows(values, gain):
    return values * lax.rsqrt(jnp.mean(values * values, axis=-1, keepdims=True) + 1e-06) * gain


def split_normed(hidden, gain, out):
    count, _, depth = out.shape
    normed = rms_rows(hidden[...].astype(F32), gain[...]).astype(BF16)
    for j in range(count):
        out[j] = normed[:, j * depth : (j + 1) * depth]


def norm_kernel(place, hidden, gain, out, split):
    split_normed(hidden, gain, split)
    for d in range(out.shape[0]):
        out[d] = split[place[SP] ^ 1 ^ 2 * d]


def norm_split(place, hidden, gain, count):
    rows, width = hidden.shape
    step = rows if rows % 32 else 32
    depth = width // count
    return call(
        norm_kernel,
        place,
        (rows // step,),
        [pl.BlockSpec((step, width), lambda i, place: (i, 0)), whole(gain)],
        [
            pl.BlockSpec((n, step, depth), lambda i, place: (0, i, 0))
            for n in (count // 2, count)
        ],
        [shape_of((n, rows, depth), BF16) for n in (count // 2, count)],
        (hidden, gain),
        (4 * rows * width, 4 * rows * width),
    )


def pack_kernel(place, cont, other, *outs):
    for d, out in enumerate(outs, 1):
        out[0] = cont[place[SP] ^ 2 * d]
        out[1] = other[d]


def pack(place, cont, other):
    count, rows, depth = cont.shape
    block = (2, rows, depth)
    sent = count // 2 - 1
    return call(
        pack_kernel,
        place,
        (1,),
        [whole(cont), whole(other)],
        [pl.BlockSpec(block, lambda i, place: (0, 0, 0))] * sent,
        [shape_of(block, BF16)] * sent,
        (cont, other),
        (0, 8 * sent * rows * depth),
    )


def pick_kernel(place, first, key, value, half, both):
    size = half.shape[1]
    half[...] = first[...]
    both[:, :size] = key[...]
    both[:, size:] = value[...]


def pick_columns(place, weight, size):
    depth = weight.shape[0]
    block = (depth, size)
    outs = [shape_of(block, BF16), shape_of((depth, 2 * size), BF16)]
    return call(
        pick_kernel,
        place,
        (1,),
        [
            pl.BlockSpec(block, lambda i, place: (0, 2 * place[HEAD] + place[GROUP])),
            pl.BlockSpec(block, lambda i, place: (0, 2 * place[HEAD])),
            pl.BlockSpec(block, lambda i, place: (0, 2 * place[HEAD] + 1)),
        ],
        [whole(out) for out in outs],
        outs,
        (weight, weight, weight),
        (0, 12 * depth * size),
    )


def query_kernel(count, place, *refs):
    cont, other, chips, (weight, keep, send) = refs[0], refs[1], refs[2:-3], refs[-3:]
    block = cont.shape[1]
    rows = [cont[place[SP]], other[0]]
    for chip in chips:
        rows += [chip[0], chip[1]]
    part = jnp.dot(jnp.concatenate(rows, axis=0), weight[...], preferred_element_type=F32)
    for d in range(count):
        at = d // 2 * block
        (keep, send)[d % 2][at : at + block, :] = part[d * block : (d + 1) * block]


def query_parts(place, cont, got, weight):
    count, block, depth = cont.shape
    width = weight.shape[1]
    step = min(width, 256)
    half = count // 2 * block
    return call(
        functools.partial(query_kernel, count),
        place,
        (width // step,),
        [whole(a) for a in (cont, *got)]
        + [pl.BlockSpec((depth, step), lambda i, place: (0, i))],
        [pl.BlockSpec((half, step), lambda i, place: (0, i))] * 2,
        [shape_of((half, width), F32)] * 2,
        (cont, *got, weight),
        (2 * count * block * depth * width, 2 * depth * width),
    )


def turn(values, cosine, sine):
    return values * cosine + pltpu.roll(values, values.shape[-1] // 2, 1) * sine


def near_kernel(place, hidden, norm_gain, cont, own, partner, prompt, out):
    split_normed(hidden, norm_gain, prompt)
    total = 0.0
    for d, weight in ((0, own), (1, partner)):
        left = jnp.concatenate([prompt[place[SP] ^ d], cont[place[SP] ^ d]], axis=0)
        total = total + jnp.dot(left, weight[...], preferred_element_type=F32)
    out[...] = total


def near_keyval(place, hidden, norm_gain, cont, own, partner):
    args = (hidden, norm_gain, cont, own, partner)
    count, cont_rows, depth = cont.shape
    prompt_rows = hidden.shape[0]
    rows = prompt_rows + cont_rows
    width = own.shape[1]
    outs = [shape_of((count, prompt_rows, depth), BF16), shape_of((rows, width), F32)]
    return call(
        near_kernel,
        place,
        (1,),
        [whole(a) for a in args],
        [whole(out) for out in outs],
        outs,
        args,
        (4 * rows * depth * width, 4 * depth * (rows * count + width)),
    )


def keyval_kernel(count, place, prompt, cont, cosine, sine, gain, near, *refs):
    weights, out = refs[:-1], refs[-1]
    size = gain.shape[1]
    total = 0.0
    for d in range(2, count):
        left = jnp.concatenate([prompt[place[SP] ^ d], cont[place[SP] ^ d]], axis=0)
        weight = jnp.concatenate([weights[2 * d - 4][...], weights[2 * d - 3][...]], axis=1)
        total = total + jnp.dot(left, weight, preferred_element_type=F32)
    swapped = place[GROUP] == 1
    first, second = total[:, :size], total[:, size:]
    key = near[:, :size] + jnp.where(swapped, second, first)
    value = near[:, size:] + jnp.where(swapped, first, second)
    out[:, :size] = turn(rms_rows(key, gain[...]), cosine[...], sine[...]).astype(BF16)
    out[:, size:] = value.astype(BF16)


def keyval_rows(place, prompt, cont, cosine, sine, gain, near, weights):
    count, prompt_rows, depth = prompt.shape
    rows = prompt_rows + cont.shape[1]
    size = gain.shape[1]
    args = (prompt, cont, cosine, sine, gain, near, *weights)
    out = shape_of((rows, 2 * size), BF16)
    return call(
        functools.partial(keyval_kernel, count),
        place,
        (1,),
        [whole(a) for a in args],
        whole(out),
        out,
        args,
        (2 * rows * count * depth * size, count * depth * (rows + 2 * size)),
    )


def starts_of(lengths, index):
    start = jnp.zeros(index.shape, jnp.int32)
    total = jnp.int32(0)
    for c in range(lengths.shape[0]):
        start = jnp.where(index >= total, total, start)
        total = total + lengths[c]
    return start


def attend_kernel(count, prompt_rows, place, lengths, mine, near, far, cosine, sine, gain, *refs):
    pairs, out = refs[:-1], refs[-1]
    rows, width = far.shape
    size = gain.shape[1]
    heads = width // size
    cosine, sine = cosine[prompt_rows:, :], sine[prompt_rows:, :]
    queries = []
    for h in range(heads):
        part = slice(h * size, (h + 1) * size)
        value = rms_rows(mine[:rows, part] + near[:rows, part] + far[:, part], gain[...])
        queries.append(turn(value, cosine, sine).astype(BF16))
    queries = jnp.concatenate(queries, axis=0)
    prompt = jnp.concatenate([pair[:prompt_rows] for pair in pairs], axis=0)
    cont = jnp.concatenate([pair[prompt_rows:] for pair in pairs], axis=0)
    scale = 1.0 / math.sqrt(size)
    by_rows = (((1,), (1,)), ((), ()))
    to_prompt = (
        lax.dot_general(queries, prompt[:, :size], by_rows, preferred_element_type=F32) * scale
    )
    to_cont = (
        lax.dot_general(queries, cont[:, :size], by_rows, preferred_element_type=F32) * scale
    )
    shape = (rows, cont.shape[0])
    own = place[SP] * rows + lax.broadcasted_iota(jnp.int32, shape, 0)
    at = lax.broadcasted_iota(jnp.int32, shape, 1)
    key = jnp.zeros(shape, jnp.int32)
    for d in range(count):
        inside = (at >= d * rows) & (at < (d + 1) * rows)
        key = jnp.where(inside, (place[SP] ^ d) * rows + at - d * rows, key)
    allowed = jnp.where((key >= starts_of(lengths, own)) & (key <= own), 0.0, -1e30)
    to_cont = to_cont + jnp.concatenate([allowed] * heads, axis=0)
    peak = jnp.maximum(
        jnp.max(to_prompt, axis=1, keepdims=True), jnp.max(to_cont, axis=1, keepdims=True)
    )
    to_prompt = jnp.exp(to_prompt - peak)
    to_cont = jnp.exp(to_cont - peak)
    divisor = jnp.sum(to_prompt, axis=1, keepdims=True) + jnp.sum(to_cont, axis=1, keepdims=True)
    result = jnp.dot(
        (to_prompt / divisor).astype(BF16), prompt[:, size:], preferred_element_type=F32
    ) + jnp.dot((to_cont / divisor).astype(BF16), cont[:, size:], preferred_element_type=F32)
    for h in range(heads):
        out[:, h * size : (h + 1) * size] = result[h * rows : (h + 1) * rows].astype(BF16)


def attend(place, lengths, mine, near, far, cosine, sine, gain, pairs, prompt_rows):
    rows, width = far.shape
    args = (mine, near, far, cosine, sine, gain, *pairs)
    out = shape_of((rows, width), BF16)
    keys = len(pairs) * pairs[0].shape[0]
    return call(
        functools.partial(attend_kernel, len(pairs), prompt_rows),
        place,
        (1,),
        [pl.BlockSpec(memory_space=pltpu.SMEM)] + [whole(a) for a in args],
        whole(out),
        out,
        (lengths, *args),
        (4 * rows * width * keys, 10 * rows * width + 512 * keys),
    )


def out_kernel(count, place, *refs):
    heads, weights, outs, part = refs[: 2 * count], refs[-count - 3 : -count - 1], refs[-count - 1 : -1], refs[-1]
    rows = heads[0].shape[0]
    total = 0.0
    for side, weight in enumerate(weights):
        left = jnp.concatenate([h[...] for h in heads[side * count : (side + 1) * count]], axis=0)
        share = jnp.dot(left, weight[...], preferred_element_type=F32)
        total = total + share.astype(BF16).astype(F32)
    total = total.astype(BF16)
    for d in range(count):
        part[d] = total[d * rows : (d + 1) * rows]
    for e in range(count):
        outs[e][...] = part[place[TP] ^ e ^ place[SP]]


def out_parts(place, heads, own, partner):
    count = len(heads) // 2
    rows = heads[0].shape[0]
    depth, width = partner.shape
    if width % 128:
        own = column_half(place, own, False)
        half = whole(own)
    else:
        half = pl.BlockSpec((depth, width), lambda i, place: (0, place[TP] % 2))
    args = (*heads, own, partner)
    return call(
        functools.partial(out_kernel, count),
        place,
        (1,),
        [whole(h) for h in heads] + [half, whole(partner)],
        [pl.BlockSpec((rows, width), lambda i, place: (0, 0))] * count,
        [shape_of((rows, width), BF16)] * count,
        args,
        (4 * count * rows * depth * width, 4 * depth * width),
        [pltpu.VMEM((count, rows, width), BF16)],
    )


def final_kernel(count, place, hidden, *refs):
    parts, out = refs[:-1], refs[-1]
    width = parts[0].shape[1]
    sums = [0.0, 0.0]
    for e, part in enumerate(parts):
        sums[e % 2] = sums[e % 2] + part[...].astype(F32)
    odd = place[SP] % 2 == 1
    left = jnp.where(odd, sums[1], sums[0])
    right = jnp.where(odd, sums[0], sums[1])
    out[:, :width] = (hidden[:, :width].astype(F32) + left).astype(BF16)
    out[:, width:] = (hidden[:, width:].astype(F32) + right).astype(BF16)


def final_sum(place, parts, hidden):
    rows, width = parts[0].shape
    width *= 2
    count = len(parts)
    if width % 128:
        hidden = lax.dynamic_slice_in_dim(hidden, place[TP] * width, width, 1)
        residual = whole(hidden)
    else:
        residual = pl.BlockSpec((rows, width), lambda i, place: (0, place[TP]))
    return call(
        functools.partial(final_kernel, count),
        place,
        (1,),
        [residual] + [whole(a) for a in parts],
        pl.BlockSpec((rows, width), lambda i, place: (0, 0)),
        shape_of((rows, width), BF16),
        (hidden, *parts),
        (count * rows * width, 12 * rows * width),
    )


def after(arrays, *others):
    return lax.optimization_barrier((arrays, others))[0]


def swap(array, axis, bits):
    return lax.ppermute(array, axis, [(i, i ^ bits) for i in range(lax.axis_size(axis))])


def swap_both(array, tp_bits, sp_bits, count):
    pairs = [
        (t * count + s, (t ^ tp_bits) * count + (s ^ sp_bits))
        for t in range(count)
        for s in range(count)
    ]
    return lax.ppermute(array, ("tp", "sp"), pairs)


def swap_bits(count):
    bits = []
    bit = 1
    while bit < count:
        bits.append(bit)
        bit *= 2
    return bits


def gather_blocks(block, axis, count):
    held = {0: block}
    bits = swap_bits(count)
    for bit in bits[1:] + bits[:1]:
        held.update({d ^ bit: swap(held[d], axis, bit) for d in sorted(held)})
    return [held[d] for d in range(count)]


def other_halves(half, axis, count):
    firsts = {0: half}
    for bit in swap_bits(count)[1:]:
        firsts.update({d ^ bit: swap(firsts[d], axis, bit) for d in sorted(firsts)})
    del firsts[0]
    return firsts


def both_cores(held, axis):
    return {**held, **{d ^ 1: swap(held[d], axis, 1) for d in sorted(held)}}


def sum_over_chips(place, keep, near, axis, count):
    rows = keep.shape[0] // (count // 2)
    held = {d: add_rows(place, keep, near, d // 2 * rows, rows) for d in range(2, count, 2)}
    far = 0.0
    for bit in swap_bits(count)[1:]:
        sent = [d for d in sorted(held) if d & bit]
        got = {d ^ bit: swap(held[d], axis, bit) for d in sent}
        far = far + got.pop(0)
        held = {d: held[d] + got[d] for d in got}
    return far


def table_kernel(prompt_rows, prompt_total, place, lengths, cosine, sine):
    rows, size = cosine.shape
    shape = cosine.shape
    row = lax.broadcasted_iota(jnp.int32, shape, 0)
    lane = lax.broadcasted_iota(jnp.int32, shape, 1)
    index = place[SP] * (rows - prompt_rows) + row - prompt_rows
    position = jnp.where(
        row < prompt_rows,
        place[SP] * prompt_rows + row,
        prompt_total + index - starts_of(lengths, index),
    )
    half = size // 2
    step = jnp.where(lane < half, lane, lane - half).astype(F32)
    angle = position.astype(F32) * jnp.exp(step * (-2.0 * math.log(1000000.0) / size))
    cosine[...] = jnp.cos(angle)
    angle = jnp.sin(angle)
    sine[...] = jnp.where(lane < half, -angle, angle)


def tables(place, lengths, prompt_rows, prompt_total, cont_rows, size):
    out = shape_of((prompt_rows + cont_rows, size), F32)
    return call(
        functools.partial(table_kernel, prompt_rows, prompt_total),
        place,
        (1,),
        [pl.BlockSpec(memory_space=pltpu.SMEM)],
        [whole(out)] * 2,
        [out] * 2,
        (lengths,),
        (100 * out.size, 8 * out.size),
    )


def slice_kernel(place, array, out):
    out[...] = array[...]


def column_half(place, array, other):
    rows, width = array.shape
    width //= 2
    side = 1 if other else 0
    if width % 128:
        at = (place[TP] + side) % 2 * width
        return lax.dynamic_slice_in_dim(array, at, width, 1)
    return call(
        slice_kernel,
        place,
        (4,),
        [pl.BlockSpec((rows // 4, width), lambda i, place: (i, (place[TP] + side) % 2))],
        pl.BlockSpec((rows // 4, width), lambda i, place: (i, 0)),
        shape_of((rows, width), BF16),
        (array,),
        (0, 4 * rows * width),
    )


def add_kernel(place, left, right, out):
    out[...] = left[...] + right[...]


def add_rows(place, left, right, at, rows):
    width = left.shape[1]
    spec = pl.BlockSpec((rows, width), lambda i, place: (at // rows, 0))
    return call(
        add_kernel,
        place,
        (1,),
        [spec, spec],
        pl.BlockSpec((rows, width), lambda i, place: (0, 0)),
        shape_of((rows, width), F32),
        (left, right),
        (rows * width, 12 * rows * width),
    )


def on_device(
    hidden_cont,
    hidden_prompt,
    norm_gain,
    query_weight,
    keyval_weight,
    out_weight,
    query_gain,
    key_gain,
    sample_lengths,
):
    size = query_gain.shape[0]
    heads_here = query_weight.shape[1] // size
    cont_rows = hidden_cont.shape[0]
    prompt_rows = hidden_prompt.shape[0]
    sp_index = lax.axis_index("sp")
    sp_count = lax.axis_size("sp")
    tp_index = lax.axis_index("tp")
    assert lax.axis_size("tp") == sp_count and lax.axis_size("groups") == 2
    place = jnp.stack(
        [
            sp_index,
            tp_index,
            lax.axis_index("groups"),
            tp_index * heads_here // (QH // KVH),
        ]
    ).astype(jnp.int32)
    norm_gain = norm_gain[None, :]
    query_gain = query_gain[None, :]
    key_gain = key_gain[None, :]

    half, both = pick_columns(place, keyval_weight, size)
    halves = other_halves(half, "sp", sp_count)
    block, cont = norm_split(after(place, half), hidden_cont, norm_gain, sp_count)
    other = swap(block, "sp", 1)
    packed = pack(place, cont, other)
    got = [swap(block, "sp", 2 * d) for d, block in enumerate(packed, 1)]
    partner = swap(both, "sp", 1)
    sent = column_half(place, after(out_weight, packed), True)
    out_partner = swap(sent, "tp", 1)
    cosine, sine = tables(
        place, sample_lengths, prompt_rows, prompt_rows * sp_count, cont_rows, size
    )
    halves = after(halves, packed, sent, cosine)
    others = {d: swap(half, "groups", 1) for d, half in halves.items()}
    halves = both_cores(halves, "sp")
    prompt, near_pair = near_keyval(
        place, hidden_prompt, norm_gain, cont, both, after(partner, halves)
    )
    got = after(got, near_pair, sent, cosine)
    others = both_cores(others, "sp")

    keep, send = query_parts(place, cont, [other] + got, query_weight)
    near = swap(send, "sp", 1)
    weights = [held[d] for d in range(2, sp_count) for held in (halves, others)]
    pair = keyval_rows(place, prompt, cont, cosine, sine, key_gain, near_pair, weights)
    pairs = gather_blocks(pair, "sp", sp_count)
    far = sum_over_chips(place, keep, after(near, pair), "sp", sp_count)
    heads = attend(
        place,
        sample_lengths,
        keep,
        near,
        far,
        cosine,
        sine,
        query_gain,
        pairs,
        prompt_rows,
    )
    chips = range(0, sp_count, 2)
    near_heads = {d: swap(heads, "sp", d) if d else heads for d in chips}
    far_heads = {d: swap_both(heads, 1, d, sp_count) for d in chips}
    near_heads = both_cores(near_heads, "sp")
    far_heads = both_cores(far_heads, "sp")
    all_heads = [held[d] for held in (near_heads, far_heads) for d in range(sp_count)]
    parts = out_parts(place, all_heads, out_weight, out_partner)
    parts = [
        lax.ppermute(
            part,
            ("tp", "sp"),
            [
                (t * sp_count + s, s * sp_count + (t ^ e))
                for t in range(sp_count)
                for s in range(sp_count)
            ],
        )
        for e, part in enumerate(parts)
    ]
    return final_sum(place, parts, hidden_cont)


def solution(mesh):
    placed = (
        P(("groups", "sp"), None),
        P(("groups", "sp"), None),
        P(),
        P("sp", "tp"),
        P("sp", None),
        P("tp", "sp"),
        P(),
        P(),
        P("groups"),
    )
    return jax.shard_map(
        on_device, mesh=mesh, in_specs=placed, out_specs=P(("groups", "sp"), "tp"), check_vma=False
    )
```

```python
import functools
import math

import jax
import jax.numpy as jnp
from jax import lax
from jax.experimental import pallas as pl
from jax.experimental.pallas import tpu as pltpu
from jax.sharding import PartitionSpec as P

QH = 32
KVH = 4
SP, TP, GROUP, HEAD = range(4)
BF16 = jnp.bfloat16
F32 = jnp.float32
ROOM = 14 * 1024 * 1024


def call(kernel, place, grid, in_specs, out_specs, out_shape, args, cost, scratch=(), room=ROOM):
    flops, moved = cost
    return pl.pallas_call(
        kernel,
        out_shape=out_shape,
        grid_spec=pltpu.PrefetchScalarGridSpec(
            num_scalar_prefetch=1,
            grid=grid,
            in_specs=in_specs,
            out_specs=out_specs,
            scratch_shapes=scratch,
        ),
        compiler_params=pltpu.CompilerParams(vmem_limit_bytes=room),
        cost_estimate=pl.CostEstimate(flops=flops, bytes_accessed=moved, transcendentals=0),
    )(place, *args)


def whole(array):
    zeros = (0,) * array.ndim
    return pl.BlockSpec(array.shape, lambda i, place: zeros)


def shape_of(shape, dtype):
    return jax.ShapeDtypeStruct(shape, dtype)


def rms_rows(values, gain):
    return values * lax.rsqrt(jnp.mean(values * values, axis=-1, keepdims=True) + 1e-06) * gain


def split_normed(hidden, gain, out):
    count, _, depth = out.shape
    normed = rms_rows(hidden[...].astype(F32), gain[...]).astype(BF16)
    for j in range(count):
        out[j] = normed[:, j * depth : (j + 1) * depth]


def norm_kernel(place, hidden, gain, out, split):
    split_normed(hidden, gain, split)
    for d in range(out.shape[0]):
        out[d] = split[place[SP] ^ 1 ^ 2 * d]


def norm_split(place, hidden, gain, count):
    rows, width = hidden.shape
    step = rows if rows % 32 else 32
    depth = width // count
    return call(
        norm_kernel,
        place,
        (rows // step,),
        [pl.BlockSpec((step, width), lambda i, place: (i, 0)), whole(gain)],
        [
            pl.BlockSpec((n, step, depth), lambda i, place: (0, i, 0))
            for n in (count // 2, count)
        ],
        [shape_of((n, rows, depth), BF16) for n in (count // 2, count)],
        (hidden, gain),
        (4 * rows * width, 4 * rows * width),
    )


def pack_kernel(place, cont, other, *outs):
    for d, out in enumerate(outs, 1):
        out[0] = cont[place[SP] ^ 2 * d]
        out[1] = other[d]


def pack(place, cont, other):
    count, rows, depth = cont.shape
    block = (2, rows, depth)
    sent = count // 2 - 1
    return call(
        pack_kernel,
        place,
        (1,),
        [whole(cont), whole(other)],
        [pl.BlockSpec(block, lambda i, place: (0, 0, 0))] * sent,
        [shape_of(block, BF16)] * sent,
        (cont, other),
        (0, 8 * sent * rows * depth),
    )


def pick_kernel(place, first, key, value, half, both):
    size = half.shape[1]
    half[...] = first[...]
    both[:, :size] = key[...]
    both[:, size:] = value[...]


def pick_columns(place, weight, size):
    depth = weight.shape[0]
    block = (depth, size)
    outs = [shape_of(block, BF16), shape_of((depth, 2 * size), BF16)]
    return call(
        pick_kernel,
        place,
        (1,),
        [
            pl.BlockSpec(block, lambda i, place: (0, 2 * place[HEAD] + place[GROUP])),
            pl.BlockSpec(block, lambda i, place: (0, 2 * place[HEAD])),
            pl.BlockSpec(block, lambda i, place: (0, 2 * place[HEAD] + 1)),
        ],
        [whole(out) for out in outs],
        outs,
        (weight, weight, weight),
        (0, 12 * depth * size),
    )


def query_kernel(count, place, *refs):
    cont, other, chips, (weight, keep, send) = refs[0], refs[1], refs[2:-3], refs[-3:]
    block = cont.shape[1]
    rows = [cont[place[SP]], other[0]]
    for chip in chips:
        rows += [chip[0], chip[1]]
    part = jnp.dot(jnp.concatenate(rows, axis=0), weight[...], preferred_element_type=F32)
    for d in range(count):
        at = d // 2 * block
        (keep, send)[d % 2][at : at + block, :] = part[d * block : (d + 1) * block]


def query_parts(place, cont, got, weight):
    count, block, depth = cont.shape
    width = weight.shape[1]
    half = count // 2 * block
    return call(
        functools.partial(query_kernel, count),
        place,
        (1,),
        [whole(a) for a in (cont, *got)]
        + [whole(weight)],
        [pl.BlockSpec((half, width), lambda i, place: (0, 0))] * 2,
        [shape_of((half, width), F32)] * 2,
        (cont, *got, weight),
        (2 * count * block * depth * width, 2 * depth * width),
    )


def turn(values, cosine, sine):
    return values * cosine + pltpu.roll(values, values.shape[-1] // 2, 1) * sine


def near_kernel(place, hidden, norm_gain, cont, own, partner, prompt, out):
    split_normed(hidden, norm_gain, prompt)
    total = 0.0
    for d, weight in ((0, own), (1, partner)):
        left = jnp.concatenate([prompt[place[SP] ^ d], cont[place[SP] ^ d]], axis=0)
        total = total + jnp.dot(left, weight[...], preferred_element_type=F32)
    out[...] = total


def near_keyval(place, hidden, norm_gain, cont, own, partner):
    args = (hidden, norm_gain, cont, own, partner)
    count, cont_rows, depth = cont.shape
    prompt_rows = hidden.shape[0]
    rows = prompt_rows + cont_rows
    width = own.shape[1]
    outs = [shape_of((count, prompt_rows, depth), BF16), shape_of((rows, width), F32)]
    return call(
        near_kernel,
        place,
        (1,),
        [whole(a) for a in args],
        [whole(out) for out in outs],
        outs,
        args,
        (4 * rows * depth * width, 4 * depth * (rows * count + width)),
    )


def keyval_kernel(count, place, prompt, cont, cosine, sine, gain, near, *refs):
    weights, out = refs[:-1], refs[-1]
    size = gain.shape[1]
    total = 0.0
    for d in range(2, count):
        left = jnp.concatenate([prompt[place[SP] ^ d], cont[place[SP] ^ d]], axis=0)
        weight = jnp.concatenate([weights[2 * d - 4][...], weights[2 * d - 3][...]], axis=1)
        total = total + jnp.dot(left, weight, preferred_element_type=F32)
    swapped = place[GROUP] == 1
    first, second = total[:, :size], total[:, size:]
    key = near[:, :size] + jnp.where(swapped, second, first)
    value = near[:, size:] + jnp.where(swapped, first, second)
    out[:, :size] = turn(rms_rows(key, gain[...]), cosine[...], sine[...]).astype(BF16)
    out[:, size:] = value.astype(BF16)


def keyval_rows(place, prompt, cont, cosine, sine, gain, near, weights):
    count, prompt_rows, depth = prompt.shape
    rows = prompt_rows + cont.shape[1]
    size = gain.shape[1]
    args = (prompt, cont, cosine, sine, gain, near, *weights)
    out = shape_of((rows, 2 * size), BF16)
    return call(
        functools.partial(keyval_kernel, count),
        place,
        (1,),
        [whole(a) for a in args],
        whole(out),
        out,
        args,
        (2 * rows * count * depth * size, count * depth * (rows + 2 * size)),
    )


def starts_of(lengths, index):
    start = jnp.zeros(index.shape, jnp.int32)
    total = jnp.int32(0)
    for c in range(lengths.shape[0]):
        start = jnp.where(index >= total, total, start)
        total = total + lengths[c]
    return start


def attend_kernel(count, prompt_rows, place, lengths, mine, near, far, cosine, sine, gain, *refs):
    pairs, out = refs[:-1], refs[-1]
    rows, width = far.shape
    size = gain.shape[1]
    heads = width // size
    cosine, sine = cosine[prompt_rows:, :], sine[prompt_rows:, :]
    queries = []
    for h in range(heads):
        part = slice(h * size, (h + 1) * size)
        value = rms_rows(mine[:rows, part] + near[:rows, part] + far[:, part], gain[...])
        queries.append(turn(value, cosine, sine).astype(BF16))
    queries = jnp.concatenate(queries, axis=0)
    prompt = jnp.concatenate([pair[:prompt_rows] for pair in pairs], axis=0)
    cont = jnp.concatenate([pair[prompt_rows:] for pair in pairs], axis=0)
    scale = 1.0 / math.sqrt(size)
    by_rows = (((1,), (1,)), ((), ()))
    to_prompt = (
        lax.dot_general(queries, prompt[:, :size], by_rows, preferred_element_type=F32) * scale
    )
    to_cont = (
        lax.dot_general(queries, cont[:, :size], by_rows, preferred_element_type=F32) * scale
    )
    shape = (rows, cont.shape[0])
    own = place[SP] * rows + lax.broadcasted_iota(jnp.int32, shape, 0)
    at = lax.broadcasted_iota(jnp.int32, shape, 1)
    key = jnp.zeros(shape, jnp.int32)
    for d in range(count):
        inside = (at >= d * rows) & (at < (d + 1) * rows)
        key = jnp.where(inside, (place[SP] ^ d) * rows + at - d * rows, key)
    allowed = jnp.where((key >= starts_of(lengths, own)) & (key <= own), 0.0, -1e30)
    to_cont = to_cont + jnp.concatenate([allowed] * heads, axis=0)
    peak = jnp.maximum(
        jnp.max(to_prompt, axis=1, keepdims=True), jnp.max(to_cont, axis=1, keepdims=True)
    )
    to_prompt = jnp.exp(to_prompt - peak)
    to_cont = jnp.exp(to_cont - peak)
    divisor = jnp.sum(to_prompt, axis=1, keepdims=True) + jnp.sum(to_cont, axis=1, keepdims=True)
    result = jnp.dot(
        (to_prompt / divisor).astype(BF16), prompt[:, size:], preferred_element_type=F32
    ) + jnp.dot((to_cont / divisor).astype(BF16), cont[:, size:], preferred_element_type=F32)
    for h in range(heads):
        out[:, h * size : (h + 1) * size] = result[h * rows : (h + 1) * rows].astype(BF16)


def attend(place, lengths, mine, near, far, cosine, sine, gain, pairs, prompt_rows):
    rows, width = far.shape
    args = (mine, near, far, cosine, sine, gain, *pairs)
    out = shape_of((rows, width), BF16)
    keys = len(pairs) * pairs[0].shape[0]
    return call(
        functools.partial(attend_kernel, len(pairs), prompt_rows),
        place,
        (1,),
        [pl.BlockSpec(memory_space=pltpu.SMEM)] + [whole(a) for a in args],
        whole(out),
        out,
        (lengths, *args),
        (4 * rows * width * keys, 10 * rows * width + 512 * keys),
    )


def out_kernel(count, place, *refs):
    heads, weights, outs, part = refs[: 2 * count], refs[-count - 3 : -count - 1], refs[-count - 1 : -1], refs[-1]
    rows = heads[0].shape[0]
    total = 0.0
    for side, weight in enumerate(weights):
        left = jnp.concatenate([h[...] for h in heads[side * count : (side + 1) * count]], axis=0)
        share = jnp.dot(left, weight[...], preferred_element_type=F32)
        total = total + share.astype(BF16).astype(F32)
    total = total.astype(BF16)
    for d in range(count):
        part[d] = total[d * rows : (d + 1) * rows]
    for e in range(count):
        outs[e][...] = part[place[TP] ^ e ^ place[SP]]


def out_parts(place, heads, own, partner):
    count = len(heads) // 2
    rows = heads[0].shape[0]
    depth, width = partner.shape
    if width % 128:
        own = column_half(place, own, False)
        half = whole(own)
    else:
        half = pl.BlockSpec((depth, width), lambda i, place: (0, place[TP] % 2))
    args = (*heads, own, partner)
    return call(
        functools.partial(out_kernel, count),
        place,
        (1,),
        [whole(h) for h in heads] + [half, whole(partner)],
        [pl.BlockSpec((rows, width), lambda i, place: (0, 0))] * count,
        [shape_of((rows, width), BF16)] * count,
        args,
        (4 * count * rows * depth * width, 4 * depth * width),
        [pltpu.VMEM((count, rows, width), BF16)],
    )


def final_kernel(count, place, hidden, *refs):
    parts, out = refs[:-1], refs[-1]
    width = parts[0].shape[1]
    sums = [0.0, 0.0]
    for e, part in enumerate(parts):
        sums[e % 2] = sums[e % 2] + part[...].astype(F32)
    odd = place[SP] % 2 == 1
    left = jnp.where(odd, sums[1], sums[0])
    right = jnp.where(odd, sums[0], sums[1])
    out[:, :width] = (hidden[:, :width].astype(F32) + left).astype(BF16)
    out[:, width:] = (hidden[:, width:].astype(F32) + right).astype(BF16)


def final_sum(place, parts, hidden):
    rows, width = parts[0].shape
    width *= 2
    count = len(parts)
    if width % 128:
        hidden = lax.dynamic_slice_in_dim(hidden, place[TP] * width, width, 1)
        residual = whole(hidden)
    else:
        residual = pl.BlockSpec((rows, width), lambda i, place: (0, place[TP]))
    return call(
        functools.partial(final_kernel, count),
        place,
        (1,),
        [residual] + [whole(a) for a in parts],
        pl.BlockSpec((rows, width), lambda i, place: (0, 0)),
        shape_of((rows, width), BF16),
        (hidden, *parts),
        (count * rows * width, 12 * rows * width),
    )


def after(arrays, *others):
    return lax.optimization_barrier((arrays, others))[0]


def swap(array, axis, bits):
    return lax.ppermute(array, axis, [(i, i ^ bits) for i in range(lax.axis_size(axis))])


def swap_both(array, tp_bits, sp_bits, count):
    pairs = [
        (t * count + s, (t ^ tp_bits) * count + (s ^ sp_bits))
        for t in range(count)
        for s in range(count)
    ]
    return lax.ppermute(array, ("tp", "sp"), pairs)


def swap_bits(count):
    bits = []
    bit = 1
    while bit < count:
        bits.append(bit)
        bit *= 2
    return bits


def gather_blocks(block, axis, count):
    held = {0: block}
    bits = swap_bits(count)
    for bit in bits[1:] + bits[:1]:
        held.update({d ^ bit: swap(held[d], axis, bit) for d in sorted(held)})
    return [held[d] for d in range(count)]


def other_halves(half, axis, count):
    firsts = {0: half}
    for bit in swap_bits(count)[1:]:
        firsts.update({d ^ bit: swap(firsts[d], axis, bit) for d in sorted(firsts)})
    del firsts[0]
    return firsts


def both_cores(held, axis):
    return {**held, **{d ^ 1: swap(held[d], axis, 1) for d in sorted(held)}}


def sum_blocks(place, keep, send, axis, count):
    near = swap(send, axis, 1)
    rows = keep.shape[0] // (count // 2)
    held = {d: add_rows(place, keep, near, d // 2 * rows, rows) for d in range(2, count, 2)}
    far = 0.0
    for bit in swap_bits(count)[1:]:
        sent = [d for d in sorted(held) if d & bit]
        got = {d ^ bit: swap(held[d], axis, bit) for d in sent}
        far = far + got.pop(0)
        held = {d: held[d] + got[d] for d in got}
    return keep, near, far


def table_kernel(prompt_rows, prompt_total, place, lengths, cosine, sine):
    rows, size = cosine.shape
    shape = cosine.shape
    row = lax.broadcasted_iota(jnp.int32, shape, 0)
    lane = lax.broadcasted_iota(jnp.int32, shape, 1)
    index = place[SP] * (rows - prompt_rows) + row - prompt_rows
    position = jnp.where(
        row < prompt_rows,
        place[SP] * prompt_rows + row,
        prompt_total + index - starts_of(lengths, index),
    )
    half = size // 2
    step = jnp.where(lane < half, lane, lane - half).astype(F32)
    angle = position.astype(F32) * jnp.exp(step * (-2.0 * math.log(1000000.0) / size))
    cosine[...] = jnp.cos(angle)
    angle = jnp.sin(angle)
    sine[...] = jnp.where(lane < half, -angle, angle)


def tables(place, lengths, prompt_rows, prompt_total, cont_rows, size):
    out = shape_of((prompt_rows + cont_rows, size), F32)
    return call(
        functools.partial(table_kernel, prompt_rows, prompt_total),
        place,
        (1,),
        [pl.BlockSpec(memory_space=pltpu.SMEM)],
        [whole(out)] * 2,
        [out] * 2,
        (lengths,),
        (100 * out.size, 8 * out.size),
    )


def slice_kernel(place, array, out):
    out[...] = array[...]


def column_half(place, array, other):
    rows, width = array.shape
    width //= 2
    side = 1 if other else 0
    if width % 128:
        at = (place[TP] + side) % 2 * width
        return lax.dynamic_slice_in_dim(array, at, width, 1)
    return call(
        slice_kernel,
        place,
        (4,),
        [pl.BlockSpec((rows // 4, width), lambda i, place: (i, (place[TP] + side) % 2))],
        pl.BlockSpec((rows // 4, width), lambda i, place: (i, 0)),
        shape_of((rows, width), BF16),
        (array,),
        (0, 4 * rows * width),
    )


def add_kernel(place, left, right, out):
    out[...] = left[...] + right[...]


def add_rows(place, left, right, at, rows):
    width = left.shape[1]
    spec = pl.BlockSpec((rows, width), lambda i, place: (at // rows, 0))
    return call(
        add_kernel,
        place,
        (1,),
        [spec, spec],
        pl.BlockSpec((rows, width), lambda i, place: (0, 0)),
        shape_of((rows, width), F32),
        (left, right),
        (rows * width, 12 * rows * width),
    )


def on_device(
    hidden_cont,
    hidden_prompt,
    norm_gain,
    query_weight,
    keyval_weight,
    out_weight,
    query_gain,
    key_gain,
    sample_lengths,
):
    size = query_gain.shape[0]
    heads_here = query_weight.shape[1] // size
    cont_rows = hidden_cont.shape[0]
    prompt_rows = hidden_prompt.shape[0]
    sp_index = lax.axis_index("sp")
    sp_count = lax.axis_size("sp")
    tp_index = lax.axis_index("tp")
    assert lax.axis_size("tp") == sp_count and lax.axis_size("groups") == 2
    place = jnp.stack(
        [
            sp_index,
            tp_index,
            lax.axis_index("groups"),
            tp_index * heads_here // (QH // KVH),
        ]
    ).astype(jnp.int32)
    norm_gain = norm_gain[None, :]
    query_gain = query_gain[None, :]
    key_gain = key_gain[None, :]

    half, both = pick_columns(place, keyval_weight, size)
    halves = other_halves(half, "sp", sp_count)
    block, cont = norm_split(after(place, half), hidden_cont, norm_gain, sp_count)
    other = swap(block, "sp", 1)
    packed = pack(place, cont, other)
    got = [swap(block, "sp", 2 * d) for d, block in enumerate(packed, 1)]
    partner = swap(both, "sp", 1)
    sent = column_half(place, after(out_weight, packed), True)
    out_partner = swap(sent, "tp", 1)
    cosine, sine = tables(
        place, sample_lengths, prompt_rows, prompt_rows * sp_count, cont_rows, size
    )
    halves = after(halves, packed, sent, cosine)
    others = {d: swap(half, "groups", 1) for d, half in halves.items()}
    halves = both_cores(halves, "sp")
    prompt, near_pair = near_keyval(
        place, hidden_prompt, norm_gain, cont, both, after(partner, halves)
    )
    got = after(got, near_pair, sent, cosine)
    others = both_cores(others, "sp")

    keep, send = query_parts(place, cont, [other] + got, query_weight)
    mine, near, far = sum_blocks(place, keep, send, "sp", sp_count)
    weights = [held[d] for d in range(2, sp_count) for held in (halves, others)]
    pair = keyval_rows(place, prompt, cont, cosine, sine, key_gain, near_pair, weights)
    pairs = gather_blocks(pair, "sp", sp_count)
    heads = attend(
        place,
        sample_lengths,
        mine,
        near,
        far,
        cosine,
        sine,
        query_gain,
        pairs,
        prompt_rows,
    )
    chips = range(0, sp_count, 2)
    near_heads = {d: swap(heads, "sp", d) if d else heads for d in chips}
    far_heads = {d: swap_both(heads, 1, d, sp_count) for d in chips}
    near_heads = both_cores(near_heads, "sp")
    far_heads = both_cores(far_heads, "sp")
    all_heads = [held[d] for held in (near_heads, far_heads) for d in range(sp_count)]
    parts = out_parts(place, all_heads, out_weight, out_partner)
    parts = [
        lax.ppermute(
            part,
            ("tp", "sp"),
            [
                (t * sp_count + s, s * sp_count + (t ^ e))
                for t in range(sp_count)
                for s in range(sp_count)
            ],
        )
        for e, part in enumerate(parts)
    ]
    return final_sum(place, parts, hidden_cont)


def solution(mesh):
    placed = (
        P(("groups", "sp"), None),
        P(("groups", "sp"), None),
        P(),
        P("sp", "tp"),
        P("sp", None),
        P("tp", "sp"),
        P(),
        P(),
        P("groups"),
    )
    return jax.shard_map(
        on_device, mesh=mesh, in_specs=placed, out_specs=P(("groups", "sp"), "tp"), check_vma=False
    )
```

```python
import functools
import math

import jax
import jax.numpy as jnp
from jax import lax
from jax.experimental import pallas as pl
from jax.experimental.pallas import tpu as pltpu
from jax.sharding import PartitionSpec as P

QH = 32
KVH = 4
SP, TP, GROUP, HEAD = range(4)
BF16 = jnp.bfloat16
F32 = jnp.float32
ROOM = 14 * 1024 * 1024


def call(kernel, place, grid, in_specs, out_specs, out_shape, args, cost, scratch=(), room=ROOM):
    flops, moved = cost
    return pl.pallas_call(
        kernel,
        out_shape=out_shape,
        grid_spec=pltpu.PrefetchScalarGridSpec(
            num_scalar_prefetch=1,
            grid=grid,
            in_specs=in_specs,
            out_specs=out_specs,
            scratch_shapes=scratch,
        ),
        compiler_params=pltpu.CompilerParams(vmem_limit_bytes=room),
        cost_estimate=pl.CostEstimate(flops=flops, bytes_accessed=moved, transcendentals=0),
    )(place, *args)


def whole(array):
    zeros = (0,) * array.ndim
    return pl.BlockSpec(array.shape, lambda i, place: zeros)


def shape_of(shape, dtype):
    return jax.ShapeDtypeStruct(shape, dtype)


def rms_rows(values, gain):
    return values * lax.rsqrt(jnp.mean(values * values, axis=-1, keepdims=True) + 1e-06) * gain


def split_normed(hidden, gain, out):
    count, _, depth = out.shape
    normed = rms_rows(hidden[...].astype(F32), gain[...]).astype(BF16)
    for j in range(count):
        out[j] = normed[:, j * depth : (j + 1) * depth]


def norm_kernel(place, hidden, gain, out, split):
    split_normed(hidden, gain, split)
    for d in range(out.shape[0]):
        out[d] = split[place[SP] ^ 1 ^ 2 * d]


def norm_split(place, hidden, gain, count):
    rows, width = hidden.shape
    step = rows if rows % 32 else 32
    depth = width // count
    return call(
        norm_kernel,
        place,
        (rows // step,),
        [pl.BlockSpec((step, width), lambda i, place: (i, 0)), whole(gain)],
        [
            pl.BlockSpec((n, step, depth), lambda i, place: (0, i, 0))
            for n in (count // 2, count)
        ],
        [shape_of((n, rows, depth), BF16) for n in (count // 2, count)],
        (hidden, gain),
        (4 * rows * width, 4 * rows * width),
    )


def pack_kernel(place, cont, other, *outs):
    for d, out in enumerate(outs, 1):
        out[0] = cont[place[SP] ^ 2 * d]
        out[1] = other[d]


def pack(place, cont, other):
    count, rows, depth = cont.shape
    block = (2, rows, depth)
    sent = count // 2 - 1
    return call(
        pack_kernel,
        place,
        (1,),
        [whole(cont), whole(other)],
        [pl.BlockSpec(block, lambda i, place: (0, 0, 0))] * sent,
        [shape_of(block, BF16)] * sent,
        (cont, other),
        (0, 8 * sent * rows * depth),
    )


def pick_kernel(place, first, key, value, half, both):
    size = half.shape[1]
    half[...] = first[...]
    both[:, :size] = key[...]
    both[:, size:] = value[...]


def pick_columns(place, weight, size):
    depth = weight.shape[0]
    block = (depth, size)
    outs = [shape_of(block, BF16), shape_of((depth, 2 * size), BF16)]
    return call(
        pick_kernel,
        place,
        (1,),
        [
            pl.BlockSpec(block, lambda i, place: (0, 2 * place[HEAD] + place[GROUP])),
            pl.BlockSpec(block, lambda i, place: (0, 2 * place[HEAD])),
            pl.BlockSpec(block, lambda i, place: (0, 2 * place[HEAD] + 1)),
        ],
        [whole(out) for out in outs],
        outs,
        (weight, weight, weight),
        (0, 12 * depth * size),
    )


def query_kernel(count, place, *refs):
    cont, other, chips, (weight, keep, send) = refs[0], refs[1], refs[2:-3], refs[-3:]
    block = cont.shape[1]
    rows = [cont[place[SP]], other[0]]
    for chip in chips:
        rows += [chip[0], chip[1]]
    part = jnp.dot(jnp.concatenate(rows, axis=0), weight[...], preferred_element_type=F32)
    for d in range(count):
        at = d // 2 * block
        (keep, send)[d % 2][at : at + block, :] = part[d * block : (d + 1) * block]


def query_parts(place, cont, got, weight):
    count, block, depth = cont.shape
    width = weight.shape[1]
    half = count // 2 * block
    return call(
        functools.partial(query_kernel, count),
        place,
        (1,),
        [whole(a) for a in (cont, *got)]
        + [whole(weight)],
        [pl.BlockSpec((half, width), lambda i, place: (0, 0))] * 2,
        [shape_of((half, width), F32)] * 2,
        (cont, *got, weight),
        (2 * count * block * depth * width, 2 * depth * width),
    )


def turn(values, cosine, sine):
    return values * cosine + pltpu.roll(values, values.shape[-1] // 2, 1) * sine


def near_kernel(place, hidden, norm_gain, cont, own, partner, prompt, out):
    split_normed(hidden, norm_gain, prompt)
    total = 0.0
    for d, weight in ((0, own), (1, partner)):
        left = jnp.concatenate([prompt[place[SP] ^ d], cont[place[SP] ^ d]], axis=0)
        total = total + jnp.dot(left, weight[...], preferred_element_type=F32)
    out[...] = total


def near_keyval(place, hidden, norm_gain, cont, own, partner):
    args = (hidden, norm_gain, cont, own, partner)
    count, cont_rows, depth = cont.shape
    prompt_rows = hidden.shape[0]
    rows = prompt_rows + cont_rows
    width = own.shape[1]
    outs = [shape_of((count, prompt_rows, depth), BF16), shape_of((rows, width), F32)]
    return call(
        near_kernel,
        place,
        (1,),
        [whole(a) for a in args],
        [whole(out) for out in outs],
        outs,
        args,
        (4 * rows * depth * width, 4 * depth * (rows * count + width)),
    )


def keyval_kernel(count, place, prompt, cont, cosine, sine, gain, near, *refs):
    weights, out = refs[:-1], refs[-1]
    size = gain.shape[1]
    total = 0.0
    for d in range(2, count):
        left = jnp.concatenate([prompt[place[SP] ^ d], cont[place[SP] ^ d]], axis=0)
        weight = jnp.concatenate([weights[2 * d - 4][...], weights[2 * d - 3][...]], axis=1)
        total = total + jnp.dot(left, weight, preferred_element_type=F32)
    swapped = place[GROUP] == 1
    first, second = total[:, :size], total[:, size:]
    key = near[:, :size] + jnp.where(swapped, second, first)
    value = near[:, size:] + jnp.where(swapped, first, second)
    out[:, :size] = turn(rms_rows(key, gain[...]), cosine[...], sine[...]).astype(BF16)
    out[:, size:] = value.astype(BF16)


def keyval_rows(place, prompt, cont, cosine, sine, gain, near, weights):
    count, prompt_rows, depth = prompt.shape
    rows = prompt_rows + cont.shape[1]
    size = gain.shape[1]
    args = (prompt, cont, cosine, sine, gain, near, *weights)
    out = shape_of((rows, 2 * size), BF16)
    return call(
        functools.partial(keyval_kernel, count),
        place,
        (1,),
        [whole(a) for a in args],
        whole(out),
        out,
        args,
        (2 * rows * count * depth * size, count * depth * (rows + 2 * size)),
    )


def starts_of(lengths, index):
    start = jnp.zeros(index.shape, jnp.int32)
    total = jnp.int32(0)
    for c in range(lengths.shape[0]):
        start = jnp.where(index >= total, total, start)
        total = total + lengths[c]
    return start


def attend_kernel(count, prompt_rows, place, lengths, mine, near, far, cosine, sine, gain, *refs):
    pairs, out = refs[:-1], refs[-1]
    rows, width = far.shape
    size = gain.shape[1]
    heads = width // size
    cosine, sine = cosine[prompt_rows:, :], sine[prompt_rows:, :]
    queries = []
    for h in range(heads):
        part = slice(h * size, (h + 1) * size)
        value = rms_rows(mine[:rows, part] + near[:rows, part] + far[:, part], gain[...])
        queries.append(turn(value, cosine, sine).astype(BF16))
    queries = jnp.concatenate(queries, axis=0)
    prompt = jnp.concatenate([pair[:prompt_rows] for pair in pairs], axis=0)
    cont = jnp.concatenate([pair[prompt_rows:] for pair in pairs], axis=0)
    scale = 1.0 / (math.sqrt(size) * math.log(2.0))
    by_rows = (((1,), (1,)), ((), ()))
    to_prompt = lax.dot_general(
        queries, prompt[:, :size], by_rows, preferred_element_type=F32
    )
    to_cont = lax.dot_general(queries, cont[:, :size], by_rows, preferred_element_type=F32)
    shape = (rows, cont.shape[0])
    own = place[SP] * rows + lax.broadcasted_iota(jnp.int32, shape, 0)
    at = lax.broadcasted_iota(jnp.int32, shape, 1)
    key = jnp.zeros(shape, jnp.int32)
    for d in range(count):
        inside = (at >= d * rows) & (at < (d + 1) * rows)
        key = jnp.where(inside, (place[SP] ^ d) * rows + at - d * rows, key)
    allowed = jnp.where((key >= starts_of(lengths, own)) & (key <= own), 0.0, -1e30)
    to_cont = to_cont + jnp.concatenate([allowed] * heads, axis=0)
    peak = jnp.maximum(
        jnp.max(to_prompt, axis=1, keepdims=True), jnp.max(to_cont, axis=1, keepdims=True)
    )
    to_prompt = jnp.exp2((to_prompt - peak) * scale)
    to_cont = jnp.exp2((to_cont - peak) * scale)
    factor = 1.0 / (
        jnp.sum(to_prompt, axis=1, keepdims=True) + jnp.sum(to_cont, axis=1, keepdims=True)
    )
    result = jnp.dot(
        (to_prompt * factor).astype(BF16), prompt[:, size:], preferred_element_type=F32
    ) + jnp.dot((to_cont * factor).astype(BF16), cont[:, size:], preferred_element_type=F32)
    for h in range(heads):
        out[:, h * size : (h + 1) * size] = result[h * rows : (h + 1) * rows].astype(BF16)


def attend(place, lengths, mine, near, far, cosine, sine, gain, pairs, prompt_rows):
    rows, width = far.shape
    args = (mine, near, far, cosine, sine, gain, *pairs)
    out = shape_of((rows, width), BF16)
    keys = len(pairs) * pairs[0].shape[0]
    return call(
        functools.partial(attend_kernel, len(pairs), prompt_rows),
        place,
        (1,),
        [pl.BlockSpec(memory_space=pltpu.SMEM)] + [whole(a) for a in args],
        whole(out),
        out,
        (lengths, *args),
        (4 * rows * width * keys, 10 * rows * width + 512 * keys),
    )


def out_kernel(count, place, *refs):
    heads, weights, outs, part = refs[: 2 * count], refs[-count - 3 : -count - 1], refs[-count - 1 : -1], refs[-1]
    rows = heads[0].shape[0]
    total = 0.0
    for side, weight in enumerate(weights):
        left = jnp.concatenate([h[...] for h in heads[side * count : (side + 1) * count]], axis=0)
        share = jnp.dot(left, weight[...], preferred_element_type=F32)
        total = total + share.astype(BF16).astype(F32)
    total = total.astype(BF16)
    for d in range(count):
        part[d] = total[d * rows : (d + 1) * rows]
    for e in range(count):
        outs[e][...] = part[place[TP] ^ e ^ place[SP]]


def out_parts(place, heads, own, partner):
    count = len(heads) // 2
    rows = heads[0].shape[0]
    depth, width = partner.shape
    if width % 128:
        own = column_half(place, own, False)
        half = whole(own)
    else:
        half = pl.BlockSpec((depth, width), lambda i, place: (0, place[TP] % 2))
    args = (*heads, own, partner)
    return call(
        functools.partial(out_kernel, count),
        place,
        (1,),
        [whole(h) for h in heads] + [half, whole(partner)],
        [pl.BlockSpec((rows, width), lambda i, place: (0, 0))] * count,
        [shape_of((rows, width), BF16)] * count,
        args,
        (4 * count * rows * depth * width, 4 * depth * width),
        [pltpu.VMEM((count, rows, width), BF16)],
    )


def final_kernel(count, place, hidden, *refs):
    parts, out = refs[:-1], refs[-1]
    width = parts[0].shape[1]
    sums = [0.0, 0.0]
    for e, part in enumerate(parts):
        sums[e % 2] = sums[e % 2] + part[...].astype(F32)
    odd = place[SP] % 2 == 1
    left = jnp.where(odd, sums[1], sums[0])
    right = jnp.where(odd, sums[0], sums[1])
    out[:, :width] = (hidden[:, :width].astype(F32) + left).astype(BF16)
    out[:, width:] = (hidden[:, width:].astype(F32) + right).astype(BF16)


def final_sum(place, parts, hidden):
    rows, width = parts[0].shape
    width *= 2
    count = len(parts)
    if width % 128:
        hidden = lax.dynamic_slice_in_dim(hidden, place[TP] * width, width, 1)
        residual = whole(hidden)
    else:
        residual = pl.BlockSpec((rows, width), lambda i, place: (0, place[TP]))
    return call(
        functools.partial(final_kernel, count),
        place,
        (1,),
        [residual] + [whole(a) for a in parts],
        pl.BlockSpec((rows, width), lambda i, place: (0, 0)),
        shape_of((rows, width), BF16),
        (hidden, *parts),
        (count * rows * width, 12 * rows * width),
    )


def after(arrays, *others):
    return lax.optimization_barrier((arrays, others))[0]


def swap(array, axis, bits):
    return lax.ppermute(array, axis, [(i, i ^ bits) for i in range(lax.axis_size(axis))])


def swap_both(array, tp_bits, sp_bits, count):
    pairs = [
        (t * count + s, (t ^ tp_bits) * count + (s ^ sp_bits))
        for t in range(count)
        for s in range(count)
    ]
    return lax.ppermute(array, ("tp", "sp"), pairs)


def swap_bits(count):
    bits = []
    bit = 1
    while bit < count:
        bits.append(bit)
        bit *= 2
    return bits


def gather_blocks(block, axis, count):
    held = {0: block}
    bits = swap_bits(count)
    for bit in bits[1:] + bits[:1]:
        held.update({d ^ bit: swap(held[d], axis, bit) for d in sorted(held)})
    return [held[d] for d in range(count)]


def other_halves(half, axis, count):
    firsts = {0: half}
    for bit in swap_bits(count)[1:]:
        firsts.update({d ^ bit: swap(firsts[d], axis, bit) for d in sorted(firsts)})
    del firsts[0]
    return firsts


def both_cores(held, axis):
    return {**held, **{d ^ 1: swap(held[d], axis, 1) for d in sorted(held)}}


def sum_blocks(place, keep, send, axis, count):
    near = swap(send, axis, 1)
    rows = keep.shape[0] // (count // 2)
    held = {d: add_rows(place, keep, near, d // 2 * rows, rows) for d in range(2, count, 2)}
    far = 0.0
    for bit in swap_bits(count)[1:]:
        sent = [d for d in sorted(held) if d & bit]
        got = {d ^ bit: swap(held[d], axis, bit) for d in sent}
        far = far + got.pop(0)
        held = {d: held[d] + got[d] for d in got}
    return keep, near, far


def table_kernel(prompt_rows, prompt_total, place, lengths, cosine, sine):
    rows, size = cosine.shape
    shape = cosine.shape
    row = lax.broadcasted_iota(jnp.int32, shape, 0)
    lane = lax.broadcasted_iota(jnp.int32, shape, 1)
    index = place[SP] * (rows - prompt_rows) + row - prompt_rows
    position = jnp.where(
        row < prompt_rows,
        place[SP] * prompt_rows + row,
        prompt_total + index - starts_of(lengths, index),
    )
    half = size // 2
    step = jnp.where(lane < half, lane, lane - half).astype(F32)
    angle = position.astype(F32) * jnp.exp(step * (-2.0 * math.log(1000000.0) / size))
    cosine[...] = jnp.cos(angle)
    angle = jnp.sin(angle)
    sine[...] = jnp.where(lane < half, -angle, angle)


def tables(place, lengths, prompt_rows, prompt_total, cont_rows, size):
    out = shape_of((prompt_rows + cont_rows, size), F32)
    return call(
        functools.partial(table_kernel, prompt_rows, prompt_total),
        place,
        (1,),
        [pl.BlockSpec(memory_space=pltpu.SMEM)],
        [whole(out)] * 2,
        [out] * 2,
        (lengths,),
        (100 * out.size, 8 * out.size),
    )


def slice_kernel(place, array, out):
    out[...] = array[...]


def column_half(place, array, other):
    rows, width = array.shape
    width //= 2
    side = 1 if other else 0
    if width % 128:
        at = (place[TP] + side) % 2 * width
        return lax.dynamic_slice_in_dim(array, at, width, 1)
    return call(
        slice_kernel,
        place,
        (4,),
        [pl.BlockSpec((rows // 4, width), lambda i, place: (i, (place[TP] + side) % 2))],
        pl.BlockSpec((rows // 4, width), lambda i, place: (i, 0)),
        shape_of((rows, width), BF16),
        (array,),
        (0, 4 * rows * width),
    )


def add_kernel(place, left, right, out):
    out[...] = left[...] + right[...]


def add_rows(place, left, right, at, rows):
    width = left.shape[1]
    spec = pl.BlockSpec((rows, width), lambda i, place: (at // rows, 0))
    return call(
        add_kernel,
        place,
        (1,),
        [spec, spec],
        pl.BlockSpec((rows, width), lambda i, place: (0, 0)),
        shape_of((rows, width), F32),
        (left, right),
        (rows * width, 12 * rows * width),
    )


def on_device(
    hidden_cont,
    hidden_prompt,
    norm_gain,
    query_weight,
    keyval_weight,
    out_weight,
    query_gain,
    key_gain,
    sample_lengths,
):
    size = query_gain.shape[0]
    heads_here = query_weight.shape[1] // size
    cont_rows = hidden_cont.shape[0]
    prompt_rows = hidden_prompt.shape[0]
    sp_index = lax.axis_index("sp")
    sp_count = lax.axis_size("sp")
    tp_index = lax.axis_index("tp")
    assert lax.axis_size("tp") == sp_count and lax.axis_size("groups") == 2
    place = jnp.stack(
        [
            sp_index,
            tp_index,
            lax.axis_index("groups"),
            tp_index * heads_here // (QH // KVH),
        ]
    ).astype(jnp.int32)
    norm_gain = norm_gain[None, :]
    query_gain = query_gain[None, :]
    key_gain = key_gain[None, :]

    half, both = pick_columns(place, keyval_weight, size)
    halves = other_halves(half, "sp", sp_count)
    block, cont = norm_split(after(place, half), hidden_cont, norm_gain, sp_count)
    other = swap(block, "sp", 1)
    packed = pack(place, cont, other)
    got = [swap(block, "sp", 2 * d) for d, block in enumerate(packed, 1)]
    partner = swap(both, "sp", 1)
    sent = column_half(place, after(out_weight, packed), True)
    out_partner = swap(sent, "tp", 1)
    cosine, sine = tables(
        place, sample_lengths, prompt_rows, prompt_rows * sp_count, cont_rows, size
    )
    halves = after(halves, packed, sent, cosine)
    others = {d: swap(half, "groups", 1) for d, half in halves.items()}
    halves = both_cores(halves, "sp")
    prompt, near_pair = near_keyval(
        place, hidden_prompt, norm_gain, cont, both, after(partner, halves)
    )
    got = after(got, near_pair, sent, cosine)
    others = both_cores(others, "sp")

    keep, send = query_parts(place, cont, [other] + got, query_weight)
    mine, near, far = sum_blocks(place, keep, send, "sp", sp_count)
    weights = [held[d] for d in range(2, sp_count) for held in (halves, others)]
    pair = keyval_rows(place, prompt, cont, cosine, sine, key_gain, near_pair, weights)
    pairs = gather_blocks(pair, "sp", sp_count)
    heads = attend(
        place,
        sample_lengths,
        mine,
        near,
        far,
        cosine,
        sine,
        query_gain,
        pairs,
        prompt_rows,
    )
    chips = range(0, sp_count, 2)
    near_heads = {d: swap(heads, "sp", d) if d else heads for d in chips}
    far_heads = {d: swap_both(heads, 1, d, sp_count) for d in chips}
    near_heads = both_cores(near_heads, "sp")
    far_heads = both_cores(far_heads, "sp")
    all_heads = [held[d] for held in (near_heads, far_heads) for d in range(sp_count)]
    parts = out_parts(place, all_heads, out_weight, out_partner)
    parts = [
        lax.ppermute(
            part,
            ("tp", "sp"),
            [
                (t * sp_count + s, s * sp_count + (t ^ e))
                for t in range(sp_count)
                for s in range(sp_count)
            ],
        )
        for e, part in enumerate(parts)
    ]
    return final_sum(place, parts, hidden_cont)


def solution(mesh):
    placed = (
        P(("groups", "sp"), None),
        P(("groups", "sp"), None),
        P(),
        P("sp", "tp"),
        P("sp", None),
        P("tp", "sp"),
        P(),
        P(),
        P("groups"),
    )
    return jax.shard_map(
        on_device, mesh=mesh, in_specs=placed, out_specs=P(("groups", "sp"), "tp"), check_vma=False
    )
```

```python
import functools
import math

import jax
import jax.numpy as jnp
from jax import lax
from jax.experimental import pallas as pl
from jax.experimental.pallas import tpu as pltpu
from jax.sharding import PartitionSpec as P

QH = 32
KVH = 4
SP, TP, GROUP, HEAD = range(4)
BF16 = jnp.bfloat16
F32 = jnp.float32
ROOM = 14 * 1024 * 1024


def call(kernel, place, grid, in_specs, out_specs, out_shape, args, cost, scratch=(), room=ROOM):
    flops, moved = cost
    return pl.pallas_call(
        kernel,
        out_shape=out_shape,
        grid_spec=pltpu.PrefetchScalarGridSpec(
            num_scalar_prefetch=1,
            grid=grid,
            in_specs=in_specs,
            out_specs=out_specs,
            scratch_shapes=scratch,
        ),
        compiler_params=pltpu.CompilerParams(vmem_limit_bytes=room),
        cost_estimate=pl.CostEstimate(flops=flops, bytes_accessed=moved, transcendentals=0),
    )(place, *args)


def whole(array):
    zeros = (0,) * array.ndim
    return pl.BlockSpec(array.shape, lambda i, place: zeros)


def shape_of(shape, dtype):
    return jax.ShapeDtypeStruct(shape, dtype)


def rms_rows(values, gain):
    return values * lax.rsqrt(jnp.mean(values * values, axis=-1, keepdims=True) + 1e-06) * gain


def split_normed(hidden, gain, out):
    count, _, depth = out.shape
    normed = rms_rows(hidden[...].astype(F32), gain[...]).astype(BF16)
    for j in range(count):
        out[j] = normed[:, j * depth : (j + 1) * depth]


def norm_kernel(place, hidden, gain, out, split):
    split_normed(hidden, gain, split)
    for d in range(out.shape[0]):
        out[d] = split[place[SP] ^ 1 ^ 2 * d]


def norm_split(place, hidden, gain, count):
    rows, width = hidden.shape
    step = rows if rows % 32 else 32
    depth = width // count
    return call(
        norm_kernel,
        place,
        (rows // step,),
        [pl.BlockSpec((step, width), lambda i, place: (i, 0)), whole(gain)],
        [
            pl.BlockSpec((n, step, depth), lambda i, place: (0, i, 0))
            for n in (count // 2, count)
        ],
        [shape_of((n, rows, depth), BF16) for n in (count // 2, count)],
        (hidden, gain),
        (4 * rows * width, 4 * rows * width),
    )


def pack_kernel(place, cont, other, *outs):
    for d, out in enumerate(outs, 1):
        out[0] = cont[place[SP] ^ 2 * d]
        out[1] = other[d]


def pack(place, cont, other):
    count, rows, depth = cont.shape
    block = (2, rows, depth)
    sent = count // 2 - 1
    return call(
        pack_kernel,
        place,
        (1,),
        [whole(cont), whole(other)],
        [pl.BlockSpec(block, lambda i, place: (0, 0, 0))] * sent,
        [shape_of(block, BF16)] * sent,
        (cont, other),
        (0, 8 * sent * rows * depth),
    )


def pick_kernel(place, columns, half, both):
    size = half.shape[1]
    both[...] = columns[...]
    half[...] = jnp.where(place[GROUP] == 1, columns[:, size:], columns[:, :size])


def pick_columns(place, weight, size):
    depth = weight.shape[0]
    outs = [shape_of((depth, n * size), BF16) for n in (1, 2)]
    return call(
        pick_kernel,
        place,
        (1,),
        [pl.BlockSpec((depth, 2 * size), lambda i, place: (0, place[HEAD]))],
        [whole(out) for out in outs],
        outs,
        (weight,),
        (0, 10 * depth * size),
    )


def query_kernel(count, place, *refs):
    cont, other, chips, (weight, keep, send) = refs[0], refs[1], refs[2:-3], refs[-3:]
    block = cont.shape[1]
    rows = [cont[place[SP]], other[0]]
    for chip in chips:
        rows += [chip[0], chip[1]]
    part = jnp.dot(jnp.concatenate(rows, axis=0), weight[...], preferred_element_type=F32)
    for d in range(count):
        at = d // 2 * block
        (keep, send)[d % 2][at : at + block, :] = part[d * block : (d + 1) * block]


def query_parts(place, cont, got, weight):
    count, block, depth = cont.shape
    width = weight.shape[1]
    half = count // 2 * block
    return call(
        functools.partial(query_kernel, count),
        place,
        (1,),
        [whole(a) for a in (cont, *got)]
        + [whole(weight)],
        [pl.BlockSpec((half, width), lambda i, place: (0, 0))] * 2,
        [shape_of((half, width), F32)] * 2,
        (cont, *got, weight),
        (2 * count * block * depth * width, 2 * depth * width),
    )


def turn(values, cosine, sine):
    return values * cosine + pltpu.roll(values, values.shape[-1] // 2, 1) * sine


def near_kernel(place, hidden, norm_gain, cont, own, partner, prompt, out):
    split_normed(hidden, norm_gain, prompt)
    total = 0.0
    for d, weight in ((0, own), (1, partner)):
        left = jnp.concatenate([prompt[place[SP] ^ d], cont[place[SP] ^ d]], axis=0)
        total = total + jnp.dot(left, weight[...], preferred_element_type=F32)
    out[...] = total


def near_keyval(place, hidden, norm_gain, cont, own, partner):
    args = (hidden, norm_gain, cont, own, partner)
    count, cont_rows, depth = cont.shape
    prompt_rows = hidden.shape[0]
    rows = prompt_rows + cont_rows
    width = own.shape[1]
    outs = [shape_of((count, prompt_rows, depth), BF16), shape_of((rows, width), F32)]
    return call(
        near_kernel,
        place,
        (1,),
        [whole(a) for a in args],
        [whole(out) for out in outs],
        outs,
        args,
        (4 * rows * depth * width, 4 * depth * (rows * count + width)),
    )


def keyval_kernel(count, place, prompt, cont, cosine, sine, gain, near, *refs):
    weights, out = refs[:-1], refs[-1]
    size = gain.shape[1]
    total = 0.0
    for d in range(2, count):
        left = jnp.concatenate([prompt[place[SP] ^ d], cont[place[SP] ^ d]], axis=0)
        weight = jnp.concatenate([weights[2 * d - 4][...], weights[2 * d - 3][...]], axis=1)
        total = total + jnp.dot(left, weight, preferred_element_type=F32)
    swapped = place[GROUP] == 1
    first, second = total[:, :size], total[:, size:]
    key = near[:, :size] + jnp.where(swapped, second, first)
    value = near[:, size:] + jnp.where(swapped, first, second)
    out[:, :size] = turn(rms_rows(key, gain[...]), cosine[...], sine[...]).astype(BF16)
    out[:, size:] = value.astype(BF16)


def keyval_rows(place, prompt, cont, cosine, sine, gain, near, weights):
    count, prompt_rows, depth = prompt.shape
    rows = prompt_rows + cont.shape[1]
    size = gain.shape[1]
    args = (prompt, cont, cosine, sine, gain, near, *weights)
    out = shape_of((rows, 2 * size), BF16)
    return call(
        functools.partial(keyval_kernel, count),
        place,
        (1,),
        [whole(a) for a in args],
        whole(out),
        out,
        args,
        (2 * rows * count * depth * size, count * depth * (rows + 2 * size)),
    )


def starts_of(lengths, index):
    start = jnp.zeros(index.shape, jnp.int32)
    total = jnp.int32(0)
    for c in range(lengths.shape[0]):
        start = jnp.where(index >= total, total, start)
        total = total + lengths[c]
    return start


def attend_kernel(count, prompt_rows, place, lengths, mine, near, far, cosine, sine, gain, *refs):
    pairs, out = refs[:-1], refs[-1]
    rows, width = far.shape
    size = gain.shape[1]
    heads = width // size
    cosine, sine = cosine[prompt_rows:, :], sine[prompt_rows:, :]
    queries = []
    for h in range(heads):
        part = slice(h * size, (h + 1) * size)
        value = rms_rows(mine[:rows, part] + near[:rows, part] + far[:, part], gain[...])
        queries.append(turn(value, cosine, sine).astype(BF16))
    queries = jnp.concatenate(queries, axis=0)
    prompt = jnp.concatenate([pair[:prompt_rows] for pair in pairs], axis=0)
    cont = jnp.concatenate([pair[prompt_rows:] for pair in pairs], axis=0)
    scale = 1.0 / (math.sqrt(size) * math.log(2.0))
    by_rows = (((1,), (1,)), ((), ()))
    to_prompt = lax.dot_general(
        queries, prompt[:, :size], by_rows, preferred_element_type=F32
    )
    to_cont = lax.dot_general(queries, cont[:, :size], by_rows, preferred_element_type=F32)
    shape = (rows, cont.shape[0])
    own = place[SP] * rows + lax.broadcasted_iota(jnp.int32, shape, 0)
    at = lax.broadcasted_iota(jnp.int32, shape, 1)
    key = jnp.zeros(shape, jnp.int32)
    for d in range(count):
        inside = (at >= d * rows) & (at < (d + 1) * rows)
        key = jnp.where(inside, (place[SP] ^ d) * rows + at - d * rows, key)
    allowed = jnp.where((key >= starts_of(lengths, own)) & (key <= own), 0.0, -1e30)
    to_cont = to_cont + jnp.concatenate([allowed] * heads, axis=0)
    peak = jnp.maximum(
        jnp.max(to_prompt, axis=1, keepdims=True), jnp.max(to_cont, axis=1, keepdims=True)
    )
    to_prompt = jnp.exp2((to_prompt - peak) * scale)
    to_cont = jnp.exp2((to_cont - peak) * scale)
    factor = 1.0 / (
        jnp.sum(to_prompt, axis=1, keepdims=True) + jnp.sum(to_cont, axis=1, keepdims=True)
    )
    result = jnp.dot(
        (to_prompt * factor).astype(BF16), prompt[:, size:], preferred_element_type=F32
    ) + jnp.dot((to_cont * factor).astype(BF16), cont[:, size:], preferred_element_type=F32)
    for h in range(heads):
        out[:, h * size : (h + 1) * size] = result[h * rows : (h + 1) * rows].astype(BF16)


def attend(place, lengths, mine, near, far, cosine, sine, gain, pairs, prompt_rows):
    rows, width = far.shape
    args = (mine, near, far, cosine, sine, gain, *pairs)
    out = shape_of((rows, width), BF16)
    keys = len(pairs) * pairs[0].shape[0]
    return call(
        functools.partial(attend_kernel, len(pairs), prompt_rows),
        place,
        (1,),
        [pl.BlockSpec(memory_space=pltpu.SMEM)] + [whole(a) for a in args],
        whole(out),
        out,
        (lengths, *args),
        (4 * rows * width * keys, 10 * rows * width + 512 * keys),
    )


def out_kernel(count, place, *refs):
    heads, weights, outs, part = refs[: 2 * count], refs[-count - 3 : -count - 1], refs[-count - 1 : -1], refs[-1]
    rows = heads[0].shape[0]
    total = 0.0
    for side, weight in enumerate(weights):
        left = jnp.concatenate([h[...] for h in heads[side * count : (side + 1) * count]], axis=0)
        share = jnp.dot(left, weight[...], preferred_element_type=F32)
        total = total + share.astype(BF16).astype(F32)
    total = total.astype(BF16)
    for d in range(count):
        part[d] = total[d * rows : (d + 1) * rows]
    for e in range(count):
        outs[e][...] = part[place[TP] ^ e ^ place[SP]]


def out_parts(place, heads, own, partner):
    count = len(heads) // 2
    rows = heads[0].shape[0]
    depth, width = partner.shape
    if width % 128:
        own = column_half(place, own, False)
        half = whole(own)
    else:
        half = pl.BlockSpec((depth, width), lambda i, place: (0, place[TP] % 2))
    args = (*heads, own, partner)
    return call(
        functools.partial(out_kernel, count),
        place,
        (1,),
        [whole(h) for h in heads] + [half, whole(partner)],
        [pl.BlockSpec((rows, width), lambda i, place: (0, 0))] * count,
        [shape_of((rows, width), BF16)] * count,
        args,
        (4 * count * rows * depth * width, 4 * depth * width),
        [pltpu.VMEM((count, rows, width), BF16)],
    )


def final_kernel(count, place, hidden, *refs):
    parts, out = refs[:-1], refs[-1]
    width = parts[0].shape[1]
    sums = [0.0, 0.0]
    for e, part in enumerate(parts):
        sums[e % 2] = sums[e % 2] + part[...].astype(F32)
    odd = place[SP] % 2 == 1
    left = jnp.where(odd, sums[1], sums[0])
    right = jnp.where(odd, sums[0], sums[1])
    out[:, :width] = (hidden[:, :width].astype(F32) + left).astype(BF16)
    out[:, width:] = (hidden[:, width:].astype(F32) + right).astype(BF16)


def final_sum(place, parts, hidden):
    rows, width = parts[0].shape
    width *= 2
    count = len(parts)
    if width % 128:
        hidden = lax.dynamic_slice_in_dim(hidden, place[TP] * width, width, 1)
        residual = whole(hidden)
    else:
        residual = pl.BlockSpec((rows, width), lambda i, place: (0, place[TP]))
    return call(
        functools.partial(final_kernel, count),
        place,
        (1,),
        [residual] + [whole(a) for a in parts],
        pl.BlockSpec((rows, width), lambda i, place: (0, 0)),
        shape_of((rows, width), BF16),
        (hidden, *parts),
        (count * rows * width, 12 * rows * width),
    )


def after(arrays, *others):
    return lax.optimization_barrier((arrays, others))[0]


def swap(array, axis, bits):
    return lax.ppermute(array, axis, [(i, i ^ bits) for i in range(lax.axis_size(axis))])


def swap_both(array, tp_bits, sp_bits, count):
    pairs = [
        (t * count + s, (t ^ tp_bits) * count + (s ^ sp_bits))
        for t in range(count)
        for s in range(count)
    ]
    return lax.ppermute(array, ("tp", "sp"), pairs)


def swap_bits(count):
    bits = []
    bit = 1
    while bit < count:
        bits.append(bit)
        bit *= 2
    return bits


def gather_blocks(block, axis, count):
    held = {0: block}
    bits = swap_bits(count)
    for bit in bits[1:] + bits[:1]:
        held.update({d ^ bit: swap(held[d], axis, bit) for d in sorted(held)})
    return [held[d] for d in range(count)]


def other_halves(half, axis, count):
    firsts = {0: half}
    for bit in swap_bits(count)[1:]:
        firsts.update({d ^ bit: swap(firsts[d], axis, bit) for d in sorted(firsts)})
    del firsts[0]
    return firsts


def both_cores(held, axis):
    return {**held, **{d ^ 1: swap(held[d], axis, 1) for d in sorted(held)}}


def sum_blocks(place, keep, send, axis, count):
    near = swap(send, axis, 1)
    rows = keep.shape[0] // (count // 2)
    held = {d: add_rows(place, keep, near, d // 2 * rows, rows) for d in range(2, count, 2)}
    far = 0.0
    for bit in swap_bits(count)[1:]:
        sent = [d for d in sorted(held) if d & bit]
        got = {d ^ bit: swap(held[d], axis, bit) for d in sent}
        far = far + got.pop(0)
        held = {d: held[d] + got[d] for d in got}
    return keep, near, far


def table_kernel(prompt_rows, prompt_total, place, lengths, cosine, sine):
    rows, size = cosine.shape
    shape = cosine.shape
    row = lax.broadcasted_iota(jnp.int32, shape, 0)
    lane = lax.broadcasted_iota(jnp.int32, shape, 1)
    index = place[SP] * (rows - prompt_rows) + row - prompt_rows
    position = jnp.where(
        row < prompt_rows,
        place[SP] * prompt_rows + row,
        prompt_total + index - starts_of(lengths, index),
    )
    half = size // 2
    step = jnp.where(lane < half, lane, lane - half).astype(F32)
    angle = position.astype(F32) * jnp.exp(step * (-2.0 * math.log(1000000.0) / size))
    cosine[...] = jnp.cos(angle)
    angle = jnp.sin(angle)
    sine[...] = jnp.where(lane < half, -angle, angle)


def tables(place, lengths, prompt_rows, prompt_total, cont_rows, size):
    out = shape_of((prompt_rows + cont_rows, size), F32)
    return call(
        functools.partial(table_kernel, prompt_rows, prompt_total),
        place,
        (1,),
        [pl.BlockSpec(memory_space=pltpu.SMEM)],
        [whole(out)] * 2,
        [out] * 2,
        (lengths,),
        (100 * out.size, 8 * out.size),
    )


def slice_kernel(place, array, out):
    out[...] = array[...]


def column_half(place, array, other):
    rows, width = array.shape
    width //= 2
    side = 1 if other else 0
    if width % 128:
        at = (place[TP] + side) % 2 * width
        return lax.dynamic_slice_in_dim(array, at, width, 1)
    return call(
        slice_kernel,
        place,
        (4,),
        [pl.BlockSpec((rows // 4, width), lambda i, place: (i, (place[TP] + side) % 2))],
        pl.BlockSpec((rows // 4, width), lambda i, place: (i, 0)),
        shape_of((rows, width), BF16),
        (array,),
        (0, 4 * rows * width),
    )


def add_kernel(place, left, right, out):
    out[...] = left[...] + right[...]


def add_rows(place, left, right, at, rows):
    width = left.shape[1]
    spec = pl.BlockSpec((rows, width), lambda i, place: (at // rows, 0))
    return call(
        add_kernel,
        place,
        (1,),
        [spec, spec],
        pl.BlockSpec((rows, width), lambda i, place: (0, 0)),
        shape_of((rows, width), F32),
        (left, right),
        (rows * width, 12 * rows * width),
    )


def on_device(
    hidden_cont,
    hidden_prompt,
    norm_gain,
    query_weight,
    keyval_weight,
    out_weight,
    query_gain,
    key_gain,
    sample_lengths,
):
    size = query_gain.shape[0]
    heads_here = query_weight.shape[1] // size
    cont_rows = hidden_cont.shape[0]
    prompt_rows = hidden_prompt.shape[0]
    sp_index = lax.axis_index("sp")
    sp_count = lax.axis_size("sp")
    tp_index = lax.axis_index("tp")
    assert lax.axis_size("tp") == sp_count and lax.axis_size("groups") == 2
    place = jnp.stack(
        [
            sp_index,
            tp_index,
            lax.axis_index("groups"),
            tp_index * heads_here // (QH // KVH),
        ]
    ).astype(jnp.int32)
    norm_gain = norm_gain[None, :]
    query_gain = query_gain[None, :]
    key_gain = key_gain[None, :]

    half, both = pick_columns(place, keyval_weight, size)
    halves = other_halves(half, "sp", sp_count)
    block, cont = norm_split(after(place, half), hidden_cont, norm_gain, sp_count)
    other = swap(block, "sp", 1)
    packed = pack(place, cont, other)
    got = [swap(block, "sp", 2 * d) for d, block in enumerate(packed, 1)]
    partner = swap(both, "sp", 1)
    sent = column_half(place, after(out_weight, packed), True)
    out_partner = swap(sent, "tp", 1)
    cosine, sine = tables(
        place, sample_lengths, prompt_rows, prompt_rows * sp_count, cont_rows, size
    )
    halves = after(halves, packed, sent, cosine)
    others = {d: swap(half, "groups", 1) for d, half in halves.items()}
    halves = both_cores(halves, "sp")
    prompt, near_pair = near_keyval(
        place, hidden_prompt, norm_gain, cont, both, after(partner, halves)
    )
    got = after(got, near_pair, sent, cosine)
    others = both_cores(others, "sp")

    keep, send = query_parts(place, cont, [other] + got, query_weight)
    mine, near, far = sum_blocks(place, keep, send, "sp", sp_count)
    weights = [held[d] for d in range(2, sp_count) for held in (halves, others)]
    pair = keyval_rows(place, prompt, cont, cosine, sine, key_gain, near_pair, weights)
    pairs = gather_blocks(pair, "sp", sp_count)
    heads = attend(
        place,
        sample_lengths,
        mine,
        near,
        far,
        cosine,
        sine,
        query_gain,
        pairs,
        prompt_rows,
    )
    chips = range(0, sp_count, 2)
    near_heads = {d: swap(heads, "sp", d) if d else heads for d in chips}
    far_heads = {d: swap_both(heads, 1, d, sp_count) for d in chips}
    near_heads = both_cores(near_heads, "sp")
    far_heads = both_cores(far_heads, "sp")
    all_heads = [held[d] for held in (near_heads, far_heads) for d in range(sp_count)]
    parts = out_parts(place, all_heads, out_weight, out_partner)
    parts = [
        lax.ppermute(
            part,
            ("tp", "sp"),
            [
                (t * sp_count + s, s * sp_count + (t ^ e))
                for t in range(sp_count)
                for s in range(sp_count)
            ],
        )
        for e, part in enumerate(parts)
    ]
    return final_sum(place, parts, hidden_cont)


def solution(mesh):
    placed = (
        P(("groups", "sp"), None),
        P(("groups", "sp"), None),
        P(),
        P("sp", "tp"),
        P("sp", None),
        P("tp", "sp"),
        P(),
        P(),
        P("groups"),
    )
    return jax.shard_map(
        on_device, mesh=mesh, in_specs=placed, out_specs=P(("groups", "sp"), "tp"), check_vma=False
    )
```
